32 devices in a mesh: dp: 4 (over y, x), ctx: 4 (over z), tp: 2 (over core).
Axes of the slice: x: 2, y: 2, z: 4, core: 2. Of those that a mesh axis runs over, the one named last changes fastest.
Arguments:
- query: bfloat16 [2048, 8192], P(('dp', 'ctx'), 'tp'), may hold values from -6 to 6
- key_in: bfloat16 [2048, 8192], P(('dp', 'ctx'), 'tp'), may hold values from -6 to 6
- value_in: bfloat16 [2048, 8192], P(('dp', 'ctx'), 'tp'), may hold values from -6 to 6
- gate: bfloat16 [2048, 8192], P(('dp', 'ctx'), 'tp'), may hold values from -6 to 6
- out_grad: bfloat16 [2048, 8192], P(('dp', 'ctx')), may hold values from -6 to 6
- proj_weight: bfloat16 [8192, 8192], P('tp', ('dp', 'ctx')), may hold values from -0.0625 to 0.0625
- mr_filter: bfloat16 [512, 128], P('tp'), may hold values from -0.5 to 0.5
- lr_rate: float32 [512, 16], P('tp'), may hold values from 3.90625e-05 to 0.05
- lr_residue: float32 [512, 16], P('tp'), may hold values from -0.6 to 0.6
Outputs:
- query_grad: bfloat16 [2048, 8192], P(('dp', 'ctx'), 'tp')
- conv_grad: bfloat16 [2048, 8192], P(('dp', 'ctx'), 'tp')
- gate_grad: bfloat16 [2048, 8192], P(('dp', 'ctx'), 'tp')
- weight_grad_t: bfloat16 [8192, 8192], P(('dp', 'ctx'), 'tp')
The draws below stay inside these ranges and needn't reach their ends.
All inputs are finite; a program needn't handle non-finite values.
Results may differ from the reference program's by a relative error of at most 0.028.
Values may be sent and summed in bfloat16 or wider, within the bound.
No kernel may reach another device: no remote copies, remote signals or barrier semaphores. Data moves between devices by JAX's collectives and lax.ppermute only.
A program may use at most 256 MiB of HBM per device.

```python
import math
import jax
import jax.numpy as jnp
from jax import lax

D = 8192
GROUP = 16
MR_TAPS = 128
ORDER = 16
TOK_DEV = 128
TOKENS = 2048
N_DP = 4
N_CTX = 4


def strengthened(values, key, source, target, shards_of, factor):
    def block_of(dim):
        return (jnp.arange(values.shape[dim]) // (values.shape[dim] // shards_of)).reshape((-1,) + (1,) * (values.ndim - 1 - dim))

    first = jax.random.permutation(key, shards_of)[block_of(target)]
    second = (block_of(target) + shards_of // 2) % shards_of
    return jnp.where((block_of(source) == first) | (block_of(source) == second), factor * values, values)


def level_of(stream_key, dims, cuts, least, high):
    def one(axis_at, blocks):
        draws = jax.random.uniform(jax.random.fold_in(jax.random.fold_in(stream_key, 6), axis_at), (blocks,), jnp.float32, least / len(cuts), high / len(cuts))
        return jnp.repeat(jnp.exp(draws), dims[axis_at] // blocks).reshape((-1,) + (1,) * (len(dims) - axis_at - 1))

    gain = one(*cuts[0])
    for cut in cuts[1:]:
        gain = gain * one(*cut)
    return gain


def noise(own_key, dims, width, limit, shards=(), dtype=jnp.bfloat16):
    gain = level_of(own_key, dims, shards, -0.22, 0.18) if shards else 1.0
    drawn = jax.random.normal(own_key, dims, jnp.float32) * width * gain
    return jnp.minimum(jnp.maximum(drawn, -limit), limit).astype(dtype)


def heavy_noise(stream_key, extent, spread, limit, pieces, heavy, dtype=jnp.bfloat16):
    values = spread * jax.random.normal(stream_key, extent, jnp.float32)
    if pieces:
        values = values * level_of(stream_key, extent, pieces, -0.22, 0.18)
    return jnp.clip(strengthened(values, jax.random.fold_in(stream_key, 3), *heavy), -limit, limit).astype(dtype)


def setup_inputs(seed: int = 0) -> dict:
    keys = jax.random.split(jax.random.key(seed), 10)
    return {
        "query": noise(keys[0], (TOKENS, D), 1.0, 6.0, ((0, 16), (1, 2))),
        "key_in": noise(keys[1], (TOKENS, D), 1.0, 6.0, ((0, 16), (1, 2))),
        "value_in": noise(keys[2], (TOKENS, D), 1.0, 6.0, ((0, 16), (1, 2))),
        "gate": noise(keys[3], (TOKENS, D), 1.0, 6.0, ((0, 16), (1, 2))),
        "out_grad": heavy_noise(keys[4], (TOKENS, D), 1.0, 6.0, ((0, 16),), (0, 1, 16, 2.0)),
        "proj_weight": noise(keys[5], (D, D), D ** -0.5, 0.0625, ((0, 2), (1, 16))),
        "mr_filter": noise(keys[6], (D // GROUP, MR_TAPS), MR_TAPS ** -0.5, 0.5, ((0, 2),)),
        "lr_rate": jnp.clip(jnp.exp(math.log(0.05) - 7.1546154 * jax.random.uniform(keys[7], (D // GROUP, ORDER), jnp.float32) ** level_of(keys[7], (D // GROUP, ORDER), ((0, 2),), -0.2, 0.2)), 3.9062499126885086e-05, 0.05),
        "lr_residue": noise(keys[8], (D // GROUP, ORDER), 0.1, 0.6, ((0, 2),), jnp.float32),
    }


HIGHEST = lax.Precision.HIGHEST


def mr_matrix(filters, row_count, taps):
    out_pos = jnp.arange(row_count)[:, None]
    in_pos = jnp.arange(row_count + taps)[None, :]
    lag_index = taps + out_pos - in_pos
    valid = (lag_index >= 0) & (lag_index < taps)
    picked = jnp.take(filters, jnp.clip(lag_index, 0, taps - 1), axis=1)
    return jnp.where(valid[None], picked, jnp.zeros_like(picked))


def lr_tables(rates, residues, row_count):
    counts = jnp.arange(row_count + 1).astype(jnp.float32)
    powers = jnp.exp(-rates[None, :, :] * counts[:, None, None])
    kernel = jnp.sum(residues[None] * powers[:row_count], axis=2)
    lag_index = jnp.arange(row_count)[:, None] - jnp.arange(row_count)[None, :]
    picked = jnp.take(kernel.T, jnp.clip(lag_index, 0, row_count - 1), axis=1)
    toeplitz = jnp.where((lag_index >= 0)[None], picked, jnp.zeros_like(picked))
    carry_coef = residues[None] * powers[1:]
    end_coef = powers[:row_count][::-1]
    start_coef = powers[:row_count]
    back_coef = residues[None] * powers[1:][::-1]
    block_decay = powers[row_count].T
    return toeplitz, carry_coef, end_coef, start_coef, back_coef, block_decay


def reference(query, key_in, value_in, gate, out_grad, proj_weight, mr_filter, lr_rate, lr_residue):
    row_count = TOK_DEV
    groups = D // GROUP
    product = (key_in.astype(jnp.float32) * value_in.astype(jnp.float32)).astype(jnp.bfloat16)
    conv_matrix = mr_matrix(mr_filter, row_count, MR_TAPS).astype(jnp.float32)
    toeplitz, carry_coef, end_coef, start_coef, back_coef, block_decay = lr_tables(lr_rate, lr_residue, row_count)
    out_delta = jnp.dot(out_grad, proj_weight.T, preferred_element_type=jnp.float32)

    def blocked(array):
        return array.reshape(N_DP, N_CTX, row_count, D)

    def forward_block(carry, inputs):
        conv_rim, state = carry
        product_blk, query_blk, gate_blk = inputs
        extended = jnp.concatenate([conv_rim, product_blk], axis=0).astype(jnp.float32)
        extended = extended.reshape(row_count + MR_TAPS, groups, GROUP)
        conv_out = jnp.einsum("gtu,ugi->tgi", conv_matrix, extended, precision=HIGHEST).reshape(row_count, D)
        mixed = (query_blk.astype(jnp.float32) * conv_out).astype(jnp.bfloat16)
        mixed_three = mixed.astype(jnp.float32).reshape(row_count, groups, GROUP)
        local_part = jnp.einsum("gtv,vgi->tgi", toeplitz, mixed_three, precision=HIGHEST)
        carried = jnp.einsum("tgn,ngi->tgi", carry_coef, state, precision=HIGHEST)
        long_out = (local_part + carried).reshape(row_count, D)
        ends = jnp.einsum("tgn,tgi->ngi", end_coef, mixed_three, precision=HIGHEST)
        new_state = block_decay[:, :, None] * state + ends
        gated = (gate_blk.astype(jnp.float32) * long_out).astype(jnp.bfloat16)
        return (product_blk[row_count - MR_TAPS:], new_state), (conv_out, long_out, gated)

    def forward_sequence(inputs):
        start = (jnp.zeros((MR_TAPS, D), jnp.bfloat16), jnp.zeros((ORDER, groups, GROUP), jnp.float32))
        final, outputs = lax.scan(forward_block, start, inputs)
        return outputs

    conv_all, long_all, gated_all = lax.map(forward_sequence, (blocked(product), blocked(query), blocked(gate)))

    def backward_block(later, inputs):
        delta_blk, gate_blk, query_blk, conv_blk, long_blk = inputs
        seed_three = (delta_blk * gate_blk.astype(jnp.float32)).reshape(row_count, groups, GROUP)
        local_back = jnp.einsum("gtv,tgi->vgi", toeplitz, seed_three, precision=HIGHEST)
        carried_back = jnp.einsum("tgn,ngi->tgi", back_coef, later, precision=HIGHEST)
        mixed_delta = (local_back + carried_back).reshape(row_count, D)
        starts = jnp.einsum("tgn,tgi->ngi", start_coef, seed_three, precision=HIGHEST)
        new_later = block_decay[:, :, None] * later + starts
        query_grad = (mixed_delta * conv_blk).astype(jnp.bfloat16)
        conv_grad = (mixed_delta * query_blk.astype(jnp.float32)).astype(jnp.bfloat16)
        gate_grad = (delta_blk * long_blk).astype(jnp.bfloat16)
        return new_later, (query_grad, conv_grad, gate_grad)

    def backward_sequence(inputs):
        start = jnp.zeros((ORDER, groups, GROUP), jnp.float32)
        final, outputs = lax.scan(backward_block, start, inputs, reverse=True)
        return outputs

    grads = lax.map(backward_sequence, (blocked(out_delta), blocked(gate), blocked(query), conv_all, long_all))
    query_grad, conv_grad, gate_grad = [item.reshape(TOKENS, D) for item in grads]

    def weight_block(total, inputs):
        delta_blk, gated_blk = inputs
        term = jnp.dot(delta_blk.T, gated_blk, preferred_element_type=jnp.float32)
        rounded = lax.optimization_barrier(term.astype(jnp.bfloat16))
        return total + rounded.astype(jnp.float32), None

    block_total = TOKENS // TOK_DEV
    weight_sum, unused = lax.scan(weight_block, jnp.zeros((D, D), jnp.float32),
                                  (out_grad.reshape(block_total, TOK_DEV, D), gated_all.reshape(block_total, TOK_DEV, D)))
    return query_grad, conv_grad, gate_grad, weight_sum.astype(jnp.bfloat16)
```

```python
import functools

import jax
import jax.numpy as jnp
from jax import lax
from jax.experimental import pallas as pl
from jax.experimental.pallas import tpu as pltpu
from jax.sharding import PartitionSpec as P

GROUP = 16
TAPS = 128
ORDER = 16
LANES = 128
PER_SLAB = LANES // GROUP
BF16 = jnp.bfloat16
F32 = jnp.float32
VMEM = 50 * 2**20


def call(body, name, flops, nbytes, **kwargs):
    return pl.pallas_call(
        body,
        name=name,
        cost_estimate=pl.CostEstimate(flops=flops, bytes_accessed=nbytes, transcendentals=0),
        compiler_params=pltpu.CompilerParams(vmem_limit_bytes=VMEM),
        **kwargs,
    )


def circulants(rows_ref, base):
    out = []
    for j in range(PER_SLAB):
        row = rows_ref[base + j : base + j + 1, :]
        out.append(
            pltpu.roll(jnp.broadcast_to(row, (LANES, LANES)), 0, 1, stride=1, stride_axis=0)
        )
    return out


def lower_mask():
    t = lax.broadcasted_iota(jnp.int32, (LANES, LANES), 0)
    u = lax.broadcasted_iota(jnp.int32, (LANES, LANES), 1)
    return u <= t


def pick_groups(stacked, rows):
    lane_group = lax.broadcasted_iota(jnp.int32, (rows, LANES), 1) // GROUP
    out = stacked[:rows]
    for j in range(1, PER_SLAB):
        out = jnp.where(lane_group == j, stacked[j * rows : (j + 1) * rows], out)
    return out


def spread_groups(state):
    tiled = jnp.concatenate([state] * PER_SLAB, axis=0)
    row_group = lax.broadcasted_iota(jnp.int32, (LANES, LANES), 0) // ORDER
    lane_group = lax.broadcasted_iota(jnp.int32, (LANES, LANES), 1) // GROUP
    return jnp.where(row_group == lane_group, tiled, jnp.zeros_like(tiled))


def dot(a, b):
    return jnp.dot(a, b, preferred_element_type=F32)


def conv_body(rim, own, query, taps, ends_coef, conv, mixed, ends):
    lower = lower_mask()
    for s in range(own.shape[1] // LANES):
        cols = slice(s * LANES, (s + 1) * LANES)
        blocks = []
        for circ in circulants(taps, s * PER_SLAB):
            zero = jnp.zeros_like(circ)
            blocks.append(
                jnp.concatenate(
                    [jnp.where(lower, zero, circ), jnp.where(lower, circ, zero)], axis=1
                ).astype(BF16)
            )
        ext = jnp.concatenate([rim[:, cols], own[:, cols]], axis=0)
        out = pick_groups(dot(jnp.concatenate(blocks, axis=0), ext), LANES)
        conv[:, cols] = out.astype(conv.dtype)
        mix = (query[:, cols].astype(F32) * out).astype(BF16)
        mixed[:, cols] = mix
        ends[:, cols] = pick_groups(
            dot(ends_coef[s * LANES : (s + 1) * LANES, :], mix), ORDER
        ).astype(ends.dtype)


def local_body(transposed, rows, x, out):
    lower = lower_mask()
    keep = ~lower | (lax.broadcasted_iota(jnp.int32, (LANES, LANES), 0)
                     == lax.broadcasted_iota(jnp.int32, (LANES, LANES), 1)) if transposed else lower
    for s in range(x.shape[1] // LANES):
        cols = slice(s * LANES, (s + 1) * LANES)
        blocks = [
            jnp.where(keep, circ, jnp.zeros_like(circ)).astype(BF16)
            for circ in circulants(rows, s * PER_SLAB)
        ]
        out[:, cols] = pick_groups(
            dot(jnp.concatenate(blocks, axis=0), x[:, cols]), LANES
        ).astype(out.dtype)


def carried(gathered, decay, coef, cols):
    state = jnp.sum(gathered[:, :, cols].astype(F32) * decay[:, :, cols], axis=0)
    return dot(coef[:, cols], spread_groups(state.astype(BF16)))


def long_body(local, gathered, decay, coef, gate, long_out, gated):
    for s in range(local.shape[1] // LANES):
        cols = slice(s * LANES, (s + 1) * LANES)
        out = local[:, cols].astype(F32) + carried(gathered, decay, coef, cols)
        long_out[:, cols] = out.astype(long_out.dtype)
        gated[:, cols] = (gate[:, cols].astype(F32) * out).astype(BF16)


def seed_body(delta, gate, long_out, starts_coef, seed, starts, gate_grad):
    for s in range(gate.shape[1] // LANES):
        cols = slice(s * LANES, (s + 1) * LANES)
        out = delta[:, cols].astype(F32)
        value = (out * gate[:, cols].astype(F32)).astype(BF16)
        seed[:, cols] = value
        starts[:, cols] = pick_groups(
            dot(starts_coef[s * LANES : (s + 1) * LANES, :], value), ORDER
        ).astype(starts.dtype)
        gate_grad[:, cols] = (out * long_out[:, cols].astype(F32)).astype(BF16)


def back_body(local, gathered, decay, coef, conv, query, query_grad, conv_grad):
    for s in range(local.shape[1] // LANES):
        cols = slice(s * LANES, (s + 1) * LANES)
        out = local[:, cols].astype(F32) + carried(gathered, decay, coef, cols)
        query_grad[:, cols] = (out * conv[:, cols].astype(F32)).astype(BF16)
        conv_grad[:, cols] = (out * query[:, cols].astype(F32)).astype(BF16)


def delta_body(grad, weight, out):
    depth = weight.shape[2]
    rows = grad[...].reshape(-1, grad.shape[-1])
    total = None
    for d in range(weight.shape[0]):
        term = lax.dot_general(
            rows[:, d * depth : (d + 1) * depth],
            weight[d],
            (((1,), (1,)), ((), ())),
            preferred_element_type=F32,
        )
        total = term if total is None else total + term
    out[...] = total.astype(out.dtype).reshape(out.shape)


def flip_body(grad, out):
    out[...] = grad[...].reshape(-1, grad.shape[-1]).T


def weight_body(grad_t, gated, out):
    out[0] = dot(grad_t[...], gated[...]).astype(out.dtype)


def wide(rows, lanes):
    return pl.BlockSpec((rows, lanes), lambda i: (0, i))


def tall(rows, cols):
    return pl.BlockSpec((rows, cols), lambda i: (i, 0))


def deep(count, rows, lanes):
    return pl.BlockSpec((count, rows, lanes), lambda i: (0, 0, i))


def shape(*dims, dtype=BF16):
    return jax.ShapeDtypeStruct(dims, dtype)


def on_device(query, key_in, value_in, gate, out_grad, proj_weight, mr_filter, lr_rate, lr_residue):
    rows, width = query.shape
    groups = width // GROUP
    n_dp, n_ctx, n_tp = (lax.axis_size(a) for a in ("dp", "ctx", "tp"))
    here = lax.axis_index("ctx")
    feats = proj_weight.shape[1]
    quarter = width // n_dp
    depth = n_dp * feats
    block = min(512, width)
    steps = width // block
    part = rows // n_tp

    product = (key_in.astype(F32) * value_in.astype(F32)).astype(BF16)
    rim = lax.ppermute(product, "ctx", [(i, i + 1) for i in range(n_ctx - 1)])
    mine = lax.dynamic_slice_in_dim(out_grad, lax.axis_index("tp") * part, part, axis=0)
    mine = mine.reshape(part, n_dp, n_ctx, feats).transpose(2, 0, 1, 3).reshape(n_ctx, part, depth)
    mine = lax.all_to_all(mine, "ctx", 0, 0, tiled=True)
    grad = lax.all_gather(mine, ("dp", "tp"), axis=0, tiled=False)
    grad = grad.reshape(n_dp, n_tp, n_ctx, part, depth)
    weight = lax.all_to_all(
        proj_weight.reshape(n_dp, quarter, feats), "dp", 0, 0, tiled=True
    )

    rate = lr_rate.reshape(-1, 1)
    residue = lr_residue.reshape(-1, 1)
    counts = jnp.arange(rows, dtype=F32)[None, :]
    ends_coef = jnp.exp(-rate * (rows - 1 - counts)).astype(BF16)
    starts_coef = jnp.exp(-rate * counts).astype(BF16)
    carry_coef = (residue.T * jnp.exp(-rate.T * (counts.T + 1))).astype(BF16)
    back_coef = (residue.T * jnp.exp(-rate.T * (rows - counts.T))).astype(BF16)
    kernel = jnp.sum(
        lr_residue[:, :, None] * jnp.exp(-lr_rate[:, :, None] * counts[:, None, :]), axis=1
    )

    def reversed_row(values):
        return jnp.roll(values[:, ::-1], 1, axis=1)

    taps = reversed_row(mr_filter.astype(F32))
    kernel_rev = reversed_row(kernel)
    lane_rate = jnp.repeat(lr_rate.T, GROUP, axis=1)[None]
    index = jnp.arange(n_ctx)[:, None, None]

    def decay_table(gap):
        powers = jnp.exp(-lane_rate * (rows * jnp.maximum(gap, 0)).astype(F32))
        return jnp.where(gap >= 0, powers, 0.0)

    decay_fwd = decay_table(here - 1 - index)
    decay_bwd = decay_table(index - here - 1)

    conv, mixed, ends = call(
        conv_body, "conv", 2 * rows * 256 * width * 8, rows * width * 10,
        grid=(steps,),
        in_specs=[wide(rows, block)] * 3 + [tall(block // GROUP, TAPS), tall(block, rows)],
        out_specs=[wide(rows, block), wide(rows, block), wide(ORDER, block)],
        out_shape=[shape(rows, width), shape(rows, width), shape(ORDER, width)],
    )(rim, product, query, taps, ends_coef)
    ends_all = lax.all_gather(ends, "ctx", axis=0)

    def local(transposed, table, x):
        return call(
            functools.partial(local_body, transposed),
            "local_t" if transposed else "local",
            2 * rows * 128 * width * 8, rows * width * 6,
            grid=(steps,),
            in_specs=[tall(block // GROUP, rows), wide(rows, block)],
            out_specs=wide(rows, block),
            out_shape=shape(rows, width, dtype=F32),
        )(table, x)

    local_fwd = local(False, kernel_rev, mixed)
    long_out, gated = call(
        long_body, "long", 2 * rows * 128 * width, rows * width * 10,
        grid=(steps,),
        in_specs=[wide(rows, block), deep(n_ctx, ORDER, block), deep(n_ctx, ORDER, block),
                  wide(rows, block), wide(rows, block)],
        out_specs=[wide(rows, block)] * 2,
        out_shape=[shape(rows, width)] * 2,
    )(local_fwd, ends_all, decay_fwd, carry_coef, gate)
    gated_all = lax.all_to_all(
        gated.reshape(rows, n_dp, quarter).transpose(1, 0, 2), "dp", 0, 0, tiled=True
    )
    gated_all = lax.all_gather(gated_all, "ctx", axis=0)
    tokens = n_ctx * n_dp * rows
    gated_all = gated_all.reshape(tokens, quarter)

    partial = call(
        delta_body, "delta", 2 * tokens * depth * quarter, 2 * tokens * (depth + quarter),
        grid=(n_ctx,),
        in_specs=[
            pl.BlockSpec((n_dp, n_tp, 1, part, depth), lambda i: (0, 0, i, 0, 0)),
            pl.BlockSpec((n_dp, quarter, feats), lambda i: (0, 0, 0)),
        ],
        out_specs=pl.BlockSpec((1, n_dp * rows, quarter), lambda i: (i, 0, 0)),
        out_shape=shape(n_ctx, n_dp * rows, quarter),
    )(grad, weight)
    partial = lax.all_to_all(partial, "ctx", 0, 0, tiled=True)
    delta = jnp.sum(partial.astype(F32), axis=0).astype(BF16)
    delta = lax.all_to_all(delta.reshape(n_dp, rows, quarter), "dp", 0, 0, tiled=True)
    delta = delta.transpose(1, 0, 2).reshape(rows, width)

    seed, starts, gate_grad = call(
        seed_body, "seed", 2 * rows * 128 * width, rows * width * 10,
        grid=(steps,),
        in_specs=[wide(rows, block)] * 3 + [tall(block, rows)],
        out_specs=[wide(rows, block), wide(ORDER, block), wide(rows, block)],
        out_shape=[shape(rows, width), shape(ORDER, width), shape(rows, width)],
    )(delta, gate, long_out, starts_coef)
    starts_all = lax.all_gather(starts, "ctx", axis=0)
    local_bwd = local(True, kernel, seed)
    query_grad, conv_grad = call(
        back_body, "back", 2 * rows * 128 * width, rows * width * 12,
        grid=(steps,),
        in_specs=[wide(rows, block), deep(n_ctx, ORDER, block), deep(n_ctx, ORDER, block),
                  wide(rows, block), wide(rows, block), wide(rows, block)],
        out_specs=[wide(rows, block)] * 2,
        out_shape=[shape(rows, width)] * 2,
    )(local_bwd, starts_all, decay_bwd, back_coef, conv, query)

    grad_t = call(
        flip_body, "flip", 0, 4 * tokens * depth,
        grid=(n_ctx, n_dp),
        in_specs=[pl.BlockSpec((1, n_tp, 1, part, depth), lambda i, j: (j, 0, i, 0, 0))],
        out_specs=pl.BlockSpec((depth, rows), lambda i, j: (0, i * n_dp + j)),
        out_shape=shape(depth, tokens),
    )(grad)
    weight_part = call(
        weight_body, "weight", 2 * tokens * depth * quarter, 2 * tokens * (depth + quarter),
        grid=(n_dp,),
        in_specs=[
            pl.BlockSpec((feats, tokens), lambda i: (i, 0)),
            pl.BlockSpec((tokens, quarter), lambda i: (0, 0)),
        ],
        out_specs=pl.BlockSpec((1, feats, quarter), lambda i: (i, 0, 0)),
        out_shape=shape(n_dp, feats, quarter),
    )(grad_t, gated_all)
    weight_grad = lax.all_to_all(weight_part, "dp", 0, 0, tiled=True)
    weight_grad = weight_grad.transpose(1, 0, 2).reshape(feats, width)
    return query_grad, conv_grad, gate_grad, weight_grad


def solution(mesh):
    rows = P(("dp", "ctx"), "tp")
    return jax.shard_map(
        on_device,
        mesh=mesh,
        in_specs=(rows, rows, rows, rows, P(("dp", "ctx"), None), P("tp", ("dp", "ctx")),
                  P("tp", None), P("tp", None), P("tp", None)),
        out_specs=(rows, rows, rows, rows),
        check_vma=False,
    )
```

```python
import functools

import jax
import jax.numpy as jnp
from jax import lax
from jax.experimental import pallas as pl
from jax.experimental.pallas import tpu as pltpu
from jax.sharding import PartitionSpec as P

GROUP = 16
TAPS = 128
ORDER = 16
LANES = 128
PER_SLAB = LANES // GROUP
BF16 = jnp.bfloat16
F32 = jnp.float32
VMEM = 50 * 2**20


def call(body, name, flops, nbytes, **kwargs):
    return pl.pallas_call(
        body,
        name=name,
        cost_estimate=pl.CostEstimate(flops=flops, bytes_accessed=nbytes, transcendentals=0),
        compiler_params=pltpu.CompilerParams(vmem_limit_bytes=VMEM),
        **kwargs,
    )


def circulants(rows_ref, base):
    out = []
    for j in range(PER_SLAB):
        row = rows_ref[base + j : base + j + 1, :]
        out.append(
            pltpu.roll(jnp.broadcast_to(row, (LANES, LANES)), 0, 1, stride=1, stride_axis=0)
        )
    return out


def lower_mask():
    t = lax.broadcasted_iota(jnp.int32, (LANES, LANES), 0)
    u = lax.broadcasted_iota(jnp.int32, (LANES, LANES), 1)
    return u <= t


def pick_groups(stacked, rows):
    lane_group = lax.broadcasted_iota(jnp.int32, (rows, LANES), 1) // GROUP
    out = stacked[:rows]
    for j in range(1, PER_SLAB):
        out = jnp.where(lane_group == j, stacked[j * rows : (j + 1) * rows], out)
    return out


def spread_groups(state):
    tiled = jnp.concatenate([state] * PER_SLAB, axis=0)
    row_group = lax.broadcasted_iota(jnp.int32, (LANES, LANES), 0) // ORDER
    lane_group = lax.broadcasted_iota(jnp.int32, (LANES, LANES), 1) // GROUP
    return jnp.where(row_group == lane_group, tiled, jnp.zeros_like(tiled))


def dot(a, b):
    return jnp.dot(a, b, preferred_element_type=F32)


def conv_body(rim, own_part, query, taps, ends_coef, conv, mixed, ends):
    lower = lower_mask()
    for s in range(rim.shape[1] // LANES):
        cols = slice(s * LANES, (s + 1) * LANES)
        blocks = [
            jnp.where(lower, jnp.zeros_like(circ), circ).astype(BF16)
            for circ in circulants(taps, s * PER_SLAB)
        ]
        out = own_part[:, cols] + pick_groups(
            dot(jnp.concatenate(blocks, axis=0), rim[:, cols]), LANES
        )
        conv[:, cols] = out.astype(conv.dtype)
        mix = (query[:, cols].astype(F32) * out).astype(BF16)
        mixed[:, cols] = mix
        ends[:, cols] = pick_groups(
            dot(ends_coef[s * LANES : (s + 1) * LANES, :], mix), ORDER
        ).astype(ends.dtype)


def local_body(transposed, rows, x, out):
    lower = lower_mask()
    keep = ~lower | (lax.broadcasted_iota(jnp.int32, (LANES, LANES), 0)
                     == lax.broadcasted_iota(jnp.int32, (LANES, LANES), 1)) if transposed else lower
    for s in range(x.shape[1] // LANES):
        cols = slice(s * LANES, (s + 1) * LANES)
        blocks = [
            jnp.where(keep, circ, jnp.zeros_like(circ)).astype(BF16)
            for circ in circulants(rows, s * PER_SLAB)
        ]
        out[:, cols] = pick_groups(
            dot(jnp.concatenate(blocks, axis=0), x[:, cols]), LANES
        ).astype(out.dtype)


def carried(gathered, decay, coef, cols):
    state = jnp.sum(gathered[:, :, cols].astype(F32) * decay[:, :, cols], axis=0)
    return dot(coef[:, cols], spread_groups(state.astype(BF16)))


def long_body(local, gathered, decay, coef, gate, long_out, gated):
    for s in range(local.shape[1] // LANES):
        cols = slice(s * LANES, (s + 1) * LANES)
        out = local[:, cols].astype(F32) + carried(gathered, decay, coef, cols)
        long_out[:, cols] = out.astype(long_out.dtype)
        gated[0, :, cols] = (gate[:, cols].astype(F32) * out).astype(BF16)


def seed_body(delta, gate, long_out, starts_coef, seed, starts, gate_grad):
    for s in range(gate.shape[1] // LANES):
        cols = slice(s * LANES, (s + 1) * LANES)
        out = jnp.sum(delta[0, :, :, cols].astype(F32), axis=0)
        value = (out * gate[:, cols].astype(F32)).astype(BF16)
        seed[:, cols] = value
        starts[:, cols] = pick_groups(
            dot(starts_coef[s * LANES : (s + 1) * LANES, :], value), ORDER
        ).astype(starts.dtype)
        gate_grad[:, cols] = (out * long_out[:, cols].astype(F32)).astype(BF16)


def back_body(local, gathered, decay, coef, conv, query, query_grad, conv_grad):
    for s in range(local.shape[1] // LANES):
        cols = slice(s * LANES, (s + 1) * LANES)
        out = local[:, cols].astype(F32) + carried(gathered, decay, coef, cols)
        query_grad[:, cols] = (out * conv[:, cols].astype(F32)).astype(BF16)
        conv_grad[:, cols] = (out * query[:, cols].astype(F32)).astype(BF16)


def pack_body(place, *refs):
    count = len(refs) // 2
    for source, target in zip(refs[:count], refs[count:]):
        target[...] = source[...]


def delta_body(place, grad, *refs):
    weights, out = refs[:-1], refs[-1]
    depth = weights[0].shape[1]
    total = None
    for k, weight in enumerate(weights):
        start = pl.multiple_of((place[0] ^ k) * depth, depth)
        rows = grad[:, :, :, :, pl.ds(start, depth)].reshape(-1, depth)
        term = lax.dot_general(
            rows, weight[...], (((1,), (1,)), ((), ())), preferred_element_type=F32
        )
        total = term if total is None else total + term
    out[...] = total.astype(out.dtype).reshape(out.shape)


def flip_body(place, grad, out):
    out[...] = grad[...].reshape(-1, grad.shape[-1]).T


def lay_body(source, target):
    target[...] = source[0]


def weight_body(grad_t, gated, out):
    out[0] = dot(grad_t[...], gated[...]).astype(out.dtype)


def wide(rows, lanes):
    return pl.BlockSpec((rows, lanes), lambda i: (0, i))


def tall(rows, cols):
    return pl.BlockSpec((rows, cols), lambda i: (i, 0))


def deep(count, rows, lanes):
    return pl.BlockSpec((count, rows, lanes), lambda i: (0, 0, i))


def shape(*dims, dtype=BF16):
    return jax.ShapeDtypeStruct(dims, dtype)


def on_device(query, key_in, value_in, gate, out_grad, proj_weight, mr_filter, lr_rate, lr_residue):
    rows, width = query.shape
    groups = width // GROUP
    n_dp, n_ctx, n_tp = (lax.axis_size(a) for a in ("dp", "ctx", "tp"))
    here = lax.axis_index("ctx")
    feats = proj_weight.shape[1]
    quarter = width // n_dp
    depth = n_dp * feats
    block = min(512, quarter)
    steps = width // block
    per = quarter // block

    def split_at(i):
        return (i // per, 0, i % per)

    part = rows // n_tp

    place = jnp.stack([lax.axis_index(a) for a in ("dp", "ctx", "tp")]).astype(jnp.int32)

    def swap(value, axis, k):
        return lax.ppermute(value, axis, [(i, i ^ k) for i in range(lax.axis_size(axis))])

    def piece(k):
        return pl.BlockSpec((part, feats), lambda j, p: (p[2], j * n_ctx + (p[1] ^ k)))

    mine = call(
        pack_body, "pack", 0, 4 * part * depth * n_ctx,
        grid_spec=pltpu.PrefetchScalarGridSpec(
            num_scalar_prefetch=1, grid=(n_dp,),
            in_specs=[piece(k) for k in range(n_ctx)],
            out_specs=[pl.BlockSpec((part, feats), lambda j, p: (0, j))] * n_ctx,
        ),
        out_shape=[shape(part, depth)] * n_ctx,
    )(place, *[out_grad] * n_ctx)
    mine = [mine[0]] + [swap(mine[k], "ctx", k) for k in range(1, n_ctx)]
    weights = [proj_weight] + [
        swap(lax.dynamic_slice_in_dim(proj_weight, (place[0] ^ k) * quarter, quarter), "dp", k)
        for k in range(1, n_dp)
    ]
    product = (key_in.astype(F32) * value_in.astype(F32)).astype(BF16)
    rim = lax.ppermute(product, "ctx", [(i, i + 1) for i in range(n_ctx - 1)])
    grad = lax.all_gather(jnp.stack(mine), ("dp", "tp"), axis=0, tiled=False)
    grad = grad.reshape(n_dp, n_tp, n_ctx, part, depth)

    rate = lr_rate.reshape(-1, 1)
    residue = lr_residue.reshape(-1, 1)
    counts = jnp.arange(rows, dtype=F32)[None, :]
    ends_coef = jnp.exp(-rate * (rows - 1 - counts)).astype(BF16)
    starts_coef = jnp.exp(-rate * counts).astype(BF16)
    carry_coef = (residue.T * jnp.exp(-rate.T * (counts.T + 1))).astype(BF16)
    back_coef = (residue.T * jnp.exp(-rate.T * (rows - counts.T))).astype(BF16)
    kernel = jnp.sum(
        lr_residue[:, :, None] * jnp.exp(-lr_rate[:, :, None] * counts[:, None, :]), axis=1
    )

    def reversed_row(values):
        return jnp.roll(values[:, ::-1], 1, axis=1)

    taps = reversed_row(mr_filter.astype(F32))
    kernel_rev = reversed_row(kernel)
    lane_rate = jnp.repeat(lr_rate.T, GROUP, axis=1)[None]
    index = jnp.arange(n_ctx)[:, None, None]

    def decay_table(gap):
        powers = jnp.exp(-lane_rate * (rows * jnp.maximum(gap, 0)).astype(F32))
        return jnp.where(gap >= 0, powers, 0.0)

    decay_fwd = decay_table(here - 1 - index)
    decay_bwd = decay_table(index - here - 1)

    def local(transposed, table, x):
        return call(
            functools.partial(local_body, transposed),
            "local_t" if transposed else "local",
            2 * rows * 128 * width * 8, rows * width * 6,
            grid=(steps,),
            in_specs=[tall(block // GROUP, rows), wide(rows, block)],
            out_specs=wide(rows, block),
            out_shape=shape(rows, width, dtype=F32),
        )(table, x)

    conv_own = local(False, taps, product)
    conv, mixed, ends = call(
        conv_body, "conv", 2 * rows * 128 * width * 8, rows * width * 14,
        grid=(steps,),
        in_specs=[wide(rows, block)] * 3 + [tall(block // GROUP, TAPS), tall(block, rows)],
        out_specs=[wide(rows, block), wide(rows, block), wide(ORDER, block)],
        out_shape=[shape(rows, width), shape(rows, width), shape(ORDER, width)],
    )(rim, conv_own, query, taps, ends_coef)
    ends_all = lax.all_gather(ends, "ctx", axis=0)

    local_fwd = local(False, kernel_rev, mixed)
    long_out, gated = call(
        long_body, "long", 2 * rows * 128 * width, rows * width * 10,
        grid=(steps,),
        in_specs=[wide(rows, block), deep(n_ctx, ORDER, block), deep(n_ctx, ORDER, block),
                  wide(rows, block), wide(rows, block)],
        out_specs=[wide(rows, block), pl.BlockSpec((1, rows, block), split_at)],
        out_shape=[shape(rows, width), shape(n_dp, rows, quarter)],
    )(local_fwd, ends_all, decay_fwd, carry_coef, gate)
    gated_all = lax.all_to_all(gated, "dp", 0, 0, tiled=True)
    gated_all = lax.all_gather(gated_all, "ctx", axis=0)
    tokens = n_ctx * n_dp * rows
    gated_all = gated_all.reshape(tokens, quarter)

    partial = call(
        delta_body, "delta", 2 * tokens * depth * quarter, 2 * tokens * (depth + quarter),
        grid_spec=pltpu.PrefetchScalarGridSpec(
            num_scalar_prefetch=1, grid=(n_ctx,),
            in_specs=[
                pl.BlockSpec((n_dp, n_tp, 1, part, depth), lambda i, p: (0, 0, i, 0, 0)),
                pl.BlockSpec((quarter, feats), lambda i, p: (p[0], 0)),
            ] + [pl.BlockSpec((quarter, feats), lambda i, p: (0, 0))] * (n_dp - 1),
            out_specs=pl.BlockSpec(
                (n_dp, 1, rows, quarter), lambda i, p: (0, p[1] ^ i, 0, 0)
            ),
        ),
        out_shape=shape(n_dp, n_ctx, rows, quarter),
    )(place, grad, *weights)
    delta = lax.all_to_all(
        partial.reshape(n_dp * n_ctx, rows, quarter), ("dp", "ctx"), 0, 0, tiled=True
    ).reshape(n_dp, n_ctx, rows, quarter)

    seed, starts, gate_grad = call(
        seed_body, "seed", 2 * rows * 128 * width, rows * width * 10,
        grid=(steps,),
        in_specs=[
            pl.BlockSpec((1, n_ctx, rows, block), lambda i: (i // per, 0, 0, i % per)),
            wide(rows, block), wide(rows, block), tall(block, rows),
        ],
        out_specs=[wide(rows, block), wide(ORDER, block), wide(rows, block)],
        out_shape=[shape(rows, width), shape(ORDER, width), shape(rows, width)],
    )(delta, gate, long_out, starts_coef)
    starts_all = lax.all_gather(starts, "ctx", axis=0)
    local_bwd = local(True, kernel, seed)
    query_grad, conv_grad = call(
        back_body, "back", 2 * rows * 128 * width, rows * width * 12,
        grid=(steps,),
        in_specs=[wide(rows, block), deep(n_ctx, ORDER, block), deep(n_ctx, ORDER, block),
                  wide(rows, block), wide(rows, block), wide(rows, block)],
        out_specs=[wide(rows, block)] * 2,
        out_shape=[shape(rows, width)] * 2,
    )(local_bwd, starts_all, decay_bwd, back_coef, conv, query)

    grad_t = call(
        flip_body, "flip", 0, 4 * tokens * depth,
        grid_spec=pltpu.PrefetchScalarGridSpec(
            num_scalar_prefetch=1, grid=(n_ctx, n_dp),
            in_specs=[
                pl.BlockSpec(
                    (1, n_tp, 1, part, depth), lambda i, j, p: (j, 0, p[1] ^ i, 0, 0)
                )
            ],
            out_specs=pl.BlockSpec((depth, rows), lambda i, j, p: (0, i * n_dp + j)),
        ),
        out_shape=shape(depth, tokens),
    )(place, grad)
    weight_part = call(
        weight_body, "weight", 2 * tokens * depth * quarter, 2 * tokens * (depth + quarter),
        grid=(n_dp,),
        in_specs=[
            pl.BlockSpec((feats, tokens), lambda i: (i, 0)),
            pl.BlockSpec((tokens, quarter), lambda i: (0, 0)),
        ],
        out_specs=pl.BlockSpec((1, feats, quarter), lambda i: (i, 0, 0)),
        out_shape=shape(n_dp, feats, quarter),
    )(grad_t, gated_all)
    weight_grad = lax.all_to_all(weight_part, "dp", 0, 0, tiled=True)
    weight_grad = call(
        lay_body, "lay", 0, 4 * feats * width,
        grid=(n_dp,),
        in_specs=[pl.BlockSpec((1, feats, quarter), lambda i: (i, 0, 0))],
        out_specs=pl.BlockSpec((feats, quarter), lambda i: (0, i)),
        out_shape=shape(feats, width),
    )(weight_grad)
    return query_grad, conv_grad, gate_grad, weight_grad


def solution(mesh):
    rows = P(("dp", "ctx"), "tp")
    return jax.shard_map(
        on_device,
        mesh=mesh,
        in_specs=(rows, rows, rows, rows, P(("dp", "ctx"), None), P("tp", ("dp", "ctx")),
                  P("tp", None), P("tp", None), P("tp", None)),
        out_specs=(rows, rows, rows, rows),
        check_vma=False,
    )
```

```python
import functools

import jax
import jax.numpy as jnp
from jax import lax
from jax.experimental import pallas as pl
from jax.experimental.pallas import tpu as pltpu
from jax.sharding import PartitionSpec as P

GROUP = 16
TAPS = 128
ORDER = 16
LANES = 128
PER_SLAB = LANES // GROUP
BF16 = jnp.bfloat16
F32 = jnp.float32
VMEM = 50 * 2**20
ANY = pl.BlockSpec(memory_space=pl.ANY)


def call(body, name, flops, nbytes, **kwargs):
    return pl.pallas_call(
        body,
        name=name,
        cost_estimate=pl.CostEstimate(flops=flops, bytes_accessed=nbytes, transcendentals=0),
        compiler_params=pltpu.CompilerParams(vmem_limit_bytes=VMEM),
        **kwargs,
    )


def circulants(rows_ref, base):
    out = []
    for j in range(PER_SLAB):
        row = rows_ref[base + j : base + j + 1, :]
        out.append(
            pltpu.roll(jnp.broadcast_to(row, (LANES, LANES)), 0, 1, stride=1, stride_axis=0)
        )
    return out


def lower_mask():
    t = lax.broadcasted_iota(jnp.int32, (LANES, LANES), 0)
    u = lax.broadcasted_iota(jnp.int32, (LANES, LANES), 1)
    return u <= t


def pick_groups(stacked, rows):
    lane_group = lax.broadcasted_iota(jnp.int32, (rows, LANES), 1) // GROUP
    out = stacked[:rows]
    for j in range(1, PER_SLAB):
        out = jnp.where(lane_group == j, stacked[j * rows : (j + 1) * rows], out)
    return out


def spread_groups(state):
    tiled = jnp.concatenate([state] * PER_SLAB, axis=0)
    row_group = lax.broadcasted_iota(jnp.int32, (LANES, LANES), 0) // ORDER
    lane_group = lax.broadcasted_iota(jnp.int32, (LANES, LANES), 1) // GROUP
    return jnp.where(row_group == lane_group, tiled, jnp.zeros_like(tiled))


def dot(a, b):
    return jnp.dot(a, b, preferred_element_type=F32)


def conv_body(rim, own_part, query, taps, ends_coef, *refs):
    conv, mixed, ends = refs[-3:]
    lower = lower_mask()
    for s in range(rim.shape[1] // LANES):
        cols = slice(s * LANES, (s + 1) * LANES)
        blocks = [
            jnp.where(lower, jnp.zeros_like(circ), circ).astype(BF16)
            for circ in circulants(taps, s * PER_SLAB)
        ]
        out = own_part[:, cols] + pick_groups(
            dot(jnp.concatenate(blocks, axis=0), rim[:, cols]), LANES
        )
        conv[:, cols] = out.astype(conv.dtype)
        mix = (query[:, cols].astype(F32) * out).astype(BF16)
        mixed[:, cols] = mix
        ends[:, cols] = pick_groups(
            dot(ends_coef[s * LANES : (s + 1) * LANES, :], mix), ORDER
        ).astype(ends.dtype)


def local_body(transposed, rows, x, out):
    lower = lower_mask()
    keep = ~lower | (lax.broadcasted_iota(jnp.int32, (LANES, LANES), 0)
                     == lax.broadcasted_iota(jnp.int32, (LANES, LANES), 1)) if transposed else lower
    for s in range(x.shape[1] // LANES):
        cols = slice(s * LANES, (s + 1) * LANES)
        blocks = [
            jnp.where(keep, circ, jnp.zeros_like(circ)).astype(BF16)
            for circ in circulants(rows, s * PER_SLAB)
        ]
        out[:, cols] = pick_groups(
            dot(jnp.concatenate(blocks, axis=0), x[:, cols]), LANES
        ).astype(out.dtype)


def carried(states, decay, coef, cols):
    state = sum(ref[:, cols].astype(F32) * decay[k, :, cols] for k, ref in enumerate(states))
    return dot(coef[:, cols], spread_groups(state.astype(BF16)))


def long_body(count, local, decay, coef, gate, *refs):
    states, (long_out, gated) = refs[:count], refs[-2:]
    for s in range(local.shape[1] // LANES):
        cols = slice(s * LANES, (s + 1) * LANES)
        out = local[:, cols].astype(F32) + carried(states, decay, coef, cols)
        long_out[:, cols] = out.astype(long_out.dtype)
        gated[0, :, cols] = (gate[:, cols].astype(F32) * out).astype(BF16)


def seed_body(delta, gate, long_out, starts_coef, seed, starts, gate_grad):
    for s in range(gate.shape[1] // LANES):
        cols = slice(s * LANES, (s + 1) * LANES)
        out = jnp.sum(delta[0, :, :, cols].astype(F32), axis=0)
        value = (out * gate[:, cols].astype(F32)).astype(BF16)
        seed[:, cols] = value
        starts[:, cols] = pick_groups(
            dot(starts_coef[s * LANES : (s + 1) * LANES, :], value), ORDER
        ).astype(starts.dtype)
        gate_grad[:, cols] = (out * long_out[:, cols].astype(F32)).astype(BF16)


def back_body(count, local, decay, coef, conv, query, *refs):
    states, (query_grad, conv_grad) = refs[:count], refs[-2:]
    for s in range(local.shape[1] // LANES):
        cols = slice(s * LANES, (s + 1) * LANES)
        out = local[:, cols].astype(F32) + carried(states, decay, coef, cols)
        query_grad[:, cols] = (out * conv[:, cols].astype(F32)).astype(BF16)
        conv_grad[:, cols] = (out * query[:, cols].astype(F32)).astype(BF16)


def pack_body(place, *refs):
    count = len(refs) // 2
    for source, target in zip(refs[:count], refs[count:]):
        target[...] = source[...]


def join_body(*refs):
    out = refs[-1]
    for k in range(out.shape[0]):
        out[k] = refs[k][...]


def delta_body(place, grad, *refs):
    weights, out = refs[:-1], refs[-1]
    depth = weights[0].shape[1]
    total = None
    for k, weight in enumerate(weights):
        start = pl.multiple_of((place[0] ^ k) * depth, depth)
        rows = grad[:, :, :, :, pl.ds(start, depth)].reshape(-1, depth)
        term = lax.dot_general(
            rows, weight[...], (((1,), (1,)), ((), ())), preferred_element_type=F32
        )
        total = term if total is None else total + term
    out[...] = total.astype(out.dtype).reshape(out.shape)


def flip_body(place, grad, after, out):
    out[...] = grad[...].reshape(-1, grad.shape[-1]).T


def lay_body(source, target):
    target[...] = source[0]


def weight_body(grad_t, gated, out):
    out[0] = dot(grad_t[...], gated[...]).astype(out.dtype)


def wide(rows, lanes):
    return pl.BlockSpec((rows, lanes), lambda i: (0, i))


def tall(rows, cols):
    return pl.BlockSpec((rows, cols), lambda i: (i, 0))


def deep(count, rows, lanes):
    return pl.BlockSpec((count, rows, lanes), lambda i: (0, 0, i))


def shape(*dims, dtype=BF16):
    return jax.ShapeDtypeStruct(dims, dtype)


def on_device(query, key_in, value_in, gate, out_grad, proj_weight, mr_filter, lr_rate, lr_residue):
    rows, width = query.shape
    groups = width // GROUP
    n_dp, n_ctx, n_tp = (lax.axis_size(a) for a in ("dp", "ctx", "tp"))
    feats = proj_weight.shape[1]
    quarter = width // n_dp
    depth = n_dp * feats
    block = min(512, quarter)
    steps = width // block
    per = quarter // block

    def split_at(i):
        return (i // per, 0, i % per)

    part = rows // n_tp

    place = jnp.stack([lax.axis_index(a) for a in ("dp", "ctx", "tp")]).astype(jnp.int32)

    def swap(value, axis, k):
        return lax.ppermute(value, axis, [(i, i ^ k) for i in range(lax.axis_size(axis))])

    def shift(value, k):
        ends = [(i, i + k) for i in range(n_ctx) if 0 <= i + k < n_ctx]
        return lax.ppermute(value, "ctx", ends)

    def piece(k):
        return pl.BlockSpec((part, feats), lambda j, p: (p[2], j * n_ctx + (p[1] ^ k)))

    mine = call(
        pack_body, "pack", 0, 4 * part * depth * n_ctx,
        grid_spec=pltpu.PrefetchScalarGridSpec(
            num_scalar_prefetch=1, grid=(n_dp,),
            in_specs=[piece(k) for k in range(n_ctx)],
            out_specs=[pl.BlockSpec((part, feats), lambda j, p: (0, j))] * n_ctx,
        ),
        out_shape=[shape(part, depth)] * n_ctx,
    )(place, *[out_grad] * n_ctx)
    mine = [mine[0]] + [swap(mine[k], "ctx", k) for k in range(1, n_ctx)]
    weights = [proj_weight] + [
        swap(lax.dynamic_slice_in_dim(proj_weight, (place[0] ^ k) * quarter, quarter), "dp", k)
        for k in range(1, n_dp)
    ]
    product = (key_in.astype(F32) * value_in.astype(F32)).astype(BF16)
    rim = shift(product, 1)
    mine = call(
        join_body, "join", 0, 4 * part * depth * n_ctx,
        grid=(n_dp,),
        in_specs=[wide(part, feats)] * n_ctx + [ANY] * (n_dp - 2),
        out_specs=deep(n_ctx, part, feats),
        out_shape=shape(n_ctx, part, depth),
    )(*mine, *weights[1:-1])
    grad = lax.all_gather(mine, ("dp", "tp"), axis=0, tiled=False)
    grad = grad.reshape(n_dp, n_tp, n_ctx, part, depth)

    rate = lr_rate.reshape(-1, 1)
    residue = lr_residue.reshape(-1, 1)
    counts = jnp.arange(rows, dtype=F32)[None, :]
    ends_coef = jnp.exp(-rate * (rows - 1 - counts)).astype(BF16)
    starts_coef = jnp.exp(-rate * counts).astype(BF16)
    carry_coef = (residue.T * jnp.exp(-rate.T * (counts.T + 1))).astype(BF16)
    back_coef = (residue.T * jnp.exp(-rate.T * (rows - counts.T))).astype(BF16)
    kernel = jnp.sum(
        lr_residue[:, :, None] * jnp.exp(-lr_rate[:, :, None] * counts[:, None, :]), axis=1
    )

    def reversed_row(values):
        return jnp.roll(values[:, ::-1], 1, axis=1)

    taps = reversed_row(mr_filter.astype(F32))
    kernel_rev = reversed_row(kernel)
    lane_rate = jnp.repeat(lr_rate.T, GROUP, axis=1)[None]
    blocks_away = jnp.arange(n_ctx - 1, dtype=F32)[:, None, None]
    decay = jnp.exp(-lane_rate * (rows * blocks_away))

    def local(transposed, table, x):
        return call(
            functools.partial(local_body, transposed),
            "local_t" if transposed else "local",
            2 * rows * 128 * width * 8, rows * width * 6,
            grid=(steps,),
            in_specs=[tall(block // GROUP, rows), wide(rows, block)],
            out_specs=wide(rows, block),
            out_shape=shape(rows, width, dtype=F32),
        )(table, x)

    late = weights[-1:]
    conv_own = local(False, taps, product)
    conv, mixed, ends = call(
        conv_body, "conv", 2 * rows * 128 * width * 8, rows * width * 14,
        grid=(steps,),
        in_specs=[wide(rows, block)] * 3 + [tall(block // GROUP, TAPS), tall(block, rows)],
        out_specs=[wide(rows, block), wide(rows, block), wide(ORDER, block)],
        out_shape=[shape(rows, width), shape(rows, width), shape(ORDER, width)],
    )(rim, conv_own, query, taps, ends_coef)
    ends_far = [shift(ends, k) for k in range(1, n_ctx)]

    local_fwd = local(False, kernel_rev, mixed)
    long_out, gated = call(
        functools.partial(long_body, n_ctx - 1), "long", 2 * rows * 128 * width, rows * width * 10,
        grid=(steps,),
        in_specs=[wide(rows, block), deep(n_ctx - 1, ORDER, block), wide(rows, block),
                  wide(rows, block)] + [wide(ORDER, block)] * (n_ctx - 1) + [ANY] * len(late),
        out_specs=[wide(rows, block), pl.BlockSpec((1, rows, block), split_at)],
        out_shape=[shape(rows, width), shape(n_dp, rows, quarter)],
    )(local_fwd, decay, carry_coef, gate, *ends_far, *late)
    gated_all = lax.all_to_all(gated, "dp", 0, 0, tiled=True)
    gated_all = lax.all_gather(gated_all, "ctx", axis=0)
    tokens = n_ctx * n_dp * rows
    gated_all = gated_all.reshape(tokens, quarter)

    partial = call(
        delta_body, "delta", 2 * tokens * depth * quarter, 2 * tokens * (depth + quarter),
        grid_spec=pltpu.PrefetchScalarGridSpec(
            num_scalar_prefetch=1, grid=(n_ctx,),
            in_specs=[
                pl.BlockSpec((n_dp, n_tp, 1, part, depth), lambda i, p: (0, 0, i, 0, 0)),
                pl.BlockSpec((quarter, feats), lambda i, p: (p[0], 0)),
            ] + [pl.BlockSpec((quarter, feats), lambda i, p: (0, 0))] * (n_dp - 1),
            out_specs=pl.BlockSpec(
                (n_dp, 1, rows, quarter), lambda i, p: (0, p[1] ^ i, 0, 0)
            ),
        ),
        out_shape=shape(n_dp, n_ctx, rows, quarter),
    )(place, grad, *weights)
    delta = lax.all_to_all(
        partial.reshape(n_dp * n_ctx, rows, quarter), ("dp", "ctx"), 0, 0, tiled=True
    ).reshape(n_dp, n_ctx, rows, quarter)

    seed, starts, gate_grad = call(
        seed_body, "seed", 2 * rows * 128 * width, rows * width * 10,
        grid=(steps,),
        in_specs=[
            pl.BlockSpec((1, n_ctx, rows, block), lambda i: (i // per, 0, 0, i % per)),
            wide(rows, block), wide(rows, block), tall(block, rows),
        ],
        out_specs=[wide(rows, block), wide(ORDER, block), wide(rows, block)],
        out_shape=[shape(rows, width), shape(ORDER, width), shape(rows, width)],
    )(delta, gate, long_out, starts_coef)
    starts_far = [shift(starts, -k) for k in range(1, n_ctx)]
    local_bwd = local(True, kernel, seed)
    query_grad, conv_grad = call(
        functools.partial(back_body, n_ctx - 1), "back", 2 * rows * 128 * width, rows * width * 12,
        grid=(steps,),
        in_specs=[wide(rows, block), deep(n_ctx - 1, ORDER, block)] + [wide(rows, block)] * 3
        + [wide(ORDER, block)] * (n_ctx - 1),
        out_specs=[wide(rows, block)] * 2,
        out_shape=[shape(rows, width)] * 2,
    )(local_bwd, decay, back_coef, conv, query, *starts_far)

    grad_t = call(
        flip_body, "flip", 0, 4 * tokens * depth,
        grid_spec=pltpu.PrefetchScalarGridSpec(
            num_scalar_prefetch=1, grid=(n_ctx, n_dp),
            in_specs=[
                pl.BlockSpec(
                    (1, n_tp, 1, part, depth), lambda i, j, p: (j, 0, p[1] ^ i, 0, 0)
                ),
                ANY,
            ],
            out_specs=pl.BlockSpec((depth, rows), lambda i, j, p: (0, i * n_dp + j)),
        ),
        out_shape=shape(depth, tokens),
    )(place, grad, partial)
    weight_part = call(
        weight_body, "weight", 2 * tokens * depth * quarter, 2 * tokens * (depth + quarter),
        grid=(n_dp,),
        in_specs=[
            pl.BlockSpec((feats, tokens), lambda i: (i, 0)),
            pl.BlockSpec((tokens, quarter), lambda i: (0, 0)),
        ],
        out_specs=pl.BlockSpec((1, feats, quarter), lambda i: (i, 0, 0)),
        out_shape=shape(n_dp, feats, quarter),
    )(grad_t, gated_all)
    weight_grad = lax.all_to_all(weight_part, "dp", 0, 0, tiled=True)
    weight_grad = call(
        lay_body, "lay", 0, 4 * feats * width,
        grid=(n_dp,),
        in_specs=[pl.BlockSpec((1, feats, quarter), lambda i: (i, 0, 0))],
        out_specs=pl.BlockSpec((feats, quarter), lambda i: (0, i)),
        out_shape=shape(feats, width),
    )(weight_grad)
    return query_grad, conv_grad, gate_grad, weight_grad


def solution(mesh):
    rows = P(("dp", "ctx"), "tp")
    return jax.shard_map(
        on_device,
        mesh=mesh,
        in_specs=(rows, rows, rows, rows, P(("dp", "ctx"), None), P("tp", ("dp", "ctx")),
                  P("tp", None), P("tp", None), P("tp", None)),
        out_specs=(rows, rows, rows, rows),
        check_vma=False,
    )
```

```python
import functools

import jax
import jax.numpy as jnp
from jax import lax
from jax.experimental import pallas as pl
from jax.experimental.pallas import tpu as pltpu
from jax.sharding import PartitionSpec as P

GROUP = 16
TAPS = 128
ORDER = 16
LANES = 128
PER_SLAB = LANES // GROUP
BF16 = jnp.bfloat16
F32 = jnp.float32
VMEM = 50 * 2**20
ANY = pl.BlockSpec(memory_space=pl.ANY)


def call(body, name, flops, nbytes, **kwargs):
    return pl.pallas_call(
        body,
        name=name,
        cost_estimate=pl.CostEstimate(flops=flops, bytes_accessed=nbytes, transcendentals=0),
        compiler_params=pltpu.CompilerParams(vmem_limit_bytes=VMEM),
        **kwargs,
    )


def circulants(rows_ref, base):
    out = []
    for j in range(PER_SLAB):
        row = rows_ref[base + j : base + j + 1, :]
        out.append(
            pltpu.roll(jnp.broadcast_to(row, (LANES, LANES)), 0, 1, stride=1, stride_axis=0)
        )
    return out


def lower_mask():
    t = lax.broadcasted_iota(jnp.int32, (LANES, LANES), 0)
    u = lax.broadcasted_iota(jnp.int32, (LANES, LANES), 1)
    return u <= t


def pick_groups(stacked, rows):
    lane_group = lax.broadcasted_iota(jnp.int32, (rows, LANES), 1) // GROUP
    out = stacked[:rows]
    for j in range(1, PER_SLAB):
        out = jnp.where(lane_group == j, stacked[j * rows : (j + 1) * rows], out)
    return out


def spread_groups(state):
    tiled = jnp.concatenate([state] * PER_SLAB, axis=0)
    row_group = lax.broadcasted_iota(jnp.int32, (LANES, LANES), 0) // ORDER
    lane_group = lax.broadcasted_iota(jnp.int32, (LANES, LANES), 1) // GROUP
    return jnp.where(row_group == lane_group, tiled, jnp.zeros_like(tiled))


def dot(a, b):
    return jnp.dot(a, b, preferred_element_type=F32)


def conv_body(rim, own_part, query, taps, ends_coef, *refs):
    conv, mixed, ends = refs[-3:]
    lower = lower_mask()
    for s in range(rim.shape[1] // LANES):
        cols = slice(s * LANES, (s + 1) * LANES)
        blocks = [
            jnp.where(lower, jnp.zeros_like(circ), circ).astype(BF16)
            for circ in circulants(taps, s * PER_SLAB)
        ]
        out = own_part[:, cols] + pick_groups(
            dot(jnp.concatenate(blocks, axis=0), rim[:, cols]), LANES
        )
        conv[:, cols] = out.astype(conv.dtype)
        mixed[:, cols] = (query[:, cols].astype(F32) * out).astype(BF16)
    for s in range(rim.shape[1] // LANES):
        cols = slice(s * LANES, (s + 1) * LANES)
        ends[:, cols] = pick_groups(
            dot(ends_coef[s * LANES : (s + 1) * LANES, :], mixed[:, cols]), ORDER
        ).astype(ends.dtype)


def local_body(transposed, rows, x, *refs):
    out = refs[-1]
    lower = lower_mask()
    keep = ~lower | (lax.broadcasted_iota(jnp.int32, (LANES, LANES), 0)
                     == lax.broadcasted_iota(jnp.int32, (LANES, LANES), 1)) if transposed else lower
    for s in range(x.shape[1] // LANES):
        cols = slice(s * LANES, (s + 1) * LANES)
        blocks = [
            jnp.where(keep, circ, jnp.zeros_like(circ)).astype(BF16)
            for circ in circulants(rows, s * PER_SLAB)
        ]
        out[:, cols] = pick_groups(
            dot(jnp.concatenate(blocks, axis=0), x[:, cols]), LANES
        ).astype(out.dtype)


def carried(states, decay, coef, cols):
    state = sum(ref[:, cols].astype(F32) * decay[k, :, cols] for k, ref in enumerate(states))
    return dot(coef[:, cols], spread_groups(state.astype(BF16)))


def long_body(count, local, decay, coef, gate, *refs):
    states, (long_out, gated) = refs[:count], refs[-2:]
    for s in range(local.shape[1] // LANES):
        cols = slice(s * LANES, (s + 1) * LANES)
        out = local[:, cols].astype(F32) + carried(states, decay, coef, cols)
        long_out[:, cols] = out.astype(long_out.dtype)
        gated[0, :, cols] = (gate[:, cols].astype(F32) * out).astype(BF16)


def seed_body(delta, gate, long_out, starts_coef, seed, starts, gate_grad):
    for s in range(gate.shape[1] // LANES):
        cols = slice(s * LANES, (s + 1) * LANES)
        out = jnp.sum(delta[0, :, :, cols].astype(F32), axis=0)
        seed[:, cols] = (out * gate[:, cols].astype(F32)).astype(BF16)
        gate_grad[:, cols] = (out * long_out[:, cols].astype(F32)).astype(BF16)
    for s in range(gate.shape[1] // LANES):
        cols = slice(s * LANES, (s + 1) * LANES)
        starts[:, cols] = pick_groups(
            dot(starts_coef[s * LANES : (s + 1) * LANES, :], seed[:, cols]), ORDER
        ).astype(starts.dtype)


def back_body(count, local, decay, coef, conv, query, *refs):
    states, (query_grad, conv_grad) = refs[:count], refs[-2:]
    for s in range(local.shape[1] // LANES):
        cols = slice(s * LANES, (s + 1) * LANES)
        out = local[:, cols].astype(F32) + carried(states, decay, coef, cols)
        query_grad[:, cols] = (out * conv[:, cols].astype(F32)).astype(BF16)
        conv_grad[:, cols] = (out * query[:, cols].astype(F32)).astype(BF16)


def pack_body(place, *refs):
    count = len(refs) // 2
    for source, target in zip(refs[:count], refs[count:]):
        target[...] = source[...]


def join_body(*refs):
    out = refs[-1]
    for k in range(out.shape[0]):
        out[k] = refs[k][...]


def delta_body(place, grad, *refs):
    weights, out = refs[:-2], refs[-1]
    depth = weights[0].shape[1]
    total = None
    for k, weight in enumerate(weights):
        start = pl.multiple_of((place[0] ^ k) * depth, depth)
        rows = grad[:, :, :, :, pl.ds(start, depth)].reshape(-1, depth)
        term = lax.dot_general(
            rows, weight[...], (((1,), (1,)), ((), ())), preferred_element_type=F32
        )
        total = term if total is None else total + term
    out[...] = total.astype(out.dtype).reshape(out.shape)


def flip_body(place, grad, after, out):
    out[...] = grad[...].reshape(-1, grad.shape[-1]).T


def lay_body(source, after, target):
    target[...] = source[0]


def weight_body(grad_t, gated, out):
    out[0] = dot(grad_t[...], gated[...]).astype(out.dtype)


def wide(rows, lanes):
    return pl.BlockSpec((rows, lanes), lambda i: (0, i))


def tall(rows, cols):
    return pl.BlockSpec((rows, cols), lambda i: (i, 0))


def deep(count, rows, lanes):
    return pl.BlockSpec((count, rows, lanes), lambda i: (0, 0, i))


def shape(*dims, dtype=BF16):
    return jax.ShapeDtypeStruct(dims, dtype)


def on_device(query, key_in, value_in, gate, out_grad, proj_weight, mr_filter, lr_rate, lr_residue):
    rows, width = query.shape
    groups = width // GROUP
    n_dp, n_ctx, n_tp = (lax.axis_size(a) for a in ("dp", "ctx", "tp"))
    feats = proj_weight.shape[1]
    quarter = width // n_dp
    depth = n_dp * feats
    block = min(1024, quarter)
    steps = width // block
    per = quarter // block

    def split_at(i):
        return (i // per, 0, i % per)

    part = rows // n_tp

    place = jnp.stack([lax.axis_index(a) for a in ("dp", "ctx", "tp")]).astype(jnp.int32)

    def swap(value, axis, k):
        return lax.ppermute(value, axis, [(i, i ^ k) for i in range(lax.axis_size(axis))])

    def shift(value, k):
        ends = [(i, i + k) for i in range(n_ctx) if 0 <= i + k < n_ctx]
        return lax.ppermute(value, "ctx", ends)

    def piece(k):
        return pl.BlockSpec((part, feats), lambda j, p: (p[2], j * n_ctx + (p[1] ^ k)))

    mine = call(
        pack_body, "pack", 0, 4 * part * depth * n_ctx,
        grid_spec=pltpu.PrefetchScalarGridSpec(
            num_scalar_prefetch=1, grid=(n_dp,),
            in_specs=[piece(k) for k in range(n_ctx)],
            out_specs=[pl.BlockSpec((part, feats), lambda j, p: (0, j))] * n_ctx,
        ),
        out_shape=[shape(part, depth)] * n_ctx,
    )(place, *[out_grad] * n_ctx)
    mine = [mine[0]] + [swap(mine[k], "ctx", k) for k in range(1, n_ctx)]
    weights = [proj_weight] + [
        swap(lax.dynamic_slice_in_dim(proj_weight, (place[0] ^ k) * quarter, quarter), "dp", k)
        for k in range(1, n_dp)
    ]
    product = (key_in.astype(F32) * value_in.astype(F32)).astype(BF16)
    rim = shift(product, 1)
    rate = lr_rate.reshape(-1, 1)
    residue = lr_residue.reshape(-1, 1)
    counts = jnp.arange(rows, dtype=F32)[None, :]
    ends_coef = jnp.exp(-rate * (rows - 1 - counts)).astype(BF16)
    starts_coef = jnp.exp(-rate * counts).astype(BF16)
    carry_coef = (residue.T * jnp.exp(-rate.T * (counts.T + 1))).astype(BF16)
    back_coef = (residue.T * jnp.exp(-rate.T * (rows - counts.T))).astype(BF16)
    kernel = jnp.sum(
        lr_residue[:, :, None] * jnp.exp(-lr_rate[:, :, None] * counts[:, None, :]), axis=1
    )

    def reversed_row(values):
        return jnp.roll(values[:, ::-1], 1, axis=1)

    taps = reversed_row(mr_filter.astype(F32))
    kernel_rev = reversed_row(kernel)
    lane_rate = jnp.repeat(lr_rate.T, GROUP, axis=1)[None]
    blocks_away = jnp.arange(n_ctx - 1, dtype=F32)[:, None, None]
    decay = jnp.exp(-lane_rate * (rows * blocks_away))

    def local(transposed, table, x, *after):
        return call(
            functools.partial(local_body, transposed),
            "local_t" if transposed else "local",
            2 * rows * 128 * width * 8, rows * width * 6,
            grid=(steps,),
            in_specs=[tall(block // GROUP, rows), wide(rows, block)] + [ANY] * len(after),
            out_specs=wide(rows, block),
            out_shape=shape(rows, width, dtype=F32),
        )(table, x, *after)

    conv_own = local(
        False, taps, product, ends_coef, starts_coef, carry_coef, back_coef, decay, kernel_rev
    )
    mine = call(
        join_body, "join", 0, 4 * part * depth * n_ctx,
        grid=(n_dp,),
        in_specs=[wide(part, feats)] * n_ctx + [ANY] * n_dp,
        out_specs=deep(n_ctx, part, feats),
        out_shape=shape(n_ctx, part, depth),
    )(*mine, *weights[1:-1], conv_own, rim)
    grad = lax.all_gather(mine, ("dp", "tp"), axis=0, tiled=False)
    grad = grad.reshape(n_dp, n_tp, n_ctx, part, depth)

    late = weights[-1:]
    conv, mixed, ends = call(
        conv_body, "conv", 2 * rows * 128 * width * 8, rows * width * 14,
        grid=(steps,),
        in_specs=[wide(rows, block)] * 3 + [tall(block // GROUP, TAPS), tall(block, rows)],
        out_specs=[wide(rows, block), wide(rows, block), wide(ORDER, block)],
        out_shape=[shape(rows, width), shape(rows, width), shape(ORDER, width)],
    )(rim, conv_own, query, taps, ends_coef)
    ends_far = [shift(ends, k) for k in range(1, n_ctx)]

    local_fwd = local(False, kernel_rev, mixed)
    long_out, gated = call(
        functools.partial(long_body, n_ctx - 1), "long", 2 * rows * 128 * width, rows * width * 10,
        grid=(steps,),
        in_specs=[wide(rows, block), deep(n_ctx - 1, ORDER, block), wide(rows, block),
                  wide(rows, block)] + [wide(ORDER, block)] * (n_ctx - 1) + [ANY] * len(late),
        out_specs=[wide(rows, block), pl.BlockSpec((1, rows, block), split_at)],
        out_shape=[shape(rows, width), shape(n_dp, rows, quarter)],
    )(local_fwd, decay, carry_coef, gate, *ends_far, *late)
    gated_far = lax.all_to_all(gated, "dp", 0, 0, tiled=True)
    gated_all = lax.all_gather(gated_far, "ctx", axis=0)
    tokens = n_ctx * n_dp * rows
    gated_all = gated_all.reshape(tokens, quarter)

    partial = call(
        delta_body, "delta", 2 * tokens * depth * quarter, 2 * tokens * (depth + quarter),
        grid_spec=pltpu.PrefetchScalarGridSpec(
            num_scalar_prefetch=1, grid=(n_ctx,),
            in_specs=[
                pl.BlockSpec((n_dp, n_tp, 1, part, depth), lambda i, p: (0, 0, i, 0, 0)),
                pl.BlockSpec((quarter, feats), lambda i, p: (p[0], 0)),
            ] + [pl.BlockSpec((quarter, feats), lambda i, p: (0, 0))] * (n_dp - 1) + [ANY],
            out_specs=pl.BlockSpec(
                (n_dp, 1, rows, quarter), lambda i, p: (0, p[1] ^ i, 0, 0)
            ),
        ),
        out_shape=shape(n_dp, n_ctx, rows, quarter),
    )(place, grad, *weights, gated_far)
    delta = lax.all_to_all(
        partial.reshape(n_dp * n_ctx, rows, quarter), ("dp", "ctx"), 0, 0, tiled=True
    ).reshape(n_dp, n_ctx, rows, quarter)

    seed, starts, gate_grad = call(
        seed_body, "seed", 2 * rows * 128 * width, rows * width * 10,
        grid=(steps,),
        in_specs=[
            pl.BlockSpec((1, n_ctx, rows, block), lambda i: (i // per, 0, 0, i % per)),
            wide(rows, block), wide(rows, block), tall(block, rows),
        ],
        out_specs=[wide(rows, block), wide(ORDER, block), wide(rows, block)],
        out_shape=[shape(rows, width), shape(ORDER, width), shape(rows, width)],
    )(delta, gate, long_out, starts_coef)
    starts_far = [shift(starts, -k) for k in range(1, n_ctx)]
    local_bwd = local(True, kernel, seed)
    query_grad, conv_grad = call(
        functools.partial(back_body, n_ctx - 1), "back", 2 * rows * 128 * width, rows * width * 12,
        grid=(steps,),
        in_specs=[wide(rows, block), deep(n_ctx - 1, ORDER, block)] + [wide(rows, block)] * 3
        + [wide(ORDER, block)] * (n_ctx - 1),
        out_specs=[wide(rows, block)] * 2,
        out_shape=[shape(rows, width)] * 2,
    )(local_bwd, decay, back_coef, conv, query, *starts_far)

    grad_t = call(
        flip_body, "flip", 0, 4 * tokens * depth,
        grid_spec=pltpu.PrefetchScalarGridSpec(
            num_scalar_prefetch=1, grid=(n_ctx, n_dp),
            in_specs=[
                pl.BlockSpec(
                    (1, n_tp, 1, part, depth), lambda i, j, p: (j, 0, p[1] ^ i, 0, 0)
                ),
                ANY,
            ],
            out_specs=pl.BlockSpec((depth, rows), lambda i, j, p: (0, i * n_dp + j)),
        ),
        out_shape=shape(depth, tokens),
    )(place, grad, partial)
    weight_part = call(
        weight_body, "weight", 2 * tokens * depth * quarter, 2 * tokens * (depth + quarter),
        grid=(n_dp,),
        in_specs=[
            pl.BlockSpec((feats, tokens), lambda i: (i, 0)),
            pl.BlockSpec((tokens, quarter), lambda i: (0, 0)),
        ],
        out_specs=pl.BlockSpec((1, feats, quarter), lambda i: (i, 0, 0)),
        out_shape=shape(n_dp, feats, quarter),
    )(grad_t, gated_all)
    weight_grad = lax.all_to_all(weight_part, "dp", 0, 0, tiled=True)
    weight_grad = call(
        lay_body, "lay", 0, 4 * feats * width,
        grid=(n_dp,),
        in_specs=[pl.BlockSpec((1, feats, quarter), lambda i: (i, 0, 0)), ANY],
        out_specs=pl.BlockSpec((feats, quarter), lambda i: (0, i)),
        out_shape=shape(feats, width),
    )(weight_grad, query_grad)
    return query_grad, conv_grad, gate_grad, weight_grad


def solution(mesh):
    rows = P(("dp", "ctx"), "tp")
    return jax.shard_map(
        on_device,
        mesh=mesh,
        in_specs=(rows, rows, rows, rows, P(("dp", "ctx"), None), P("tp", ("dp", "ctx")),
                  P("tp", None), P("tp", None), P("tp", None)),
        out_specs=(rows, rows, rows, rows),
        check_vma=False,
    )
```

```python
import functools

import jax
import jax.numpy as jnp
from jax import lax
from jax.experimental import pallas as pl
from jax.experimental.pallas import tpu as pltpu
from jax.sharding import PartitionSpec as P

GROUP = 16
TAPS = 128
ORDER = 16
LANES = 128
PER_SLAB = LANES // GROUP
BF16 = jnp.bfloat16
F32 = jnp.float32
VMEM = 50 * 2**20
ANY = pl.BlockSpec(memory_space=pl.ANY)


def call(body, name, flops, nbytes, **kwargs):
    return pl.pallas_call(
        body,
        name=name,
        cost_estimate=pl.CostEstimate(flops=flops, bytes_accessed=nbytes, transcendentals=0),
        compiler_params=pltpu.CompilerParams(vmem_limit_bytes=VMEM),
        **kwargs,
    )


def circulants(rows_ref, base):
    out = []
    for j in range(PER_SLAB):
        row = rows_ref[base + j : base + j + 1, :]
        out.append(
            pltpu.roll(jnp.broadcast_to(row, (LANES, LANES)), 0, 1, stride=1, stride_axis=0)
        )
    return out


def lower_mask():
    t = lax.broadcasted_iota(jnp.int32, (LANES, LANES), 0)
    u = lax.broadcasted_iota(jnp.int32, (LANES, LANES), 1)
    return u <= t


def pick_groups(stacked, rows):
    lane_group = lax.broadcasted_iota(jnp.int32, (rows, LANES), 1) // GROUP
    out = stacked[:rows]
    for j in range(1, PER_SLAB):
        out = jnp.where(lane_group == j, stacked[j * rows : (j + 1) * rows], out)
    return out


def spread_groups(state):
    tiled = jnp.concatenate([state] * PER_SLAB, axis=0)
    row_group = lax.broadcasted_iota(jnp.int32, (LANES, LANES), 0) // ORDER
    lane_group = lax.broadcasted_iota(jnp.int32, (LANES, LANES), 1) // GROUP
    return jnp.where(row_group == lane_group, tiled, jnp.zeros_like(tiled))


def dot(a, b):
    return jnp.dot(a, b, preferred_element_type=F32)


def conv_body(rim, own_part, query, taps, ends_coef, *refs):
    conv, mixed, ends = refs[-3:]
    lower = lower_mask()
    for s in range(rim.shape[1] // LANES):
        cols = slice(s * LANES, (s + 1) * LANES)
        blocks = [
            jnp.where(lower, jnp.zeros_like(circ), circ).astype(BF16)
            for circ in circulants(taps, s * PER_SLAB)
        ]
        out = own_part[:, cols] + pick_groups(
            dot(jnp.concatenate(blocks, axis=0), rim[:, cols]), LANES
        )
        conv[:, cols] = out.astype(conv.dtype)
        mixed[:, cols] = (query[:, cols].astype(F32) * out).astype(BF16)
    for s in range(rim.shape[1] // LANES):
        cols = slice(s * LANES, (s + 1) * LANES)
        ends[:, cols] = pick_groups(
            dot(ends_coef[s * LANES : (s + 1) * LANES, :], mixed[:, cols]), ORDER
        ).astype(ends.dtype)


def local_body(transposed, rows, x, *refs):
    out = refs[-1]
    lower = lower_mask()
    keep = ~lower | (lax.broadcasted_iota(jnp.int32, (LANES, LANES), 0)
                     == lax.broadcasted_iota(jnp.int32, (LANES, LANES), 1)) if transposed else lower
    for s in range(x.shape[1] // LANES):
        cols = slice(s * LANES, (s + 1) * LANES)
        blocks = [
            jnp.where(keep, circ, jnp.zeros_like(circ)).astype(BF16)
            for circ in circulants(rows, s * PER_SLAB)
        ]
        out[:, cols] = pick_groups(
            dot(jnp.concatenate(blocks, axis=0), x[:, cols]), LANES
        ).astype(out.dtype)


def carried(states, decay, coef, cols):
    state = sum(ref[:, cols].astype(F32) * decay[k, :, cols] for k, ref in enumerate(states))
    return dot(coef[:, cols], spread_groups(state.astype(BF16)))


def long_body(count, local, decay, coef, gate, *refs):
    states, (long_out, gated) = refs[:count], refs[-2:]
    for s in range(local.shape[1] // LANES):
        cols = slice(s * LANES, (s + 1) * LANES)
        out = local[:, cols].astype(F32) + carried(states, decay, coef, cols)
        long_out[:, cols] = out.astype(long_out.dtype)
        gated[0, :, cols] = (gate[:, cols].astype(F32) * out).astype(BF16)


def seed_body(delta_a, delta_b, gate, long_out, starts_coef, after, seed, starts, gate_grad):
    per_half = delta_a.shape[-1] // LANES
    for s in range(gate.shape[1] // LANES):
        cols = slice(s * LANES, (s + 1) * LANES)
        delta, at = (delta_a, s) if s < per_half else (delta_b, s - per_half)
        out = jnp.sum(delta[0, :, :, at * LANES : (at + 1) * LANES].astype(F32), axis=0)
        seed[:, cols] = (out * gate[:, cols].astype(F32)).astype(BF16)
        gate_grad[:, cols] = (out * long_out[:, cols].astype(F32)).astype(BF16)
    for s in range(gate.shape[1] // LANES):
        cols = slice(s * LANES, (s + 1) * LANES)
        starts[:, cols] = pick_groups(
            dot(starts_coef[s * LANES : (s + 1) * LANES, :], seed[:, cols]), ORDER
        ).astype(starts.dtype)


def back_body(count, local, decay, coef, conv, query, *refs):
    states, (query_grad, conv_grad) = refs[:count], refs[-2:]
    for s in range(local.shape[1] // LANES):
        cols = slice(s * LANES, (s + 1) * LANES)
        out = local[:, cols].astype(F32) + carried(states, decay, coef, cols)
        query_grad[:, cols] = (out * conv[:, cols].astype(F32)).astype(BF16)
        conv_grad[:, cols] = (out * query[:, cols].astype(F32)).astype(BF16)


def pack_body(place, *refs):
    count = len(refs) // 2
    for source, target in zip(refs[:count], refs[count:]):
        target[...] = source[...]


def join_body(*refs):
    out = refs[-1]
    for k in range(out.shape[0]):
        out[k] = refs[k][...]


def delta_body(place, grad, *refs):
    weights, out = refs[:-2], refs[-1]
    depth = weights[0].shape[1]
    total = None
    for k, weight in enumerate(weights):
        start = pl.multiple_of((place[0] ^ k) * depth, depth)
        rows = grad[:, :, :, :, pl.ds(start, depth)].reshape(-1, depth)
        term = lax.dot_general(
            rows, weight[...], (((1,), (1,)), ((), ())), preferred_element_type=F32
        )
        total = term if total is None else total + term
    out[...] = total.astype(out.dtype).reshape(out.shape)


def flip_body(place, grad, after, out):
    out[...] = grad[...].reshape(-1, grad.shape[-1]).T


def lay_body(source, after, target):
    target[...] = source[0]


def wait_body(*refs):
    pass


def weight_body(grad_t, gated, out):
    out[0] = dot(grad_t[...], gated[...]).astype(out.dtype)


def wide(rows, lanes):
    return pl.BlockSpec((rows, lanes), lambda i: (0, i))


def tall(rows, cols):
    return pl.BlockSpec((rows, cols), lambda i: (i, 0))


def deep(count, rows, lanes):
    return pl.BlockSpec((count, rows, lanes), lambda i: (0, 0, i))


def shape(*dims, dtype=BF16):
    return jax.ShapeDtypeStruct(dims, dtype)


def on_device(query, key_in, value_in, gate, out_grad, proj_weight, mr_filter, lr_rate, lr_residue):
    rows, width = query.shape
    groups = width // GROUP
    n_dp, n_ctx, n_tp = (lax.axis_size(a) for a in ("dp", "ctx", "tp"))
    feats = proj_weight.shape[1]
    quarter = width // n_dp
    depth = n_dp * feats
    block = quarter
    steps = width // block
    part = rows // n_tp

    place = jnp.stack([lax.axis_index(a) for a in ("dp", "ctx", "tp")]).astype(jnp.int32)

    def swap(value, axis, k):
        return lax.ppermute(value, axis, [(i, i ^ k) for i in range(lax.axis_size(axis))])

    def shift(value, k):
        ends = [(i, i + k) for i in range(n_ctx) if 0 <= i + k < n_ctx]
        return lax.ppermute(value, "ctx", ends)

    def piece(k):
        return pl.BlockSpec((part, feats), lambda j, p: (p[2], j * n_ctx + (p[1] ^ k)))

    mine = call(
        pack_body, "pack", 0, 4 * part * depth * n_ctx,
        grid_spec=pltpu.PrefetchScalarGridSpec(
            num_scalar_prefetch=1, grid=(n_dp,),
            in_specs=[piece(k) for k in range(n_ctx)],
            out_specs=[pl.BlockSpec((part, feats), lambda j, p: (0, j))] * n_ctx,
        ),
        out_shape=[shape(part, depth)] * n_ctx,
    )(place, *[out_grad] * n_ctx)
    mine = [mine[0]] + [swap(mine[k], "ctx", k) for k in range(1, n_ctx)]
    weights = [proj_weight] + [
        swap(lax.dynamic_slice_in_dim(proj_weight, (place[0] ^ k) * quarter, quarter), "dp", k)
        for k in range(1, n_dp)
    ]
    product = (key_in.astype(F32) * value_in.astype(F32)).astype(BF16)
    rim = shift(product, 1)
    rate = lr_rate.reshape(-1, 1)
    residue = lr_residue.reshape(-1, 1)
    counts = jnp.arange(rows, dtype=F32)[None, :]
    ends_coef = jnp.exp(-rate * (rows - 1 - counts)).astype(BF16)
    starts_coef = jnp.exp(-rate * counts).astype(BF16)
    carry_coef = (residue.T * jnp.exp(-rate.T * (counts.T + 1))).astype(BF16)
    back_coef = (residue.T * jnp.exp(-rate.T * (rows - counts.T))).astype(BF16)
    kernel = jnp.sum(
        lr_residue[:, :, None] * jnp.exp(-lr_rate[:, :, None] * counts[:, None, :]), axis=1
    )

    def reversed_row(values):
        return jnp.roll(values[:, ::-1], 1, axis=1)

    taps = reversed_row(mr_filter.astype(F32))
    kernel_rev = reversed_row(kernel)
    lane_rate = jnp.repeat(lr_rate.T, GROUP, axis=1)[None]
    blocks_away = jnp.arange(n_ctx - 1, dtype=F32)[:, None, None]
    decay = jnp.exp(-lane_rate * (rows * blocks_away))

    def local(transposed, table, x, *after):
        return call(
            functools.partial(local_body, transposed),
            "local_t" if transposed else "local",
            2 * rows * 128 * width * 8, rows * width * 6,
            grid=(steps,),
            in_specs=[tall(block // GROUP, rows), wide(rows, block)] + [ANY] * len(after),
            out_specs=wide(rows, block),
            out_shape=shape(rows, width, dtype=F32),
        )(table, x, *after)

    conv_own = local(
        False, taps, product, ends_coef, starts_coef, carry_coef, back_coef, decay, kernel_rev
    )
    mine = call(
        join_body, "join", 0, 4 * part * depth * n_ctx,
        grid=(n_dp,),
        in_specs=[wide(part, feats)] * n_ctx + [ANY] * (n_dp + 1),
        out_specs=deep(n_ctx, part, feats),
        out_shape=shape(n_ctx, part, depth),
    )(*mine, *weights[1:], conv_own, rim)
    grad = lax.all_gather(mine, ("dp", "tp"), axis=0, tiled=False)
    grad = grad.reshape(n_dp, n_tp, n_ctx, part, depth)
    conv, mixed, ends = call(
        conv_body, "conv", 2 * rows * 128 * width * 8, rows * width * 14,
        grid=(steps,),
        in_specs=[wide(rows, block)] * 3 + [tall(block // GROUP, TAPS), tall(block, rows), ANY],
        out_specs=[wide(rows, block), wide(rows, block), wide(ORDER, block)],
        out_shape=[shape(rows, width), shape(rows, width), shape(ORDER, width)],
    )(rim, conv_own, query, taps, ends_coef, mine)
    ends_far = [shift(ends, k) for k in range(1, n_ctx)]


    local_fwd = local(False, kernel_rev, mixed)
    long_out, gated = call(
        functools.partial(long_body, n_ctx - 1), "long", 2 * rows * 128 * width, rows * width * 10,
        grid=(steps,),
        in_specs=[wide(rows, block), deep(n_ctx - 1, ORDER, block), wide(rows, block),
                  wide(rows, block)] + [wide(ORDER, block)] * (n_ctx - 1),
        out_specs=[wide(rows, block), pl.BlockSpec((1, rows, block), lambda i: (i, 0, 0))],
        out_shape=[shape(rows, width), shape(n_dp, rows, quarter)],
    )(local_fwd, decay, carry_coef, gate, *ends_far)
    gated_far = lax.all_to_all(gated, "dp", 0, 0, tiled=True)
    tokens = n_ctx * n_dp * rows
    half = quarter // 2
    gated_all = lax.all_gather(gated_far, "ctx", axis=0).reshape(tokens, quarter)

    def project(h):
        return call(
            delta_body, "delta", 2 * tokens * depth * half, 2 * tokens * (depth + half),
            grid_spec=pltpu.PrefetchScalarGridSpec(
                num_scalar_prefetch=1, grid=(n_ctx,),
                in_specs=[
                    pl.BlockSpec((n_dp, n_tp, 1, part, depth), lambda i, p: (0, 0, i, 0, 0)),
                    pl.BlockSpec((half, feats), lambda i, p: (2 * p[0] + h, 0)),
                ] + [pl.BlockSpec((half, feats), lambda i, p: (h, 0))] * (n_dp - 1) + [ANY],
                out_specs=pl.BlockSpec(
                    (n_dp, 1, rows, half), lambda i, p: (0, p[1] ^ i, 0, 0)
                ),
            ),
            out_shape=shape(n_dp, n_ctx, rows, half),
        )(place, grad, *weights, gated_far)

    def scatter(partial):
        moved = lax.all_to_all(
            partial.reshape(n_dp * n_ctx, rows, half), ("dp", "ctx"), 0, 0, tiled=True
        )
        return moved.reshape(n_dp, n_ctx, rows, half)

    partial, partial_b = project(0), project(1)
    grad_t = call(
        flip_body, "flip", 0, 4 * tokens * depth,
        grid_spec=pltpu.PrefetchScalarGridSpec(
            num_scalar_prefetch=1, grid=(n_ctx, n_dp),
            in_specs=[
                pl.BlockSpec(
                    (1, n_tp, 1, part, depth), lambda i, j, p: (j, 0, p[1] ^ i, 0, 0)
                ),
                ANY,
            ],
            out_specs=pl.BlockSpec((depth, rows), lambda i, j, p: (0, i * n_dp + j)),
        ),
        out_shape=shape(depth, tokens),
    )(place, grad, partial)
    partial_b = call(
        wait_body, "wait", 0, 0,
        in_specs=[ANY] * 3, out_specs=ANY,
        out_shape=shape(*partial_b.shape), input_output_aliases={0: 0},
    )(partial_b, gated_all, grad_t)
    delta = scatter(partial), scatter(partial_b)
    weight_part = call(
        weight_body, "weight", 2 * tokens * depth * quarter, 2 * tokens * (depth + quarter),
        grid=(n_dp,),
        in_specs=[
            pl.BlockSpec((feats, tokens), lambda i: (i, 0)),
            pl.BlockSpec((tokens, quarter), lambda i: (0, 0)),
        ],
        out_specs=pl.BlockSpec((1, feats, quarter), lambda i: (i, 0, 0)),
        out_shape=shape(n_dp, feats, quarter),
    )(grad_t, gated_all)

    seed, starts, gate_grad = call(
        seed_body, "seed", 2 * rows * 128 * width, rows * width * 10,
        grid=(steps,),
        in_specs=[
            pl.BlockSpec((1, n_ctx, rows, half), lambda i: (i, 0, 0, 0)),
            pl.BlockSpec((1, n_ctx, rows, half), lambda i: (i, 0, 0, 0)),
            wide(rows, block), wide(rows, block), tall(block, rows), ANY,
        ],
        out_specs=[wide(rows, block), wide(ORDER, block), wide(rows, block)],
        out_shape=[shape(rows, width), shape(ORDER, width), shape(rows, width)],
    )(*delta, gate, long_out, starts_coef, weight_part)
    starts_far = [shift(starts, -k) for k in range(1, n_ctx)]
    local_bwd = local(True, kernel, seed)
    query_grad, conv_grad = call(
        functools.partial(back_body, n_ctx - 1), "back", 2 * rows * 128 * width, rows * width * 12,
        grid=(steps,),
        in_specs=[wide(rows, block), deep(n_ctx - 1, ORDER, block)] + [wide(rows, block)] * 3
        + [wide(ORDER, block)] * (n_ctx - 1),
        out_specs=[wide(rows, block)] * 2,
        out_shape=[shape(rows, width)] * 2,
    )(local_bwd, decay, back_coef, conv, query, *starts_far)

    weight_grad = call(
        lay_body, "lay", 0, 4 * feats * width,
        grid=(n_dp,),
        in_specs=[pl.BlockSpec((1, feats, quarter), lambda i: (i, 0, 0)), ANY],
        out_specs=pl.BlockSpec((feats, quarter), lambda i: (0, i)),
        out_shape=shape(feats, width),
    )(lax.all_to_all(weight_part, "dp", 0, 0, tiled=True), starts)
    return query_grad, conv_grad, gate_grad, weight_grad


def solution(mesh):
    rows = P(("dp", "ctx"), "tp")
    return jax.shard_map(
        on_device,
        mesh=mesh,
        in_specs=(rows, rows, rows, rows, P(("dp", "ctx"), None), P("tp", ("dp", "ctx")),
                  P("tp", None), P("tp", None), P("tp", None)),
        out_specs=(rows, rows, rows, rows),
        check_vma=False,
    )
```

```python
import functools

import jax
import jax.numpy as jnp
from jax import lax
from jax.experimental import pallas as pl
from jax.experimental.pallas import tpu as pltpu
from jax.sharding import PartitionSpec as P

GROUP = 16
TAPS = 128
ORDER = 16
LANES = 128
PER_SLAB = LANES // GROUP
BF16 = jnp.bfloat16
F32 = jnp.float32
VMEM = 50 * 2**20
ANY = pl.BlockSpec(memory_space=pl.ANY)


def call(body, name, flops, nbytes, **kwargs):
    return pl.pallas_call(
        body,
        name=name,
        cost_estimate=pl.CostEstimate(flops=flops, bytes_accessed=nbytes, transcendentals=0),
        compiler_params=pltpu.CompilerParams(vmem_limit_bytes=VMEM),
        **kwargs,
    )


def circulants(rows_ref, base):
    out = []
    for j in range(PER_SLAB):
        row = rows_ref[base + j : base + j + 1, :]
        out.append(
            pltpu.roll(jnp.broadcast_to(row, (LANES, LANES)), 0, 1, stride=1, stride_axis=0)
        )
    return out


def lower_mask():
    t = lax.broadcasted_iota(jnp.int32, (LANES, LANES), 0)
    u = lax.broadcasted_iota(jnp.int32, (LANES, LANES), 1)
    return u <= t


def pick_groups(stacked, rows):
    lane_group = lax.broadcasted_iota(jnp.int32, (rows, LANES), 1) // GROUP
    out = stacked[:rows]
    for j in range(1, PER_SLAB):
        out = jnp.where(lane_group == j, stacked[j * rows : (j + 1) * rows], out)
    return out


def spread_groups(state):
    tiled = jnp.concatenate([state] * PER_SLAB, axis=0)
    row_group = lax.broadcasted_iota(jnp.int32, (LANES, LANES), 0) // ORDER
    lane_group = lax.broadcasted_iota(jnp.int32, (LANES, LANES), 1) // GROUP
    return jnp.where(row_group == lane_group, tiled, jnp.zeros_like(tiled))


def dot(a, b):
    return jnp.dot(a, b, preferred_element_type=F32)


def conv_body(rim, own_part, query, taps, ends_coef, *refs):
    conv, mixed, ends = refs[-3:]
    lower = lower_mask()
    for s in range(rim.shape[1] // LANES):
        cols = slice(s * LANES, (s + 1) * LANES)
        blocks = [
            jnp.where(lower, jnp.zeros_like(circ), circ).astype(BF16)
            for circ in circulants(taps, s * PER_SLAB)
        ]
        out = own_part[:, cols] + pick_groups(
            dot(jnp.concatenate(blocks, axis=0), rim[:, cols]), LANES
        )
        conv[:, cols] = out.astype(conv.dtype)
        mixed[:, cols] = (query[:, cols].astype(F32) * out).astype(BF16)
    for s in range(rim.shape[1] // LANES):
        cols = slice(s * LANES, (s + 1) * LANES)
        ends[:, cols] = pick_groups(
            dot(ends_coef[s * LANES : (s + 1) * LANES, :], mixed[:, cols]), ORDER
        ).astype(ends.dtype)


def local_body(transposed, rows, x, *refs):
    out = refs[-1]
    lower = lower_mask()
    keep = ~lower | (lax.broadcasted_iota(jnp.int32, (LANES, LANES), 0)
                     == lax.broadcasted_iota(jnp.int32, (LANES, LANES), 1)) if transposed else lower
    for s in range(x.shape[1] // LANES):
        cols = slice(s * LANES, (s + 1) * LANES)
        blocks = [
            jnp.where(keep, circ, jnp.zeros_like(circ)).astype(BF16)
            for circ in circulants(rows, s * PER_SLAB)
        ]
        out[:, cols] = pick_groups(
            dot(jnp.concatenate(blocks, axis=0), x[:, cols]), LANES
        ).astype(out.dtype)


def carried(states, decay, coef, cols):
    state = sum(ref[:, cols].astype(F32) * decay[k, :, cols] for k, ref in enumerate(states))
    return dot(coef[:, cols], spread_groups(state.astype(BF16)))


def long_body(count, local, decay, coef, gate, *refs):
    states, (long_out, gated) = refs[:count], refs[-2:]
    for s in range(local.shape[1] // LANES):
        cols = slice(s * LANES, (s + 1) * LANES)
        out = local[:, cols].astype(F32) + carried(states, decay, coef, cols)
        long_out[:, cols] = out.astype(long_out.dtype)
        gated[0, :, cols] = (gate[:, cols].astype(F32) * out).astype(BF16)


def seed_body(delta, gate, long_out, starts_coef, seed, starts, gate_grad):
    for s in range(gate.shape[1] // LANES):
        cols = slice(s * LANES, (s + 1) * LANES)
        out = delta[0, :, cols].astype(F32)
        seed[:, cols] = (out * gate[:, cols].astype(F32)).astype(BF16)
        gate_grad[:, cols] = (out * long_out[:, cols].astype(F32)).astype(BF16)
    for s in range(gate.shape[1] // LANES):
        cols = slice(s * LANES, (s + 1) * LANES)
        starts[:, cols] = pick_groups(
            dot(starts_coef[s * LANES : (s + 1) * LANES, :], seed[:, cols]), ORDER
        ).astype(starts.dtype)


def back_body(count, local, decay, coef, conv, query, *refs):
    states, (query_grad, conv_grad) = refs[:count], refs[-2:]
    for s in range(local.shape[1] // LANES):
        cols = slice(s * LANES, (s + 1) * LANES)
        out = local[:, cols].astype(F32) + carried(states, decay, coef, cols)
        query_grad[:, cols] = (out * conv[:, cols].astype(F32)).astype(BF16)
        conv_grad[:, cols] = (out * query[:, cols].astype(F32)).astype(BF16)


def pack_body(place, *refs):
    count = len(refs) // 2
    for source, target in zip(refs[:count], refs[count:]):
        target[...] = source[...]


def join_body(*refs):
    out = refs[-1]
    for k in range(out.shape[0]):
        out[k] = refs[k][...]


def delta_body(place, dest, grad, *refs):
    weights, out = refs[:-2], refs[-1]
    depth = weights[0].shape[1]
    total = None
    for k, weight in enumerate(weights):
        start = pl.multiple_of((place[0] ^ k) * depth, depth)
        rows = grad[:, :, :, :, pl.ds(start, depth)].reshape(-1, depth)
        term = lax.dot_general(
            rows, weight[...], (((1,), (1,)), ((), ())), preferred_element_type=F32
        )
        total = term if total is None else total + term
    out[...] = total.astype(out.dtype).reshape(out.shape)


def flip_body(place, grad, after, out):
    out[...] = grad[...].reshape(-1, grad.shape[-1]).T


def lay_body(place, source, *refs):
    refs[-1][...] = source[...]


def add_body(dests, partial_right, partial_left, right, left, out_right, out_left):
    out_right[...] = (partial_right[...].astype(F32) + right[...].astype(F32)).astype(BF16)
    out_left[...] = (partial_left[...].astype(F32) + left[...].astype(F32)).astype(BF16)


def sum_body(dest, partial, right, left, out):
    total = partial[0].astype(F32) + right[0].astype(F32) + left[0].astype(F32)
    out[...] = total.astype(BF16)


def weight_body(place, grad_t, gated, after, out):
    out[...] = dot(grad_t[...], gated[...]).astype(out.dtype)


def wide(rows, lanes):
    return pl.BlockSpec((rows, lanes), lambda i: (0, i))


def tall(rows, cols):
    return pl.BlockSpec((rows, cols), lambda i: (i, 0))


def deep(count, rows, lanes):
    return pl.BlockSpec((count, rows, lanes), lambda i: (0, 0, i))


def shape(*dims, dtype=BF16):
    return jax.ShapeDtypeStruct(dims, dtype)


def on_device(query, key_in, value_in, gate, out_grad, proj_weight, mr_filter, lr_rate, lr_residue):
    rows, width = query.shape
    groups = width // GROUP
    n_dp, n_ctx, n_tp = (lax.axis_size(a) for a in ("dp", "ctx", "tp"))
    feats = proj_weight.shape[1]
    quarter = width // n_dp
    depth = n_dp * feats
    block = quarter
    steps = width // block
    part = rows // n_tp

    place = jnp.stack([lax.axis_index(a) for a in ("dp", "ctx", "tp")]).astype(jnp.int32)

    def swap(value, axis, k):
        return lax.ppermute(value, axis, [(i, i ^ k) for i in range(lax.axis_size(axis))])

    def shift(value, k):
        ends = [(i, i + k) for i in range(n_ctx) if 0 <= i + k < n_ctx]
        return lax.ppermute(value, "ctx", ends)

    def piece(k):
        return pl.BlockSpec((part, feats), lambda j, p: (p[2], j * n_ctx + (p[1] ^ k)))

    mine = call(
        pack_body, "pack", 0, 4 * part * depth * n_ctx,
        grid_spec=pltpu.PrefetchScalarGridSpec(
            num_scalar_prefetch=1, grid=(n_dp,),
            in_specs=[piece(k) for k in range(n_ctx)],
            out_specs=[pl.BlockSpec((part, feats), lambda j, p: (0, j))] * n_ctx,
        ),
        out_shape=[shape(part, depth)] * n_ctx,
    )(place, *[out_grad] * n_ctx)
    mine = [mine[0]] + [swap(mine[k], "ctx", k) for k in range(1, n_ctx)]
    weights = [proj_weight] + [
        swap(lax.dynamic_slice_in_dim(proj_weight, (place[0] ^ k) * quarter, quarter), "dp", k)
        for k in range(1, n_dp)
    ]
    product = (key_in.astype(F32) * value_in.astype(F32)).astype(BF16)
    rim = shift(product, 1)
    rate = lr_rate.reshape(-1, 1)
    residue = lr_residue.reshape(-1, 1)
    counts = jnp.arange(rows, dtype=F32)[None, :]
    ends_coef = jnp.exp(-rate * (rows - 1 - counts)).astype(BF16)
    starts_coef = jnp.exp(-rate * counts).astype(BF16)
    carry_coef = (residue.T * jnp.exp(-rate.T * (counts.T + 1))).astype(BF16)
    back_coef = (residue.T * jnp.exp(-rate.T * (rows - counts.T))).astype(BF16)
    kernel = jnp.sum(
        lr_residue[:, :, None] * jnp.exp(-lr_rate[:, :, None] * counts[:, None, :]), axis=1
    )

    def reversed_row(values):
        return jnp.roll(values[:, ::-1], 1, axis=1)

    taps = reversed_row(mr_filter.astype(F32))
    kernel_rev = reversed_row(kernel)
    lane_rate = jnp.repeat(lr_rate.T, GROUP, axis=1)[None]
    blocks_away = jnp.arange(n_ctx - 1, dtype=F32)[:, None, None]
    decay = jnp.exp(-lane_rate * (rows * blocks_away))

    def local(transposed, table, x, *after):
        return call(
            functools.partial(local_body, transposed),
            "local_t" if transposed else "local",
            2 * rows * 128 * width * 8, rows * width * 6,
            grid=(steps,),
            in_specs=[tall(block // GROUP, rows), wide(rows, block)] + [ANY] * len(after),
            out_specs=wide(rows, block),
            out_shape=shape(rows, width, dtype=F32),
        )(table, x, *after)

    conv_own = local(
        False, taps, product, ends_coef, starts_coef, carry_coef, back_coef, decay, kernel_rev
    )
    mine = call(
        join_body, "join", 0, 4 * part * depth * n_ctx,
        grid=(n_dp,),
        in_specs=[wide(part, feats)] * n_ctx + [ANY] * (n_dp - 1),
        out_specs=deep(n_ctx, part, feats),
        out_shape=shape(n_ctx, part, depth),
    )(*mine, *weights[1:-1], conv_own)
    grad = lax.all_gather(mine, ("dp", "tp"), axis=0, tiled=False)
    grad = grad.reshape(n_dp, n_tp, n_ctx, part, depth)
    conv, mixed, ends = call(
        conv_body, "conv", 2 * rows * 128 * width * 8, rows * width * 14,
        grid=(steps,),
        in_specs=[wide(rows, block)] * 3 + [tall(block // GROUP, TAPS), tall(block, rows)],
        out_specs=[wide(rows, block), wide(rows, block), wide(ORDER, block)],
        out_shape=[shape(rows, width), shape(rows, width), shape(ORDER, width)],
    )(rim, conv_own, query, taps, ends_coef)
    ends_far = [shift(ends, k) for k in range(1, n_ctx)]


    local_fwd = local(False, kernel_rev, mixed)
    long_out, gated = call(
        functools.partial(long_body, n_ctx - 1), "long", 2 * rows * 128 * width, rows * width * 10,
        grid=(steps,),
        in_specs=[wide(rows, block), deep(n_ctx - 1, ORDER, block), wide(rows, block),
                  wide(rows, block)] + [wide(ORDER, block)] * (n_ctx - 1) + [ANY],
        out_specs=[wide(rows, block), pl.BlockSpec((1, rows, block), lambda i: (i, 0, 0))],
        out_shape=[shape(rows, width), shape(n_dp, rows, quarter)],
    )(local_fwd, decay, carry_coef, gate, *ends_far, weights[-1])
    gated_far = lax.all_to_all(gated, "dp", 0, 0, tiled=True)
    tokens = n_ctx * n_dp * rows
    gated_all = lax.all_gather(gated_far, "ctx", axis=0).reshape(tokens, quarter)

    last = n_ctx - 1
    first_dest = jnp.where(place[1] < n_ctx // 2, last, 0)
    chunk = (1, n_dp, rows, quarter)

    def project(count, dest, after):
        return call(
            delta_body, "delta", 2 * count * n_dp * rows * depth * quarter,
            2 * tokens * depth + 2 * depth * quarter + 2 * count * n_dp * rows * quarter,
            grid_spec=pltpu.PrefetchScalarGridSpec(
                num_scalar_prefetch=2, grid=(count,),
                in_specs=[
                    pl.BlockSpec(
                        (n_dp, n_tp, 1, part, depth), lambda i, p, q: (0, 0, p[1] ^ q[i], 0, 0)
                    ),
                    pl.BlockSpec((quarter, feats), lambda i, p, q: (p[0], 0)),
                ] + [pl.BlockSpec((quarter, feats), lambda i, p, q: (0, 0))] * (n_dp - 1) + [ANY],
                out_specs=pl.BlockSpec(chunk, lambda i, p, q: (i, 0, 0, 0)),
            ),
            out_shape=shape(count, n_dp, rows, quarter),
        )(place, dest, grad, *weights, after)

    first = project(1, first_dest[None], gated_far)
    partial = project(n_ctx, jnp.arange(n_ctx, dtype=jnp.int32), first)
    right, left = shift(first, 1), shift(first, -1)

    def pick(ahead):
        return pl.BlockSpec(
            (1, 1, rows, quarter), lambda i, q: (q[ahead], i, 0, 0)
        )

    piece_of = pl.BlockSpec((1, 1, rows, quarter), lambda i, q: (0, i, 0, 0))
    for t in range(1, last):
        dests = jnp.clip(jnp.stack([last - t + place[1], t - last + place[1]]), 0, last)
        right, left = call(
            add_body, "add", 0, 12 * n_dp * rows * quarter,
            grid_spec=pltpu.PrefetchScalarGridSpec(
                num_scalar_prefetch=1, grid=(n_dp,),
                in_specs=[pick(0), pick(1), piece_of, piece_of],
                out_specs=[piece_of] * 2,
            ),
            out_shape=[shape(*chunk)] * 2,
        )(dests, partial, partial, right, left)
        right, left = shift(right, 1), shift(left, -1)
    delta = call(
        sum_body, "sum", 0, 8 * n_dp * rows * quarter,
        grid_spec=pltpu.PrefetchScalarGridSpec(
            num_scalar_prefetch=1, grid=(n_dp,),
            in_specs=[pick(0), piece_of, piece_of],
            out_specs=pl.BlockSpec((1, rows, quarter), lambda i, q: (i, 0, 0)),
        ),
        out_shape=shape(n_dp, rows, quarter),
    )(place[1:2], partial, right, left)
    delta_far = lax.all_to_all(delta, "dp", 0, 0, tiled=True)

    grad_t = call(
        flip_body, "flip", 0, 4 * tokens * depth,
        grid_spec=pltpu.PrefetchScalarGridSpec(
            num_scalar_prefetch=1, grid=(n_ctx, n_dp),
            in_specs=[
                pl.BlockSpec(
                    (1, n_tp, 1, part, depth), lambda i, j, p: (j, 0, p[1] ^ i, 0, 0)
                ),
                ANY,
            ],
            out_specs=pl.BlockSpec((depth, rows), lambda i, j, p: (0, i * n_dp + j)),
        ),
        out_shape=shape(depth, tokens),
    )(place, grad, partial)
    weight_far, token = [], delta
    for k in list(range(1, n_dp)) + [0]:
        token = call(
            weight_body, "weight", 2 * tokens * feats * quarter, 2 * tokens * (feats + quarter),
            grid_spec=pltpu.PrefetchScalarGridSpec(
                num_scalar_prefetch=1, grid=(2,),
                in_specs=[
                    pl.BlockSpec((feats, tokens), lambda i, p, k=k: (p[0] ^ k, 0)),
                    pl.BlockSpec((tokens, quarter // 2), lambda i, p: (0, i)),
                    ANY,
                ],
                out_specs=pl.BlockSpec((feats, quarter // 2), lambda i, p: (0, i)),
            ),
            out_shape=shape(feats, quarter),
        )(place, grad_t, gated_all, token)
        weight_far.append((k, swap(token, "dp", k) if k else token))

    seed, starts, gate_grad = call(
        seed_body, "seed", 2 * rows * 128 * width, rows * width * 10,
        grid=(steps,),
        in_specs=[
            pl.BlockSpec((1, rows, block), lambda i: (i, 0, 0)),
            wide(rows, block), wide(rows, block), tall(block, rows),
        ],
        out_specs=[wide(rows, block), wide(ORDER, block), wide(rows, block)],
        out_shape=[shape(rows, width), shape(ORDER, width), shape(rows, width)],
    )(delta_far, gate, long_out, starts_coef)
    starts_far = [shift(starts, -k) for k in range(1, n_ctx)]
    local_bwd = local(True, kernel, seed)
    query_grad, conv_grad = call(
        functools.partial(back_body, n_ctx - 1), "back", 2 * rows * 128 * width, rows * width * 12,
        grid=(steps,),
        in_specs=[wide(rows, block), deep(n_ctx - 1, ORDER, block)] + [wide(rows, block)] * 3
        + [wide(ORDER, block)] * (n_ctx - 1),
        out_specs=[wide(rows, block)] * 2,
        out_shape=[shape(rows, width)] * 2,
    )(local_bwd, decay, back_coef, conv, query, *starts_far)

    weight_grad = None
    for k, source in weight_far[-1:] + weight_far[:-1]:
        before = [] if weight_grad is None else [weight_grad]
        weight_grad = call(
            lay_body, "lay", 0, 4 * feats * quarter,
            grid_spec=pltpu.PrefetchScalarGridSpec(
                num_scalar_prefetch=1, grid=(1,),
                in_specs=[pl.BlockSpec((feats, quarter), lambda i, p: (0, 0)), ANY]
                + [ANY] * len(before),
                out_specs=pl.BlockSpec((feats, quarter), lambda i, p, k=k: (0, p[0] ^ k)),
            ),
            out_shape=shape(feats, width),
            input_output_aliases={3: 0} if before else {},
        )(place, source, starts, *before)
    return query_grad, conv_grad, gate_grad, weight_grad


def solution(mesh):
    rows = P(("dp", "ctx"), "tp")
    return jax.shard_map(
        on_device,
        mesh=mesh,
        in_specs=(rows, rows, rows, rows, P(("dp", "ctx"), None), P("tp", ("dp", "ctx")),
                  P("tp", None), P("tp", None), P("tp", None)),
        out_specs=(rows, rows, rows, rows),
        check_vma=False,
    )
```

```python
import functools

import jax
import jax.numpy as jnp
from jax import lax
from jax.experimental import pallas as pl
from jax.experimental.pallas import tpu as pltpu
from jax.sharding import PartitionSpec as P

GROUP = 16
TAPS = 128
ORDER = 16
LANES = 128
PER_SLAB = LANES // GROUP
BF16 = jnp.bfloat16
F32 = jnp.float32
VMEM = 50 * 2**20
ANY = pl.BlockSpec(memory_space=pl.ANY)


def call(body, name, flops, nbytes, **kwargs):
    return pl.pallas_call(
        body,
        name=name,
        cost_estimate=pl.CostEstimate(flops=flops, bytes_accessed=nbytes, transcendentals=0),
        compiler_params=pltpu.CompilerParams(vmem_limit_bytes=VMEM),
        **kwargs,
    )


def circulants(rows_ref, base):
    out = []
    for j in range(PER_SLAB):
        row = rows_ref[base + j : base + j + 1, :]
        out.append(
            pltpu.roll(jnp.broadcast_to(row, (LANES, LANES)), 0, 1, stride=1, stride_axis=0)
        )
    return out


def lower_mask():
    t = lax.broadcasted_iota(jnp.int32, (LANES, LANES), 0)
    u = lax.broadcasted_iota(jnp.int32, (LANES, LANES), 1)
    return u <= t


def pick_groups(stacked, rows):
    lane_group = lax.broadcasted_iota(jnp.int32, (rows, LANES), 1) // GROUP
    out = stacked[:rows]
    for j in range(1, PER_SLAB):
        out = jnp.where(lane_group == j, stacked[j * rows : (j + 1) * rows], out)
    return out


def spread_groups(state):
    tiled = jnp.concatenate([state] * PER_SLAB, axis=0)
    row_group = lax.broadcasted_iota(jnp.int32, (LANES, LANES), 0) // ORDER
    lane_group = lax.broadcasted_iota(jnp.int32, (LANES, LANES), 1) // GROUP
    return jnp.where(row_group == lane_group, tiled, jnp.zeros_like(tiled))


def dot(a, b):
    return jnp.dot(a, b, preferred_element_type=F32)


def conv_body(rim, own_part, query, taps, ends_coef, *refs):
    conv, mixed, ends = refs[-3:]
    lower = lower_mask()
    for s in range(rim.shape[1] // LANES):
        cols = slice(s * LANES, (s + 1) * LANES)
        blocks = [
            jnp.where(lower, jnp.zeros_like(circ), circ).astype(BF16)
            for circ in circulants(taps, s * PER_SLAB)
        ]
        out = own_part[:, cols] + pick_groups(
            dot(jnp.concatenate(blocks, axis=0), rim[:, cols]), LANES
        )
        conv[:, cols] = out.astype(conv.dtype)
        mixed[:, cols] = (query[:, cols].astype(F32) * out).astype(BF16)
    for s in range(rim.shape[1] // LANES):
        cols = slice(s * LANES, (s + 1) * LANES)
        ends[:, cols] = pick_groups(
            dot(ends_coef[s * LANES : (s + 1) * LANES, :], mixed[:, cols]), ORDER
        ).astype(ends.dtype)


def local_body(transposed, rows, x, *refs):
    out = refs[-1]
    lower = lower_mask()
    keep = ~lower | (lax.broadcasted_iota(jnp.int32, (LANES, LANES), 0)
                     == lax.broadcasted_iota(jnp.int32, (LANES, LANES), 1)) if transposed else lower
    for s in range(x.shape[1] // LANES):
        cols = slice(s * LANES, (s + 1) * LANES)
        blocks = [
            jnp.where(keep, circ, jnp.zeros_like(circ)).astype(BF16)
            for circ in circulants(rows, s * PER_SLAB)
        ]
        out[:, cols] = pick_groups(
            dot(jnp.concatenate(blocks, axis=0), x[:, cols]), LANES
        ).astype(out.dtype)


def carried(states, coef, cols):
    wide_states = jnp.concatenate([spread_groups(ref[:, cols]) for ref in states], axis=0)
    count = len(states)
    rows = coef.shape[0] // count
    parts = [coef[k * rows : (k + 1) * rows, cols] for k in range(count)]
    return dot(jnp.concatenate(parts, axis=1), wide_states)


def long_body(count, local, coef, gate, *refs):
    states, (long_out, gated) = refs[:count], refs[-2:]
    for s in range(local.shape[1] // LANES):
        cols = slice(s * LANES, (s + 1) * LANES)
        out = local[:, cols].astype(F32) + carried(states, coef, cols)
        long_out[:, cols] = out.astype(long_out.dtype)
        gated[0, :, cols] = (gate[:, cols].astype(F32) * out).astype(BF16)


def seed_body(delta, gate, long_out, starts_coef, seed, starts, gate_grad):
    for s in range(gate.shape[1] // LANES):
        cols = slice(s * LANES, (s + 1) * LANES)
        out = delta[0, :, cols].astype(F32)
        seed[:, cols] = (out * gate[:, cols].astype(F32)).astype(BF16)
        gate_grad[:, cols] = (out * long_out[:, cols].astype(F32)).astype(BF16)
    for s in range(gate.shape[1] // LANES):
        cols = slice(s * LANES, (s + 1) * LANES)
        starts[:, cols] = pick_groups(
            dot(starts_coef[s * LANES : (s + 1) * LANES, :], seed[:, cols]), ORDER
        ).astype(starts.dtype)


def back_body(count, local, coef, conv, query, *refs):
    states, (query_grad, conv_grad) = refs[:count], refs[-2:]
    for s in range(local.shape[1] // LANES):
        cols = slice(s * LANES, (s + 1) * LANES)
        out = local[:, cols].astype(F32) + carried(states, coef, cols)
        query_grad[:, cols] = (out * conv[:, cols].astype(F32)).astype(BF16)
        conv_grad[:, cols] = (out * query[:, cols].astype(F32)).astype(BF16)


def pack_body(place, *refs):
    count = len(refs) // 2
    for source, target in zip(refs[:count], refs[count:]):
        target[...] = source[...]


def join_body(*refs):
    out = refs[-1]
    for k in range(out.shape[0]):
        out[k] = refs[k][...]


def delta_body(place, dest, grad, *refs):
    weights, out = refs[:-2], refs[-1]
    depth = weights[0].shape[1]
    total = None
    for k, weight in enumerate(weights):
        start = pl.multiple_of((place[0] ^ k) * depth, depth)
        rows = grad[:, :, :, :, pl.ds(start, depth)].reshape(-1, depth)
        term = lax.dot_general(
            rows, weight[...], (((1,), (1,)), ((), ())), preferred_element_type=F32
        )
        total = term if total is None else total + term
    out[...] = total.astype(out.dtype).reshape(out.shape)


def flip_body(place, grad, after, out):
    out[...] = grad[...].reshape(-1, grad.shape[-1]).T


def lay_body(place, source, *refs):
    refs[-1][...] = source[...]


def add_body(dests, partial_right, partial_left, right, left, out_right, out_left):
    out_right[...] = (partial_right[...].astype(F32) + right[...].astype(F32)).astype(BF16)
    out_left[...] = (partial_left[...].astype(F32) + left[...].astype(F32)).astype(BF16)


def sum_body(dest, partial, right, left, out):
    total = partial[0].astype(F32) + right[0].astype(F32) + left[0].astype(F32)
    out[...] = total.astype(BF16)


def weight_body(place, grad_t, gated, after, out):
    out[...] = dot(grad_t[...], gated[...]).astype(out.dtype)


def wide(rows, lanes):
    return pl.BlockSpec((rows, lanes), lambda i: (0, i))


def tall(rows, cols):
    return pl.BlockSpec((rows, cols), lambda i: (i, 0))


def deep(count, rows, lanes):
    return pl.BlockSpec((count, rows, lanes), lambda i: (0, 0, i))


def shape(*dims, dtype=BF16):
    return jax.ShapeDtypeStruct(dims, dtype)


def on_device(query, key_in, value_in, gate, out_grad, proj_weight, mr_filter, lr_rate, lr_residue):
    rows, width = query.shape
    groups = width // GROUP
    n_dp, n_ctx, n_tp = (lax.axis_size(a) for a in ("dp", "ctx", "tp"))
    feats = proj_weight.shape[1]
    quarter = width // n_dp
    depth = n_dp * feats
    block = quarter
    steps = width // block
    part = rows // n_tp

    place = jnp.stack([lax.axis_index(a) for a in ("dp", "ctx", "tp")]).astype(jnp.int32)

    def swap(value, axis, k):
        return lax.ppermute(value, axis, [(i, i ^ k) for i in range(lax.axis_size(axis))])

    def shift(value, k, senders=None):
        ends = [(i, i + k) for i in senders or range(n_ctx) if 0 <= i + k < n_ctx]
        return lax.ppermute(value, "ctx", ends)

    def piece(k):
        return pl.BlockSpec((part, feats), lambda j, p: (p[2], j * n_ctx + (p[1] ^ k)))

    mine = call(
        pack_body, "pack", 0, 4 * part * depth * n_ctx,
        grid_spec=pltpu.PrefetchScalarGridSpec(
            num_scalar_prefetch=1, grid=(n_dp,),
            in_specs=[piece(k) for k in range(n_ctx)],
            out_specs=[pl.BlockSpec((part, feats), lambda j, p: (0, j))] * n_ctx,
        ),
        out_shape=[shape(part, depth)] * n_ctx,
    )(place, *[out_grad] * n_ctx)
    mine = [mine[0]] + [swap(mine[k], "ctx", k) for k in range(1, n_ctx)]
    weights = [proj_weight] + [
        swap(lax.dynamic_slice_in_dim(proj_weight, (place[0] ^ k) * quarter, quarter), "dp", k)
        for k in range(1, n_dp)
    ]
    product = (key_in.astype(F32) * value_in.astype(F32)).astype(BF16)
    rim = shift(product, 1)
    rate = lr_rate.reshape(-1, 1)
    residue = lr_residue.reshape(-1, 1)
    counts = jnp.arange(rows, dtype=F32)[None, :]
    ends_coef = jnp.exp(-rate * (rows - 1 - counts)).astype(BF16)
    starts_coef = jnp.exp(-rate * counts).astype(BF16)
    away = jnp.arange((n_ctx - 1) * rows, dtype=F32)[:, None]
    inside = away % rows
    carry_coef = (residue.T * jnp.exp(-rate.T * (away + 1))).astype(BF16)
    back_coef = (residue.T * jnp.exp(-rate.T * (away + rows - 2 * inside))).astype(BF16)
    kernel = jnp.sum(
        lr_residue[:, :, None] * jnp.exp(-lr_rate[:, :, None] * counts[:, None, :]), axis=1
    )

    def reversed_row(values):
        return jnp.roll(values[:, ::-1], 1, axis=1)

    taps = reversed_row(mr_filter.astype(F32))
    kernel_rev = reversed_row(kernel)
    def local(transposed, table, x, *after):
        return call(
            functools.partial(local_body, transposed),
            "local_t" if transposed else "local",
            2 * rows * 128 * width * 8, rows * width * 6,
            grid=(steps,),
            in_specs=[tall(block // GROUP, rows), wide(rows, block)] + [ANY] * len(after),
            out_specs=wide(rows, block),
            out_shape=shape(rows, width, dtype=F32),
        )(table, x, *after)

    conv_own = local(False, taps, product)
    mine = call(
        join_body, "join", 0, 4 * part * depth * n_ctx,
        grid=(n_dp,),
        in_specs=[wide(part, feats)] * n_ctx + [ANY] * (n_dp - 2),
        out_specs=deep(n_ctx, part, feats),
        out_shape=shape(n_ctx, part, depth),
    )(*mine, *weights[1:-1])
    grad = lax.all_gather(mine, ("dp", "tp"), axis=0, tiled=False)
    grad = grad.reshape(n_dp, n_tp, n_ctx, part, depth)
    conv, mixed, ends = call(
        conv_body, "conv", 2 * rows * 128 * width * 8, rows * width * 14,
        grid=(steps,),
        in_specs=[wide(rows, block)] * 3 + [tall(block // GROUP, TAPS), tall(block, rows)],
        out_specs=[wide(rows, block), wide(rows, block), wide(ORDER, block)],
        out_shape=[shape(rows, width), shape(rows, width), shape(ORDER, width)],
    )(rim, conv_own, query, taps, ends_coef)
    ends_far = [shift(ends, k) for k in range(1, n_ctx)]


    local_fwd = local(False, kernel_rev, mixed)
    long_out, gated = call(
        functools.partial(long_body, n_ctx - 1), "long", 2 * rows * 128 * width, rows * width * 10,
        grid=(steps,),
        in_specs=[wide(rows, block), wide((n_ctx - 1) * rows, block), wide(rows, block)] + [wide(ORDER, block)] * (n_ctx - 1) + [ANY],
        out_specs=[wide(rows, block), pl.BlockSpec((1, rows, block), lambda i: (i, 0, 0))],
        out_shape=[shape(rows, width), shape(n_dp, rows, quarter)],
    )(local_fwd, carry_coef, gate, *ends_far, weights[-1])
    gated_far = lax.all_to_all(gated, "dp", 0, 0, tiled=True)
    tokens = n_ctx * n_dp * rows
    gated_all = lax.all_gather(gated_far, "ctx", axis=0).reshape(tokens, quarter)

    last = n_ctx - 1
    first_dest = jnp.where(place[1] < n_ctx // 2, last, 0)
    chunk = (1, n_dp, rows, quarter)

    def project(count, dest, after):
        return call(
            delta_body, "delta", 2 * count * n_dp * rows * depth * quarter,
            2 * tokens * depth + 2 * depth * quarter + 2 * count * n_dp * rows * quarter,
            grid_spec=pltpu.PrefetchScalarGridSpec(
                num_scalar_prefetch=2, grid=(count,),
                in_specs=[
                    pl.BlockSpec(
                        (n_dp, n_tp, 1, part, depth), lambda i, p, q: (0, 0, p[1] ^ q[i], 0, 0)
                    ),
                    pl.BlockSpec((quarter, feats), lambda i, p, q: (p[0], 0)),
                ] + [pl.BlockSpec((quarter, feats), lambda i, p, q: (0, 0))] * (n_dp - 1) + [ANY],
                out_specs=pl.BlockSpec(chunk, lambda i, p, q: (i, 0, 0, 0)),
            ),
            out_shape=shape(count, n_dp, rows, quarter),
        )(place, dest, grad, *weights, after)

    first = project(1, first_dest[None], gated_far)
    partial = project(n_ctx, jnp.arange(n_ctx, dtype=jnp.int32), first)
    right, left = shift(first, 1, [0]), shift(first, -1, [last])

    def pick(ahead):
        return pl.BlockSpec(
            (1, 1, rows, quarter), lambda i, q: (q[ahead], i, 0, 0)
        )

    piece_of = pl.BlockSpec((1, 1, rows, quarter), lambda i, q: (0, i, 0, 0))
    for t in range(1, last):
        dests = jnp.clip(jnp.stack([last - t + place[1], t - last + place[1]]), 0, last)
        right, left = call(
            add_body, "add", 0, 12 * n_dp * rows * quarter,
            grid_spec=pltpu.PrefetchScalarGridSpec(
                num_scalar_prefetch=1, grid=(n_dp,),
                in_specs=[pick(0), pick(1), piece_of, piece_of],
                out_specs=[piece_of] * 2,
            ),
            out_shape=[shape(*chunk)] * 2,
        )(dests, partial, partial, right, left)
        right = shift(right, 1, range(t + 1))
        left = shift(left, -1, range(last - t, n_ctx))
    delta = call(
        sum_body, "sum", 0, 8 * n_dp * rows * quarter,
        grid_spec=pltpu.PrefetchScalarGridSpec(
            num_scalar_prefetch=1, grid=(n_dp,),
            in_specs=[pick(0), piece_of, piece_of],
            out_specs=pl.BlockSpec((1, rows, quarter), lambda i, q: (i, 0, 0)),
        ),
        out_shape=shape(n_dp, rows, quarter),
    )(place[1:2], partial, right, left)
    delta_far = lax.all_to_all(delta, "dp", 0, 0, tiled=True)

    grad_t = call(
        flip_body, "flip", 0, 4 * tokens * depth,
        grid_spec=pltpu.PrefetchScalarGridSpec(
            num_scalar_prefetch=1, grid=(n_ctx, n_dp),
            in_specs=[
                pl.BlockSpec(
                    (1, n_tp, 1, part, depth), lambda i, j, p: (j, 0, p[1] ^ i, 0, 0)
                ),
                ANY,
            ],
            out_specs=pl.BlockSpec((depth, rows), lambda i, j, p: (0, i * n_dp + j)),
        ),
        out_shape=shape(depth, tokens),
    )(place, grad, partial)
    weight_far, token = [], delta
    for k in list(range(1, n_dp)) + [0]:
        token = call(
            weight_body, "weight", 2 * tokens * feats * quarter, 2 * tokens * (feats + quarter),
            grid_spec=pltpu.PrefetchScalarGridSpec(
                num_scalar_prefetch=1, grid=(2,),
                in_specs=[
                    pl.BlockSpec((feats, tokens), lambda i, p, k=k: (p[0] ^ k, 0)),
                    pl.BlockSpec((tokens, quarter // 2), lambda i, p: (0, i)),
                    ANY,
                ],
                out_specs=pl.BlockSpec((feats, quarter // 2), lambda i, p: (0, i)),
            ),
            out_shape=shape(feats, quarter),
        )(place, grad_t, gated_all, token)
        weight_far.append((k, swap(token, "dp", k) if k else token))

    seed, starts, gate_grad = call(
        seed_body, "seed", 2 * rows * 128 * width, rows * width * 10,
        grid=(steps,),
        in_specs=[
            pl.BlockSpec((1, rows, block), lambda i: (i, 0, 0)),
            wide(rows, block), wide(rows, block), tall(block, rows),
        ],
        out_specs=[wide(rows, block), wide(ORDER, block), wide(rows, block)],
        out_shape=[shape(rows, width), shape(ORDER, width), shape(rows, width)],
    )(delta_far, gate, long_out, starts_coef)
    starts_far = [shift(starts, -k) for k in range(1, n_ctx)]
    local_bwd = local(True, kernel, seed)
    query_grad, conv_grad = call(
        functools.partial(back_body, n_ctx - 1), "back", 2 * rows * 128 * width, rows * width * 12,
        grid=(steps,),
        in_specs=[wide(rows, block), wide((n_ctx - 1) * rows, block)] + [wide(rows, block)] * 2
        + [wide(ORDER, block)] * (n_ctx - 1),
        out_specs=[wide(rows, block)] * 2,
        out_shape=[shape(rows, width)] * 2,
    )(local_bwd, back_coef, conv, query, *starts_far)

    weight_grad = None
    for k, source in weight_far[-1:] + weight_far[:-1]:
        before = [] if weight_grad is None else [weight_grad]
        weight_grad = call(
            lay_body, "lay", 0, 4 * feats * quarter,
            grid_spec=pltpu.PrefetchScalarGridSpec(
                num_scalar_prefetch=1, grid=(1,),
                in_specs=[pl.BlockSpec((feats, quarter), lambda i, p: (0, 0)), ANY]
                + [ANY] * len(before),
                out_specs=pl.BlockSpec((feats, quarter), lambda i, p, k=k: (0, p[0] ^ k)),
            ),
            out_shape=shape(feats, width),
            input_output_aliases={3: 0} if before else {},
        )(place, source, starts, *before)
    return query_grad, conv_grad, gate_grad, weight_grad


def solution(mesh):
    rows = P(("dp", "ctx"), "tp")
    return jax.shard_map(
        on_device,
        mesh=mesh,
        in_specs=(rows, rows, rows, rows, P(("dp", "ctx"), None), P("tp", ("dp", "ctx")),
                  P("tp", None), P("tp", None), P("tp", None)),
        out_specs=(rows, rows, rows, rows),
        check_vma=False,
    )
```

```python
import functools

import jax
import jax.numpy as jnp
from jax import lax
from jax.experimental import pallas as pl
from jax.experimental.pallas import tpu as pltpu
from jax.sharding import PartitionSpec as P

GROUP = 16
TAPS = 128
ORDER = 16
LANES = 128
PER_SLAB = LANES // GROUP
BF16 = jnp.bfloat16
F32 = jnp.float32
VMEM = 50 * 2**20
ANY = pl.BlockSpec(memory_space=pl.ANY)


def call(body, name, flops, nbytes, **kwargs):
    return pl.pallas_call(
        body,
        name=name,
        cost_estimate=pl.CostEstimate(flops=flops, bytes_accessed=nbytes, transcendentals=0),
        compiler_params=pltpu.CompilerParams(vmem_limit_bytes=VMEM),
        **kwargs,
    )


def circulants(rows_ref, base):
    out = []
    for j in range(PER_SLAB):
        row = rows_ref[base + j : base + j + 1, :]
        out.append(
            pltpu.roll(jnp.broadcast_to(row, (LANES, LANES)), 0, 1, stride=1, stride_axis=0)
        )
    return out


def lower_mask():
    t = lax.broadcasted_iota(jnp.int32, (LANES, LANES), 0)
    u = lax.broadcasted_iota(jnp.int32, (LANES, LANES), 1)
    return u <= t


def pick_groups(stacked, rows):
    lane_group = lax.broadcasted_iota(jnp.int32, (rows, LANES), 1) // GROUP
    out = stacked[:rows]
    for j in range(1, PER_SLAB):
        out = jnp.where(lane_group == j, stacked[j * rows : (j + 1) * rows], out)
    return out


def spread_groups(state):
    tiled = jnp.concatenate([state] * PER_SLAB, axis=0)
    row_group = lax.broadcasted_iota(jnp.int32, (LANES, LANES), 0) // ORDER
    lane_group = lax.broadcasted_iota(jnp.int32, (LANES, LANES), 1) // GROUP
    return jnp.where(row_group == lane_group, tiled, jnp.zeros_like(tiled))


def dot(a, b):
    return jnp.dot(a, b, preferred_element_type=F32)


def conv_body(rim, own_part, query, taps, ends_coef, *refs):
    conv, mixed, ends = refs[-3:]
    lower = lower_mask()
    for s in range(rim.shape[1] // LANES):
        cols = slice(s * LANES, (s + 1) * LANES)
        blocks = [
            jnp.where(lower, jnp.zeros_like(circ), circ).astype(BF16)
            for circ in circulants(taps, s * PER_SLAB)
        ]
        out = own_part[:, cols] + pick_groups(
            dot(jnp.concatenate(blocks, axis=0), rim[:, cols]), LANES
        )
        conv[:, cols] = out.astype(conv.dtype)
        mixed[:, cols] = (query[:, cols].astype(F32) * out).astype(BF16)
    for s in range(rim.shape[1] // LANES):
        cols = slice(s * LANES, (s + 1) * LANES)
        ends[:, cols] = pick_groups(
            dot(ends_coef[s * LANES : (s + 1) * LANES, :], mixed[:, cols]), ORDER
        ).astype(ends.dtype)


def local_body(transposed, rows, x, *refs):
    out = refs[-1]
    lower = lower_mask()
    keep = ~lower | (lax.broadcasted_iota(jnp.int32, (LANES, LANES), 0)
                     == lax.broadcasted_iota(jnp.int32, (LANES, LANES), 1)) if transposed else lower
    for s in range(x.shape[1] // LANES):
        cols = slice(s * LANES, (s + 1) * LANES)
        blocks = [
            jnp.where(keep, circ, jnp.zeros_like(circ)).astype(BF16)
            for circ in circulants(rows, s * PER_SLAB)
        ]
        out[:, cols] = pick_groups(
            dot(jnp.concatenate(blocks, axis=0), x[:, cols]), LANES
        ).astype(out.dtype)


def carried(states, coef, cols):
    wide_states = jnp.concatenate([spread_groups(ref[:, cols]) for ref in states], axis=0)
    count = len(states)
    rows = coef.shape[0] // count
    parts = [coef[k * rows : (k + 1) * rows, cols] for k in range(count)]
    return dot(jnp.concatenate(parts, axis=1), wide_states)


def long_body(count, local, coef, gate, *refs):
    states, (long_out, gated) = refs[:count], refs[-2:]
    for s in range(local.shape[1] // LANES):
        cols = slice(s * LANES, (s + 1) * LANES)
        out = local[:, cols].astype(F32) + carried(states, coef, cols)
        long_out[:, cols] = out.astype(long_out.dtype)
        gated[0, :, cols] = (gate[:, cols].astype(F32) * out).astype(BF16)


def seed_body(delta, gate, long_out, starts_coef, seed, starts, gate_grad):
    for s in range(gate.shape[1] // LANES):
        cols = slice(s * LANES, (s + 1) * LANES)
        out = delta[0, :, cols].astype(F32)
        seed[:, cols] = (out * gate[:, cols].astype(F32)).astype(BF16)
        gate_grad[:, cols] = (out * long_out[:, cols].astype(F32)).astype(BF16)
    for s in range(gate.shape[1] // LANES):
        cols = slice(s * LANES, (s + 1) * LANES)
        starts[:, cols] = pick_groups(
            dot(starts_coef[s * LANES : (s + 1) * LANES, :], seed[:, cols]), ORDER
        ).astype(starts.dtype)


def back_body(count, local, coef, conv, query, *refs):
    states, (query_grad, conv_grad) = refs[:count], refs[-2:]
    for s in range(local.shape[1] // LANES):
        cols = slice(s * LANES, (s + 1) * LANES)
        out = local[:, cols].astype(F32) + carried(states, coef, cols)
        query_grad[:, cols] = (out * conv[:, cols].astype(F32)).astype(BF16)
        conv_grad[:, cols] = (out * query[:, cols].astype(F32)).astype(BF16)


def pack_body(count, place, *refs):
    for source, target in zip(refs[:count], refs[-count:]):
        target[...] = source[...]


def join_body(*refs):
    out = refs[-1]
    for k in range(out.shape[0]):
        out[k] = refs[k][...]


def delta_body(count, place, dest, grad, *refs):
    weights, out = refs[:count], refs[-1]
    depth = weights[0].shape[1]
    total = None
    for k, weight in enumerate(weights):
        start = pl.multiple_of((place[0] ^ k) * depth, depth)
        rows = grad[:, :, :, :, pl.ds(start, depth)].reshape(-1, depth)
        term = lax.dot_general(
            rows, weight[...], (((1,), (1,)), ((), ())), preferred_element_type=F32
        )
        total = term if total is None else total + term
    out[...] = total.astype(out.dtype).reshape(out.shape)


def flip_body(place, grad, after, out):
    out[...] = grad[...].reshape(-1, grad.shape[-1]).T


def lay_body(place, *refs):
    sources, out = refs[:-2], refs[-1]
    for k, source in enumerate(sources):
        lanes = source.shape[1]
        out[:, pl.ds(pl.multiple_of((place[0] ^ k) * lanes, lanes), lanes)] = source[...]


def add_body(dests, partial_right, partial_left, right, left, *refs):
    out_right, out_left = refs[-2:]
    out_right[...] = (partial_right[...].astype(F32) + right[...].astype(F32)).astype(BF16)
    out_left[...] = (partial_left[...].astype(F32) + left[...].astype(F32)).astype(BF16)


def merge_body(own, *refs):
    out = refs[-1]
    count = out.shape[0] - 1
    out[0] = own[...]
    for k in range(count):
        out[k + 1] = refs[k][...] + refs[count + k][...]


def sum_body(dest, partial, right, left, out):
    total = partial[0].astype(F32) + right[0].astype(F32) + left[0].astype(F32)
    out[...] = total.astype(BF16)


def weight_body(place, grad_t, gated, after, out):
    out[...] = dot(grad_t[...], gated[...]).astype(out.dtype)


def wide(rows, lanes):
    return pl.BlockSpec((rows, lanes), lambda i: (0, i))


def tall(rows, cols):
    return pl.BlockSpec((rows, cols), lambda i: (i, 0))


def deep(count, rows, lanes):
    return pl.BlockSpec((count, rows, lanes), lambda i: (0, 0, i))


def shape(*dims, dtype=BF16):
    return jax.ShapeDtypeStruct(dims, dtype)


def on_device(query, key_in, value_in, gate, out_grad, proj_weight, mr_filter, lr_rate, lr_residue):
    rows, width = query.shape
    groups = width // GROUP
    n_dp, n_ctx, n_tp = (lax.axis_size(a) for a in ("dp", "ctx", "tp"))
    feats = proj_weight.shape[1]
    quarter = width // n_dp
    depth = n_dp * feats
    block = quarter
    steps = width // block
    part = rows // n_tp

    place = jnp.stack([lax.axis_index(a) for a in ("dp", "ctx", "tp")]).astype(jnp.int32)

    def swap(value, axis, k):
        return lax.ppermute(value, axis, [(i, i ^ k) for i in range(lax.axis_size(axis))])

    def shift(value, k, senders=None):
        ends = [(i, i + k) for i in senders or range(n_ctx) if 0 <= i + k < n_ctx]
        return lax.ppermute(value, "ctx", ends)

    def piece(k):
        return pl.BlockSpec((part, feats), lambda j, p: (p[2], j * n_ctx + (p[1] ^ k)))

    sent = [
        lax.dynamic_slice_in_dim(proj_weight, (place[0] ^ k) * quarter, quarter)
        for k in range(1, n_dp)
    ]
    weights = [proj_weight] + [swap(value, "dp", k) for k, value in enumerate(sent, 1)]
    mine = call(
        functools.partial(pack_body, n_ctx), "pack", 0, 4 * part * depth * n_ctx,
        grid_spec=pltpu.PrefetchScalarGridSpec(
            num_scalar_prefetch=1, grid=(n_dp,),
            in_specs=[piece(k) for k in range(n_ctx)] + [ANY] * len(sent),
            out_specs=[pl.BlockSpec((part, feats), lambda j, p: (0, j))] * n_ctx,
        ),
        out_shape=[shape(part, depth)] * n_ctx,
    )(place, *[out_grad] * n_ctx, *sent)
    mine = [mine[0]] + [swap(mine[k], "ctx", k) for k in range(1, n_ctx)]
    product = (key_in.astype(F32) * value_in.astype(F32)).astype(BF16)
    rim = shift(product, 1)
    rate = lr_rate.reshape(-1, 1)
    residue = lr_residue.reshape(-1, 1)
    counts = jnp.arange(rows, dtype=F32)[None, :]
    ends_coef = jnp.exp(-rate * (rows - 1 - counts)).astype(BF16)
    starts_coef = jnp.exp(-rate * counts).astype(BF16)
    away = jnp.arange((n_ctx - 1) * rows, dtype=F32)[:, None]
    inside = away % rows
    carry_coef = (residue.T * jnp.exp(-rate.T * (away + 1))).astype(BF16)
    back_coef = (residue.T * jnp.exp(-rate.T * (away + rows - 2 * inside))).astype(BF16)
    kernel = jnp.sum(
        lr_residue[:, :, None] * jnp.exp(-lr_rate[:, :, None] * counts[:, None, :]), axis=1
    )

    def reversed_row(values):
        return jnp.roll(values[:, ::-1], 1, axis=1)

    taps = reversed_row(mr_filter.astype(F32))
    kernel_rev = reversed_row(kernel)
    def local(transposed, table, x, *after):
        return call(
            functools.partial(local_body, transposed),
            "local_t" if transposed else "local",
            2 * rows * 128 * width * 8, rows * width * 6,
            grid=(steps,),
            in_specs=[tall(block // GROUP, rows), wide(rows, block)] + [ANY] * len(after),
            out_specs=wide(rows, block),
            out_shape=shape(rows, width, dtype=F32),
        )(table, x, *after)

    conv_own = local(False, taps, product)
    conv, mixed, ends = call(
        conv_body, "conv", 2 * rows * 128 * width * 8, rows * width * 14,
        grid=(steps,),
        in_specs=[wide(rows, block)] * 3 + [tall(block // GROUP, TAPS), tall(block, rows)],
        out_specs=[wide(rows, block), wide(rows, block), wide(ORDER, block)],
        out_shape=[shape(rows, width), shape(rows, width), shape(ORDER, width)],
    )(rim, conv_own, query, taps, ends_coef)
    ends_far = [shift(ends, k) for k in range(1, n_ctx)]
    mine = call(
        join_body, "join", 0, 4 * part * depth * n_ctx,
        grid=(n_dp,),
        in_specs=[wide(part, feats)] * n_ctx + [ANY] * n_dp,
        out_specs=deep(n_ctx, part, feats),
        out_shape=shape(n_ctx, part, depth),
    )(*mine, *weights[1:], mixed)
    grad = lax.all_gather(mine, ("dp", "tp"), axis=0, tiled=False)
    grad = grad.reshape(n_dp, n_tp, n_ctx, part, depth)


    local_fwd = local(False, kernel_rev, mixed, mine)
    long_out, gated = call(
        functools.partial(long_body, n_ctx - 1), "long", 2 * rows * 128 * width, rows * width * 10,
        grid=(steps,),
        in_specs=[wide(rows, block), wide((n_ctx - 1) * rows, block), wide(rows, block)] + [wide(ORDER, block)] * (n_ctx - 1),
        out_specs=[wide(rows, block), pl.BlockSpec((1, rows, block), lambda i: (i, 0, 0))],
        out_shape=[shape(rows, width), shape(n_dp, rows, quarter)],
    )(local_fwd, carry_coef, gate, *ends_far)
    gated_far = lax.all_to_all(gated, "dp", 0, 0, tiled=True)
    tokens = n_ctx * n_dp * rows
    last = n_ctx - 1
    from_left, from_right = [], []
    right = left = gated_far
    for t in range(last):
        right = shift(right, 1, range(t, last))
        left = shift(left, -1, range(1, n_ctx - t))
        from_left.append(right)
        from_right.append(left)

    first_dest = jnp.where(place[1] < n_ctx // 2, last, 0)
    chunk = (1, n_dp, rows, quarter)

    def project(count, dest, *after):
        return call(
            functools.partial(delta_body, n_dp), "delta", 2 * count * n_dp * rows * depth * quarter,
            2 * tokens * depth + 2 * depth * quarter + 2 * count * n_dp * rows * quarter,
            grid_spec=pltpu.PrefetchScalarGridSpec(
                num_scalar_prefetch=2, grid=(count,),
                in_specs=[
                    pl.BlockSpec(
                        (n_dp, n_tp, 1, part, depth), lambda i, p, q: (0, 0, p[1] ^ q[i], 0, 0)
                    ),
                    pl.BlockSpec((quarter, feats), lambda i, p, q: (p[0], 0)),
                ] + [pl.BlockSpec((quarter, feats), lambda i, p, q: (0, 0))] * (n_dp - 1)
                + [ANY] * len(after),
                out_specs=pl.BlockSpec(chunk, lambda i, p, q: (i, 0, 0, 0)),
            ),
            out_shape=shape(count, n_dp, rows, quarter),
        )(place, dest, grad, *weights, *after)

    first = project(1, first_dest[None], from_left[0], from_right[0])
    partial = project(n_ctx, jnp.arange(n_ctx, dtype=jnp.int32), first)
    right, left = shift(first, 1, [0]), shift(first, -1, [last])

    def pick(ahead):
        return pl.BlockSpec(
            (1, 1, rows, quarter), lambda i, q: (q[ahead], i, 0, 0)
        )

    piece_of = pl.BlockSpec((1, 1, rows, quarter), lambda i, q: (0, i, 0, 0))
    for t in range(1, last):
        dests = jnp.clip(jnp.stack([last - t + place[1], t - last + place[1]]), 0, last)
        right, left = call(
            add_body, "add", 0, 12 * n_dp * rows * quarter,
            grid_spec=pltpu.PrefetchScalarGridSpec(
                num_scalar_prefetch=1, grid=(n_dp,),
                in_specs=[pick(0), pick(1), piece_of, piece_of, ANY, ANY],
                out_specs=[piece_of] * 2,
            ),
            out_shape=[shape(*chunk)] * 2,
        )(dests, partial, partial, right, left, from_left[t], from_right[t])
        token = right
        right = shift(right, 1, range(t + 1))
        left = shift(left, -1, range(last - t, n_ctx))
    delta = call(
        sum_body, "sum", 0, 8 * n_dp * rows * quarter,
        grid_spec=pltpu.PrefetchScalarGridSpec(
            num_scalar_prefetch=1, grid=(n_dp,),
            in_specs=[pick(0), piece_of, piece_of],
            out_specs=pl.BlockSpec((1, rows, quarter), lambda i, q: (i, 0, 0)),
        ),
        out_shape=shape(n_dp, rows, quarter),
    )(place[1:2], partial, right, left)
    delta_far = lax.all_to_all(delta, "dp", 0, 0, tiled=True)

    grad_t = call(
        flip_body, "flip", 0, 4 * tokens * depth,
        grid_spec=pltpu.PrefetchScalarGridSpec(
            num_scalar_prefetch=1, grid=(n_ctx, n_dp),
            in_specs=[
                pl.BlockSpec(
                    (1, n_tp, 1, part, depth),
                    lambda i, j, p: (j, 0, p[1] ^ ((p[1] + n_ctx - i) % n_ctx), 0, 0),
                ),
                ANY,
            ],
            out_specs=pl.BlockSpec((depth, rows), lambda i, j, p: (0, i * n_dp + j)),
        ),
        out_shape=shape(depth, tokens),
    )(place, grad, partial)
    gated_all = call(
        merge_body, "merge", 0, 2 * (2 * n_ctx + last) * n_dp * rows * quarter,
        grid=(n_dp,),
        in_specs=[pl.BlockSpec((1, rows, quarter), lambda i: (i, 0, 0))] * (1 + 2 * last) + [ANY],
        out_specs=pl.BlockSpec((n_ctx, 1, rows, quarter), lambda i: (0, i, 0, 0)),
        out_shape=shape(n_ctx, n_dp, rows, quarter),
    )(gated_far, *from_left, *from_right[::-1], token).reshape(tokens, quarter)
    weight_far = []
    for k in list(range(1, n_dp)) + [0]:
        token = call(
            weight_body, "weight", 2 * tokens * feats * quarter, 2 * tokens * (feats + quarter),
            grid_spec=pltpu.PrefetchScalarGridSpec(
                num_scalar_prefetch=1, grid=(2,),
                in_specs=[
                    pl.BlockSpec((feats, tokens), lambda i, p, k=k: (p[0] ^ k, 0)),
                    pl.BlockSpec((tokens, quarter // 2), lambda i, p: (0, i)),
                    ANY,
                ],
                out_specs=pl.BlockSpec((feats, quarter // 2), lambda i, p: (0, i)),
            ),
            out_shape=shape(feats, quarter),
        )(place, grad_t, gated_all, token)
        weight_far.append(swap(token, "dp", k) if k else token)

    seed, starts, gate_grad = call(
        seed_body, "seed", 2 * rows * 128 * width, rows * width * 10,
        grid=(steps,),
        in_specs=[
            pl.BlockSpec((1, rows, block), lambda i: (i, 0, 0)),
            wide(rows, block), wide(rows, block), tall(block, rows),
        ],
        out_specs=[wide(rows, block), wide(ORDER, block), wide(rows, block)],
        out_shape=[shape(rows, width), shape(ORDER, width), shape(rows, width)],
    )(delta_far, gate, long_out, starts_coef)
    starts_far = [shift(starts, -k) for k in range(1, n_ctx)]
    local_bwd = local(True, kernel, seed)
    query_grad, conv_grad = call(
        functools.partial(back_body, n_ctx - 1), "back", 2 * rows * 128 * width, rows * width * 12,
        grid=(steps,),
        in_specs=[wide(rows, block), wide((n_ctx - 1) * rows, block)] + [wide(rows, block)] * 2
        + [wide(ORDER, block)] * (n_ctx - 1),
        out_specs=[wide(rows, block)] * 2,
        out_shape=[shape(rows, width)] * 2,
    )(local_bwd, back_coef, conv, query, *starts_far)

    cut = feats // n_dp
    weight_grad = call(
        lay_body, "lay", 0, 4 * feats * width,
        grid_spec=pltpu.PrefetchScalarGridSpec(
            num_scalar_prefetch=1, grid=(n_dp,),
            in_specs=[pl.BlockSpec((cut, quarter), lambda i, p: (i, 0))] * n_dp + [ANY],
            out_specs=pl.BlockSpec((cut, width), lambda i, p: (i, 0)),
        ),
        out_shape=shape(feats, width),
    )(place, weight_far[-1], *weight_far[:-1], query_grad)
    return query_grad, conv_grad, gate_grad, weight_grad


def solution(mesh):
    rows = P(("dp", "ctx"), "tp")
    return jax.shard_map(
        on_device,
        mesh=mesh,
        in_specs=(rows, rows, rows, rows, P(("dp", "ctx"), None), P("tp", ("dp", "ctx")),
                  P("tp", None), P("tp", None), P("tp", None)),
        out_specs=(rows, rows, rows, rows),
        check_vma=False,
    )
```

```python
import functools

import jax
import jax.numpy as jnp
from jax import lax
from jax.experimental import pallas as pl
from jax.experimental.pallas import tpu as pltpu
from jax.sharding import PartitionSpec as P

GROUP = 16
TAPS = 128
ORDER = 16
LANES = 128
PER_SLAB = LANES // GROUP
BF16 = jnp.bfloat16
F32 = jnp.float32
VMEM = 50 * 2**20
ANY = pl.BlockSpec(memory_space=pl.ANY)


def call(body, name, flops, nbytes, **kwargs):
    return pl.pallas_call(
        body,
        name=name,
        cost_estimate=pl.CostEstimate(flops=flops, bytes_accessed=nbytes, transcendentals=0),
        compiler_params=pltpu.CompilerParams(vmem_limit_bytes=VMEM),
        **kwargs,
    )


def circulants(rows_ref, base):
    out = []
    for j in range(PER_SLAB):
        row = rows_ref[base + j : base + j + 1, :]
        out.append(
            pltpu.roll(jnp.broadcast_to(row, (LANES, LANES)), 0, 1, stride=1, stride_axis=0)
        )
    return out


def lower_mask():
    t = lax.broadcasted_iota(jnp.int32, (LANES, LANES), 0)
    u = lax.broadcasted_iota(jnp.int32, (LANES, LANES), 1)
    return u <= t


def pick_groups(stacked, rows):
    lane_group = lax.broadcasted_iota(jnp.int32, (rows, LANES), 1) // GROUP
    out = stacked[:rows]
    for j in range(1, PER_SLAB):
        out = jnp.where(lane_group == j, stacked[j * rows : (j + 1) * rows], out)
    return out


def spread_groups(state):
    tiled = jnp.concatenate([state] * PER_SLAB, axis=0)
    row_group = lax.broadcasted_iota(jnp.int32, (LANES, LANES), 0) // ORDER
    lane_group = lax.broadcasted_iota(jnp.int32, (LANES, LANES), 1) // GROUP
    return jnp.where(row_group == lane_group, tiled, jnp.zeros_like(tiled))


def dot(a, b):
    return jnp.dot(a, b, preferred_element_type=F32)


def conv_body(rim, own_part, query, taps, ends_coef, *refs):
    conv, mixed, ends = refs[-3:]
    lower = lower_mask()
    for s in range(rim.shape[1] // LANES):
        cols = slice(s * LANES, (s + 1) * LANES)
        blocks = [
            jnp.where(lower, jnp.zeros_like(circ), circ).astype(BF16)
            for circ in circulants(taps, s * PER_SLAB)
        ]
        out = own_part[:, cols] + pick_groups(
            dot(jnp.concatenate(blocks, axis=0), rim[:, cols]), LANES
        )
        conv[:, cols] = out.astype(conv.dtype)
        mixed[:, cols] = (query[:, cols].astype(F32) * out).astype(BF16)
    for s in range(rim.shape[1] // LANES):
        cols = slice(s * LANES, (s + 1) * LANES)
        ends[:, cols] = pick_groups(
            dot(ends_coef[s * LANES : (s + 1) * LANES, :], mixed[:, cols]), ORDER
        ).astype(ends.dtype)


def local_body(transposed, rows, x, *refs):
    out = refs[-1]
    lower = lower_mask()
    keep = ~lower | (lax.broadcasted_iota(jnp.int32, (LANES, LANES), 0)
                     == lax.broadcasted_iota(jnp.int32, (LANES, LANES), 1)) if transposed else lower
    for s in range(x.shape[1] // LANES):
        cols = slice(s * LANES, (s + 1) * LANES)
        blocks = [
            jnp.where(keep, circ, jnp.zeros_like(circ)).astype(BF16)
            for circ in circulants(rows, s * PER_SLAB)
        ]
        out[:, cols] = pick_groups(
            dot(jnp.concatenate(blocks, axis=0), x[:, cols]), LANES
        ).astype(out.dtype)


def carried(states, coef, cols):
    wide_states = jnp.concatenate([spread_groups(ref[:, cols]) for ref in states], axis=0)
    count = len(states)
    rows = coef.shape[0] // count
    parts = [coef[k * rows : (k + 1) * rows, cols] for k in range(count)]
    return dot(jnp.concatenate(parts, axis=1), wide_states)


def long_body(count, local, coef, gate, *refs):
    states, (long_out, gated) = refs[:count], refs[-2:]
    for s in range(local.shape[1] // LANES):
        cols = slice(s * LANES, (s + 1) * LANES)
        out = local[:, cols].astype(F32) + carried(states, coef, cols)
        long_out[:, cols] = out.astype(long_out.dtype)
        gated[0, :, cols] = (gate[:, cols].astype(F32) * out).astype(BF16)


def seed_body(delta, gate, long_out, starts_coef, seed, starts, gate_grad):
    for s in range(gate.shape[1] // LANES):
        cols = slice(s * LANES, (s + 1) * LANES)
        out = delta[0, :, cols].astype(F32)
        seed[:, cols] = (out * gate[:, cols].astype(F32)).astype(BF16)
        gate_grad[:, cols] = (out * long_out[:, cols].astype(F32)).astype(BF16)
    for s in range(gate.shape[1] // LANES):
        cols = slice(s * LANES, (s + 1) * LANES)
        starts[:, cols] = pick_groups(
            dot(starts_coef[s * LANES : (s + 1) * LANES, :], seed[:, cols]), ORDER
        ).astype(starts.dtype)


def back_body(count, local, coef, conv, query, *refs):
    states, (query_grad, conv_grad) = refs[:count], refs[-2:]
    for s in range(local.shape[1] // LANES):
        cols = slice(s * LANES, (s + 1) * LANES)
        out = local[:, cols].astype(F32) + carried(states, coef, cols)
        query_grad[:, cols] = (out * conv[:, cols].astype(F32)).astype(BF16)
        conv_grad[:, cols] = (out * query[:, cols].astype(F32)).astype(BF16)


def pack_body(place, *refs):
    count = len(refs) // 2
    for source, target in zip(refs[:count], refs[-count:]):
        target[...] = source[...]


def join_body(*refs):
    out = refs[-1]
    for k in range(out.shape[0]):
        out[k] = refs[k][...]


def delta_body(place, dest, grad, weights, *refs):
    depth = weights.shape[2]
    total = None
    for k in range(weights.shape[0]):
        rows = grad[:, :, :, :, k * depth : (k + 1) * depth].reshape(-1, depth)
        term = lax.dot_general(
            rows, weights[k], (((1,), (1,)), ((), ())), preferred_element_type=F32
        )
        total = term if total is None else total + term
    refs[-1][...] = total.astype(BF16).reshape(refs[-1].shape)


def flip_body(place, grad, after, out):
    out[...] = grad[...].reshape(-1, grad.shape[-1]).T


def lay_body(place, *refs):
    sources, out = refs[:-2], refs[-1]
    for k, source in enumerate(sources):
        lanes = source.shape[1]
        out[:, pl.ds(pl.multiple_of((place[0] ^ k) * lanes, lanes), lanes)] = source[...]


def add_body(dests, partial_right, partial_left, right, left, *refs):
    out_right, out_left = refs[-2:]
    out_right[...] = (partial_right[...].astype(F32) + right[...].astype(F32)).astype(BF16)
    out_left[...] = (partial_left[...].astype(F32) + left[...].astype(F32)).astype(BF16)


def merge_body(own, *refs):
    out = refs[-1]
    count = out.shape[0] - 1
    out[0] = own[...]
    for k in range(count):
        out[k + 1] = refs[k][...] + refs[count + k][...]


def sum_body(dest, partial, right, left, out):
    total = partial[0].astype(F32) + right[0].astype(F32) + left[0].astype(F32)
    out[...] = total.astype(BF16)


def weight_body(place, grad_t, gated, after, out):
    out[...] = dot(grad_t[...], gated[...]).astype(out.dtype)


def wide(rows, lanes):
    return pl.BlockSpec((rows, lanes), lambda i: (0, i))


def tall(rows, cols):
    return pl.BlockSpec((rows, cols), lambda i: (i, 0))


def deep(count, rows, lanes):
    return pl.BlockSpec((count, rows, lanes), lambda i: (0, 0, i))


def shape(*dims, dtype=BF16):
    return jax.ShapeDtypeStruct(dims, dtype)


def on_device(query, key_in, value_in, gate, out_grad, proj_weight, mr_filter, lr_rate, lr_residue):
    rows, width = query.shape
    groups = width // GROUP
    n_dp, n_ctx, n_tp = (lax.axis_size(a) for a in ("dp", "ctx", "tp"))
    feats = proj_weight.shape[1]
    quarter = width // n_dp
    depth = n_dp * feats
    block = quarter
    steps = width // block
    part = rows // n_tp

    place = jnp.stack([lax.axis_index(a) for a in ("dp", "ctx", "tp")]).astype(jnp.int32)

    def swap(value, axis, k):
        return lax.ppermute(value, axis, [(i, i ^ k) for i in range(lax.axis_size(axis))])

    def shift(value, k, senders=None):
        ends = [(i, i + k) for i in senders or range(n_ctx) if 0 <= i + k < n_ctx]
        return lax.ppermute(value, "ctx", ends)

    def piece(k):
        return pl.BlockSpec((part, feats), lambda j, p: (p[2], j * n_ctx + (p[1] ^ k)))

    weights = lax.all_to_all(proj_weight.reshape(n_dp, quarter, feats), "dp", 0, 0, tiled=True)
    mine = call(
        pack_body, "pack", 0, 4 * part * depth * n_ctx,
        grid_spec=pltpu.PrefetchScalarGridSpec(
            num_scalar_prefetch=1, grid=(n_dp,),
            in_specs=[piece(k) for k in range(n_ctx)],
            out_specs=[pl.BlockSpec((part, feats), lambda j, p: (0, j))] * n_ctx,
        ),
        out_shape=[shape(part, depth)] * n_ctx,
    )(place, *[out_grad] * n_ctx)
    mine = [mine[0]] + [swap(mine[k], "ctx", k) for k in range(1, n_ctx)]
    product = (key_in.astype(F32) * value_in.astype(F32)).astype(BF16)
    rim = shift(product, 1)
    rate = lr_rate.reshape(-1, 1)
    residue = lr_residue.reshape(-1, 1)
    counts = jnp.arange(rows, dtype=F32)[None, :]
    ends_coef = jnp.exp(-rate * (rows - 1 - counts)).astype(BF16)
    starts_coef = jnp.exp(-rate * counts).astype(BF16)
    away = jnp.arange((n_ctx - 1) * rows, dtype=F32)[:, None]
    inside = away % rows
    carry_coef = (residue.T * jnp.exp(-rate.T * (away + 1))).astype(BF16)
    back_coef = (residue.T * jnp.exp(-rate.T * (away + rows - 2 * inside))).astype(BF16)
    kernel = jnp.sum(
        lr_residue[:, :, None] * jnp.exp(-lr_rate[:, :, None] * counts[:, None, :]), axis=1
    )

    def reversed_row(values):
        return jnp.roll(values[:, ::-1], 1, axis=1)

    taps = reversed_row(mr_filter.astype(F32))
    kernel_rev = reversed_row(kernel)
    def local(transposed, table, x, *after):
        return call(
            functools.partial(local_body, transposed),
            "local_t" if transposed else "local",
            2 * rows * 128 * width * 8, rows * width * 6,
            grid=(steps,),
            in_specs=[tall(block // GROUP, rows), wide(rows, block)] + [ANY] * len(after),
            out_specs=wide(rows, block),
            out_shape=shape(rows, width, dtype=F32),
        )(table, x, *after)

    conv_own = local(
        False, taps, product, ends_coef, starts_coef, carry_coef, back_coef, kernel_rev, kernel
    )
    conv, mixed, ends = call(
        conv_body, "conv", 2 * rows * 128 * width * 8, rows * width * 14,
        grid=(steps,),
        in_specs=[wide(rows, block)] * 3 + [tall(block // GROUP, TAPS), tall(block, rows)],
        out_specs=[wide(rows, block), wide(rows, block), wide(ORDER, block)],
        out_shape=[shape(rows, width), shape(rows, width), shape(ORDER, width)],
    )(rim, conv_own, query, taps, ends_coef)
    ends_far = [shift(ends, k) for k in range(1, n_ctx)]
    mine = call(
        join_body, "join", 0, 4 * part * depth * n_ctx,
        grid=(n_dp,),
        in_specs=[wide(part, feats)] * n_ctx + [ANY] * 2,
        out_specs=deep(n_ctx, part, feats),
        out_shape=shape(n_ctx, part, depth),
    )(*mine, weights, mixed)
    grad = lax.all_gather(mine, ("dp", "tp"), axis=0, tiled=False)
    grad = grad.reshape(n_dp, n_tp, n_ctx, part, depth)


    local_fwd = local(False, kernel_rev, mixed, mine)
    long_out, gated = call(
        functools.partial(long_body, n_ctx - 1), "long", 2 * rows * 128 * width, rows * width * 10,
        grid=(steps,),
        in_specs=[wide(rows, block), wide((n_ctx - 1) * rows, block), wide(rows, block)] + [wide(ORDER, block)] * (n_ctx - 1),
        out_specs=[wide(rows, block), pl.BlockSpec((1, rows, block), lambda i: (i, 0, 0))],
        out_shape=[shape(rows, width), shape(n_dp, rows, quarter)],
    )(local_fwd, carry_coef, gate, *ends_far)
    gated_far = lax.all_to_all(gated, "dp", 0, 0, tiled=True)
    tokens = n_ctx * n_dp * rows
    last = n_ctx - 1
    from_left, from_right = [], []
    right = left = gated_far
    for t in range(last):
        right = shift(right, 1, range(t, last))
        left = shift(left, -1, range(1, n_ctx - t))
        from_left.append(right)
        from_right.append(left)

    first_dest = jnp.where(place[1] < n_ctx // 2, last, 0)
    chunk = (1, n_dp, rows, quarter)

    def project(count, dest, *after):
        return call(
            delta_body, "delta", 2 * count * n_dp * rows * depth * quarter,
            2 * tokens * depth + 2 * depth * quarter + 2 * count * n_dp * rows * quarter,
            grid_spec=pltpu.PrefetchScalarGridSpec(
                num_scalar_prefetch=2, grid=(count,),
                in_specs=[
                    pl.BlockSpec(
                        (n_dp, n_tp, 1, part, depth), lambda i, p, q: (0, 0, p[1] ^ q[i], 0, 0)
                    ),
                    pl.BlockSpec((n_dp, quarter, feats), lambda i, p, q: (0, 0, 0)),
                ] + [ANY] * len(after),
                out_specs=pl.BlockSpec(chunk, lambda i, p, q: (i, 0, 0, 0)),
            ),
            out_shape=shape(count, n_dp, rows, quarter),
        )(place, dest, grad, weights, *after)

    first = project(1, first_dest[None], from_left[0], from_right[0])
    partial = project(n_ctx, jnp.arange(n_ctx, dtype=jnp.int32), first)
    grad_t = call(
        flip_body, "flip", 0, 4 * tokens * depth,
        grid_spec=pltpu.PrefetchScalarGridSpec(
            num_scalar_prefetch=1, grid=(n_ctx, n_dp),
            in_specs=[
                pl.BlockSpec(
                    (1, n_tp, 1, part, depth),
                    lambda i, j, p: (j, 0, p[1] ^ ((p[1] + n_ctx - i) % n_ctx), 0, 0),
                ),
                ANY,
            ],
            out_specs=pl.BlockSpec((depth, rows), lambda i, j, p: (0, i * n_dp + j)),
        ),
        out_shape=shape(depth, tokens),
    )(place, grad, partial)
    right, left = shift(first, 1, [0]), shift(first, -1, [last])

    def pick(ahead):
        return pl.BlockSpec(
            (1, 1, rows, quarter), lambda i, q: (q[ahead], i, 0, 0)
        )

    piece_of = pl.BlockSpec((1, 1, rows, quarter), lambda i, q: (0, i, 0, 0))
    for t in range(1, last):
        after = (from_left[t], from_right[t]) + ((grad_t,) if t == last - 1 else ())
        dests = jnp.clip(jnp.stack([last - t + place[1], t - last + place[1]]), 0, last)
        right, left = call(
            add_body, "add", 0, 12 * n_dp * rows * quarter,
            grid_spec=pltpu.PrefetchScalarGridSpec(
                num_scalar_prefetch=1, grid=(n_dp,),
                in_specs=[pick(0), pick(1), piece_of, piece_of] + [ANY] * len(after),
                out_specs=[piece_of] * 2,
            ),
            out_shape=[shape(*chunk)] * 2,
        )(dests, partial, partial, right, left, *after)
        token = right
        right = shift(right, 1, range(t + 1))
        left = shift(left, -1, range(last - t, n_ctx))
    delta = call(
        sum_body, "sum", 0, 8 * n_dp * rows * quarter,
        grid_spec=pltpu.PrefetchScalarGridSpec(
            num_scalar_prefetch=1, grid=(n_dp,),
            in_specs=[pick(0), piece_of, piece_of],
            out_specs=pl.BlockSpec((1, rows, quarter), lambda i, q: (i, 0, 0)),
        ),
        out_shape=shape(n_dp, rows, quarter),
    )(place[1:2], partial, right, left)
    delta_far = lax.all_to_all(delta, "dp", 0, 0, tiled=True)

    gated_all = call(
        merge_body, "merge", 0, 2 * (2 * n_ctx + last) * n_dp * rows * quarter,
        grid=(n_dp,),
        in_specs=[pl.BlockSpec((1, rows, quarter), lambda i: (i, 0, 0))] * (1 + 2 * last) + [ANY],
        out_specs=pl.BlockSpec((n_ctx, 1, rows, quarter), lambda i: (0, i, 0, 0)),
        out_shape=shape(n_ctx, n_dp, rows, quarter),
    )(gated_far, *from_left, *from_right[::-1], token).reshape(tokens, quarter)
    weight_far = []
    for k in list(range(1, n_dp)) + [0]:
        token = call(
            weight_body, "weight", 2 * tokens * feats * quarter, 2 * tokens * (feats + quarter),
            grid_spec=pltpu.PrefetchScalarGridSpec(
                num_scalar_prefetch=1, grid=(2,),
                in_specs=[
                    pl.BlockSpec((feats, tokens), lambda i, p, k=k: (p[0] ^ k, 0)),
                    pl.BlockSpec((tokens, quarter // 2), lambda i, p: (0, i)),
                    ANY,
                ],
                out_specs=pl.BlockSpec((feats, quarter // 2), lambda i, p: (0, i)),
            ),
            out_shape=shape(feats, quarter),
        )(place, grad_t, gated_all, token)
        weight_far.append(swap(token, "dp", k) if k else token)

    seed, starts, gate_grad = call(
        seed_body, "seed", 2 * rows * 128 * width, rows * width * 10,
        grid=(steps,),
        in_specs=[
            pl.BlockSpec((1, rows, block), lambda i: (i, 0, 0)),
            wide(rows, block), wide(rows, block), tall(block, rows),
        ],
        out_specs=[wide(rows, block), wide(ORDER, block), wide(rows, block)],
        out_shape=[shape(rows, width), shape(ORDER, width), shape(rows, width)],
    )(delta_far, gate, long_out, starts_coef)
    starts_far = [shift(starts, -k) for k in range(1, n_ctx)]
    local_bwd = local(True, kernel, seed)
    query_grad, conv_grad = call(
        functools.partial(back_body, n_ctx - 1), "back", 2 * rows * 128 * width, rows * width * 12,
        grid=(steps,),
        in_specs=[wide(rows, block), wide((n_ctx - 1) * rows, block)] + [wide(rows, block)] * 2
        + [wide(ORDER, block)] * (n_ctx - 1),
        out_specs=[wide(rows, block)] * 2,
        out_shape=[shape(rows, width)] * 2,
    )(local_bwd, back_coef, conv, query, *starts_far)

    cut = feats // n_dp
    weight_grad = call(
        lay_body, "lay", 0, 4 * feats * width,
        grid_spec=pltpu.PrefetchScalarGridSpec(
            num_scalar_prefetch=1, grid=(n_dp,),
            in_specs=[pl.BlockSpec((cut, quarter), lambda i, p: (i, 0))] * n_dp + [ANY],
            out_specs=pl.BlockSpec((cut, width), lambda i, p: (i, 0)),
        ),
        out_shape=shape(feats, width),
    )(place, weight_far[-1], *weight_far[:-1], query_grad)
    return query_grad, conv_grad, gate_grad, weight_grad


def solution(mesh):
    rows = P(("dp", "ctx"), "tp")
    return jax.shard_map(
        on_device,
        mesh=mesh,
        in_specs=(rows, rows, rows, rows, P(("dp", "ctx"), None), P("tp", ("dp", "ctx")),
                  P("tp", None), P("tp", None), P("tp", None)),
        out_specs=(rows, rows, rows, rows),
        check_vma=False,
    )
```

```python
import functools

import jax
import jax.numpy as jnp
from jax import lax
from jax.experimental import pallas as pl
from jax.experimental.pallas import tpu as pltpu
from jax.sharding import PartitionSpec as P

GROUP = 16
TAPS = 128
ORDER = 16
LANES = 128
PER_SLAB = LANES // GROUP
BF16 = jnp.bfloat16
F32 = jnp.float32
VMEM = 50 * 2**20
ANY = pl.BlockSpec(memory_space=pl.ANY)


def call(body, name, flops, nbytes, **kwargs):
    return pl.pallas_call(
        body,
        name=name,
        cost_estimate=pl.CostEstimate(flops=flops, bytes_accessed=nbytes, transcendentals=0),
        compiler_params=pltpu.CompilerParams(vmem_limit_bytes=VMEM),
        **kwargs,
    )


def circulants(rows_ref, base):
    out = []
    for j in range(PER_SLAB):
        row = rows_ref[base + j : base + j + 1, :]
        out.append(
            pltpu.roll(jnp.broadcast_to(row, (LANES, LANES)), 0, 1, stride=1, stride_axis=0)
        )
    return out


def lower_mask():
    t = lax.broadcasted_iota(jnp.int32, (LANES, LANES), 0)
    u = lax.broadcasted_iota(jnp.int32, (LANES, LANES), 1)
    return u <= t


def pick_groups(stacked, rows):
    lane_group = lax.broadcasted_iota(jnp.int32, (rows, LANES), 1) // GROUP
    out = stacked[:rows]
    for j in range(1, PER_SLAB):
        out = jnp.where(lane_group == j, stacked[j * rows : (j + 1) * rows], out)
    return out


def spread_groups(state):
    tiled = jnp.concatenate([state] * PER_SLAB, axis=0)
    row_group = lax.broadcasted_iota(jnp.int32, (LANES, LANES), 0) // ORDER
    lane_group = lax.broadcasted_iota(jnp.int32, (LANES, LANES), 1) // GROUP
    return jnp.where(row_group == lane_group, tiled, jnp.zeros_like(tiled))


def dot(a, b):
    return jnp.dot(a, b, preferred_element_type=F32)


def conv_body(rim, own_part, query, taps, ends_coef, *refs):
    conv, mixed, ends = refs[-3:]
    lower = lower_mask()
    for s in range(rim.shape[1] // LANES):
        cols = slice(s * LANES, (s + 1) * LANES)
        blocks = [
            jnp.where(lower, jnp.zeros_like(circ), circ).astype(BF16)
            for circ in circulants(taps, s * PER_SLAB)
        ]
        out = own_part[:, cols] + pick_groups(
            dot(jnp.concatenate(blocks, axis=0), rim[:, cols]), LANES
        )
        conv[:, cols] = out.astype(conv.dtype)
        mixed[:, cols] = (query[:, cols].astype(F32) * out).astype(BF16)
    for s in range(rim.shape[1] // LANES):
        cols = slice(s * LANES, (s + 1) * LANES)
        ends[:, cols] = pick_groups(
            dot(ends_coef[s * LANES : (s + 1) * LANES, :], mixed[:, cols]), ORDER
        ).astype(ends.dtype)


def local_body(transposed, rows, x, *refs):
    out = refs[-1]
    lower = lower_mask()
    keep = ~lower | (lax.broadcasted_iota(jnp.int32, (LANES, LANES), 0)
                     == lax.broadcasted_iota(jnp.int32, (LANES, LANES), 1)) if transposed else lower
    for s in range(x.shape[1] // LANES):
        cols = slice(s * LANES, (s + 1) * LANES)
        blocks = [
            jnp.where(keep, circ, jnp.zeros_like(circ)).astype(BF16)
            for circ in circulants(rows, s * PER_SLAB)
        ]
        out[:, cols] = pick_groups(
            dot(jnp.concatenate(blocks, axis=0), x[:, cols]), LANES
        ).astype(out.dtype)


def carried(states, coef, cols):
    wide_states = jnp.concatenate([spread_groups(ref[:, cols]) for ref in states], axis=0)
    count = len(states)
    rows = coef.shape[0] // count
    parts = [coef[k * rows : (k + 1) * rows, cols] for k in range(count)]
    return dot(jnp.concatenate(parts, axis=1), wide_states)


def long_body(count, local, coef, gate, *refs):
    states, (long_out, gated) = refs[:count], refs[-2:]
    for s in range(local.shape[1] // LANES):
        cols = slice(s * LANES, (s + 1) * LANES)
        out = local[:, cols].astype(F32) + carried(states, coef, cols)
        long_out[:, cols] = out.astype(long_out.dtype)
        gated[0, :, cols] = (gate[:, cols].astype(F32) * out).astype(BF16)


def seed_body(delta, gate, long_out, starts_coef, seed, starts, gate_grad):
    for s in range(gate.shape[1] // LANES):
        cols = slice(s * LANES, (s + 1) * LANES)
        out = delta[0, :, cols].astype(F32)
        seed[:, cols] = (out * gate[:, cols].astype(F32)).astype(BF16)
        gate_grad[:, cols] = (out * long_out[:, cols].astype(F32)).astype(BF16)
    for s in range(gate.shape[1] // LANES):
        cols = slice(s * LANES, (s + 1) * LANES)
        starts[:, cols] = pick_groups(
            dot(starts_coef[s * LANES : (s + 1) * LANES, :], seed[:, cols]), ORDER
        ).astype(starts.dtype)


def back_body(count, local, coef, conv, query, *refs):
    states, (query_grad, conv_grad) = refs[:count], refs[-2:]
    for s in range(local.shape[1] // LANES):
        cols = slice(s * LANES, (s + 1) * LANES)
        out = local[:, cols].astype(F32) + carried(states, coef, cols)
        query_grad[:, cols] = (out * conv[:, cols].astype(F32)).astype(BF16)
        conv_grad[:, cols] = (out * query[:, cols].astype(F32)).astype(BF16)


def pack_body(place, *refs):
    count = len(refs) // 2
    for source, target in zip(refs[:count], refs[-count:]):
        target[...] = source[...]


def join_body(*refs):
    out = refs[-1]
    for k in range(out.shape[0]):
        out[k] = refs[k][...]


def delta_body(whole, place, dest, grad, weights, *refs):
    depth, out = weights.shape[2], refs[-1]

    def multiply():
        total = None
        for k in range(weights.shape[0]):
            rows = grad[:, :, :, :, k * depth : (k + 1) * depth].reshape(-1, depth)
            term = lax.dot_general(
                rows, weights[k], (((1,), (1,)), ((), ())), preferred_element_type=F32
            )
            total = term if total is None else total + term
        out[...] = total.astype(BF16).reshape(out.shape)

    if not whole:
        return multiply()
    is_last = pl.program_id(0) == pl.num_programs(0) - 1
    pl.when(jnp.logical_not(is_last))(multiply)

    @pl.when(is_last)
    def _():
        out[...] = refs[0][...]


def flip_body(place, grad, after, out):
    out[...] = grad[...].reshape(-1, grad.shape[-1]).T


def lay_body(place, *refs):
    sources, out = refs[:-2], refs[-1]
    for k, source in enumerate(sources):
        lanes = source.shape[1]
        out[:, pl.ds(pl.multiple_of((place[0] ^ k) * lanes, lanes), lanes)] = source[...]


def wait_body(*refs):
    pass


def add_body(dests, partial_right, partial_left, right, left, *refs):
    out_right, out_left = refs[-2:]
    out_right[...] = (partial_right[...].astype(F32) + right[...].astype(F32)).astype(BF16)
    out_left[...] = (partial_left[...].astype(F32) + left[...].astype(F32)).astype(BF16)


def merge_body(own, *refs):
    out = refs[-1]
    count = out.shape[0] - 1
    out[0] = own[...]
    for k in range(count):
        out[k + 1] = refs[k][...] + refs[count + k][...]


def sum_body(dest, partial, right, left, out):
    total = partial[0].astype(F32) + right[0].astype(F32) + left[0].astype(F32)
    out[...] = total.astype(BF16)


def weight_body(place, grad_t, gated, after, out):
    out[...] = dot(grad_t[...], gated[...]).astype(out.dtype)


def wide(rows, lanes):
    return pl.BlockSpec((rows, lanes), lambda i: (0, i))


def tall(rows, cols):
    return pl.BlockSpec((rows, cols), lambda i: (i, 0))


def deep(count, rows, lanes):
    return pl.BlockSpec((count, rows, lanes), lambda i: (0, 0, i))


def shape(*dims, dtype=BF16):
    return jax.ShapeDtypeStruct(dims, dtype)


def on_device(query, key_in, value_in, gate, out_grad, proj_weight, mr_filter, lr_rate, lr_residue):
    rows, width = query.shape
    groups = width // GROUP
    n_dp, n_ctx, n_tp = (lax.axis_size(a) for a in ("dp", "ctx", "tp"))
    feats = proj_weight.shape[1]
    quarter = width // n_dp
    depth = n_dp * feats
    block = quarter
    steps = width // block
    part = rows // n_tp

    place = jnp.stack([lax.axis_index(a) for a in ("dp", "ctx", "tp")]).astype(jnp.int32)

    def swap(value, axis, k):
        return lax.ppermute(value, axis, [(i, i ^ k) for i in range(lax.axis_size(axis))])

    def shift(value, k, senders=None):
        ends = [(i, i + k) for i in senders or range(n_ctx) if 0 <= i + k < n_ctx]
        return lax.ppermute(value, "ctx", ends)

    def piece(k):
        return pl.BlockSpec((part, feats), lambda j, p: (p[2], j * n_ctx + (p[1] ^ k)))

    weights = lax.all_to_all(proj_weight.reshape(n_dp, quarter, feats), "dp", 0, 0, tiled=True)
    mine = call(
        pack_body, "pack", 0, 4 * part * depth * n_ctx,
        grid_spec=pltpu.PrefetchScalarGridSpec(
            num_scalar_prefetch=1, grid=(n_dp,),
            in_specs=[piece(k) for k in range(n_ctx)],
            out_specs=[pl.BlockSpec((part, feats), lambda j, p: (0, j))] * n_ctx,
        ),
        out_shape=[shape(part, depth)] * n_ctx,
    )(place, *[out_grad] * n_ctx)
    mine = [mine[0]] + [swap(mine[k], "ctx", k) for k in range(1, n_ctx)]
    product = (key_in.astype(F32) * value_in.astype(F32)).astype(BF16)
    rim = shift(product, 1)
    rate = lr_rate.reshape(-1, 1)
    residue = lr_residue.reshape(-1, 1)
    counts = jnp.arange(rows, dtype=F32)[None, :]
    ends_coef = jnp.exp(-rate * (rows - 1 - counts)).astype(BF16)
    starts_coef = jnp.exp(-rate * counts).astype(BF16)
    away = jnp.arange((n_ctx - 1) * rows, dtype=F32)[:, None]
    inside = away % rows
    carry_coef = (residue.T * jnp.exp(-rate.T * (away + 1))).astype(BF16)
    back_coef = (residue.T * jnp.exp(-rate.T * (away + rows - 2 * inside))).astype(BF16)
    kernel = jnp.sum(
        lr_residue[:, :, None] * jnp.exp(-lr_rate[:, :, None] * counts[:, None, :]), axis=1
    )

    def reversed_row(values):
        return jnp.roll(values[:, ::-1], 1, axis=1)

    taps = reversed_row(mr_filter.astype(F32))
    kernel_rev = reversed_row(kernel)
    def local(transposed, table, x, *after):
        return call(
            functools.partial(local_body, transposed),
            "local_t" if transposed else "local",
            2 * rows * 128 * width * 8, rows * width * 6,
            grid=(steps,),
            in_specs=[tall(block // GROUP, rows), wide(rows, block)] + [ANY] * len(after),
            out_specs=wide(rows, block),
            out_shape=shape(rows, width, dtype=F32),
        )(table, x, *after)

    conv_own = local(
        False, taps, product, ends_coef, starts_coef, carry_coef, back_coef, kernel_rev, kernel
    )
    conv, mixed, ends = call(
        conv_body, "conv", 2 * rows * 128 * width * 8, rows * width * 14,
        grid=(steps,),
        in_specs=[wide(rows, block)] * 3 + [tall(block // GROUP, TAPS), tall(block, rows)],
        out_specs=[wide(rows, block), wide(rows, block), wide(ORDER, block)],
        out_shape=[shape(rows, width), shape(rows, width), shape(ORDER, width)],
    )(rim, conv_own, query, taps, ends_coef)
    ends_far = [shift(ends, k) for k in range(1, n_ctx)]


    local_fwd = local(False, kernel_rev, mixed)
    mine = call(
        join_body, "join", 0, 4 * part * depth * n_ctx,
        grid=(n_dp,),
        in_specs=[wide(part, feats)] * n_ctx + [ANY] * 2,
        out_specs=deep(n_ctx, part, feats),
        out_shape=shape(n_ctx, part, depth),
    )(*mine, weights, local_fwd)
    grad = lax.all_gather(mine, ("dp", "tp"), axis=0, tiled=False)
    grad = grad.reshape(n_dp, n_tp, n_ctx, part, depth)
    long_out, gated = call(
        functools.partial(long_body, n_ctx - 1), "long", 2 * rows * 128 * width, rows * width * 10,
        grid=(steps,),
        in_specs=[wide(rows, block), wide((n_ctx - 1) * rows, block), wide(rows, block)] + [wide(ORDER, block)] * (n_ctx - 1) + [ANY],
        out_specs=[wide(rows, block), pl.BlockSpec((1, rows, block), lambda i: (i, 0, 0))],
        out_shape=[shape(rows, width), shape(n_dp, rows, quarter)],
    )(local_fwd, carry_coef, gate, *ends_far, mine)
    gated_far = lax.all_to_all(gated, "dp", 0, 0, tiled=True)
    tokens = n_ctx * n_dp * rows
    last = n_ctx - 1
    from_left, from_right = [], []
    right = left = gated_far
    for t in range(last):
        right = shift(right, 1, range(t, last))
        left = shift(left, -1, range(1, n_ctx - t))
        from_left.append(right)
        from_right.append(left)

    first_dest = jnp.where(place[1] < n_ctx // 2, last, 0)
    chunk = (1, n_dp, rows, quarter)

    def project(dests, *after):
        count = dests.shape[0]
        whole = count > 1
        return call(
            functools.partial(delta_body, whole), "delta",
            2 * max(count - 1, 1) * n_dp * rows * depth * quarter,
            2 * tokens * depth + 2 * depth * quarter + 2 * count * n_dp * rows * quarter,
            grid_spec=pltpu.PrefetchScalarGridSpec(
                num_scalar_prefetch=2, grid=(count,),
                in_specs=[
                    pl.BlockSpec(
                        (n_dp, n_tp, 1, part, depth), lambda i, p, q: (0, 0, p[1] ^ q[i], 0, 0)
                    ),
                    pl.BlockSpec((n_dp, quarter, feats), lambda i, p, q: (0, 0, 0)),
                ] + ([pl.BlockSpec(chunk, lambda i, p, q: (0, 0, 0, 0))] if whole
                     else [ANY] * len(after)),
                out_specs=pl.BlockSpec(
                    chunk, lambda i, p, q: (q[i] if whole else 0, 0, 0, 0)
                ),
            ),
            out_shape=shape(count, n_dp, rows, quarter),
        )(place, dests, grad, weights, *after)

    first = project(first_dest[None], from_left[0], from_right[0])
    others = (first_dest + 1 + jnp.arange(n_ctx, dtype=jnp.int32)) % n_ctx
    partial = project(others.astype(jnp.int32), first)
    grad_t = call(
        flip_body, "flip", 0, 4 * tokens * depth,
        grid_spec=pltpu.PrefetchScalarGridSpec(
            num_scalar_prefetch=1, grid=(n_ctx, n_dp),
            in_specs=[
                pl.BlockSpec(
                    (1, n_tp, 1, part, depth),
                    lambda i, j, p: (j, 0, p[1] ^ ((p[1] + n_ctx - i) % n_ctx), 0, 0),
                ),
                ANY,
            ],
            out_specs=pl.BlockSpec((depth, rows), lambda i, j, p: (0, i * n_dp + j)),
        ),
        out_shape=shape(depth, tokens),
    )(place, grad, partial)
    right, left = shift(first, 1, [0]), shift(first, -1, [last])

    def pick(ahead):
        return pl.BlockSpec(
            (1, 1, rows, quarter), lambda i, q: (q[ahead], i, 0, 0)
        )

    piece_of = pl.BlockSpec((1, 1, rows, quarter), lambda i, q: (0, i, 0, 0))
    for t in range(1, last):
        after = (from_left[t], from_right[t]) + ((grad_t,) if t == last - 1 else ())
        dests = jnp.clip(jnp.stack([last - t + place[1], t - last + place[1]]), 0, last)
        right, left = call(
            add_body, "add", 0, 12 * n_dp * rows * quarter,
            grid_spec=pltpu.PrefetchScalarGridSpec(
                num_scalar_prefetch=1, grid=(n_dp,),
                in_specs=[pick(0), pick(1), piece_of, piece_of] + [ANY] * len(after),
                out_specs=[piece_of] * 2,
            ),
            out_shape=[shape(*chunk)] * 2,
        )(dests, partial, partial, right, left, *after)
        token = right
        right = shift(right, 1, range(t + 1))
        left = shift(left, -1, range(last - t, n_ctx))
    delta = call(
        sum_body, "sum", 0, 8 * n_dp * rows * quarter,
        grid_spec=pltpu.PrefetchScalarGridSpec(
            num_scalar_prefetch=1, grid=(n_dp,),
            in_specs=[pick(0), piece_of, piece_of],
            out_specs=pl.BlockSpec((1, rows, quarter), lambda i, q: (i, 0, 0)),
        ),
        out_shape=shape(n_dp, rows, quarter),
    )(place[1:2], partial, right, left)
    delta_far = lax.all_to_all(delta, "dp", 0, 0, tiled=True)

    gated_all = call(
        merge_body, "merge", 0, 2 * (2 * n_ctx + last) * n_dp * rows * quarter,
        grid=(n_dp,),
        in_specs=[pl.BlockSpec((1, rows, quarter), lambda i: (i, 0, 0))] * (1 + 2 * last) + [ANY],
        out_specs=pl.BlockSpec((n_ctx, 1, rows, quarter), lambda i: (0, i, 0, 0)),
        out_shape=shape(n_ctx, n_dp, rows, quarter),
    )(gated_far, *from_left, *from_right[::-1], token).reshape(tokens, quarter)
    pieces = {}
    for k in list(range(n_dp - 1, -1, -1)):
        token = pieces[k] = call(
            weight_body, "weight", 2 * tokens * feats * quarter, 2 * tokens * (feats + quarter),
            grid_spec=pltpu.PrefetchScalarGridSpec(
                num_scalar_prefetch=1, grid=(2,),
                in_specs=[
                    pl.BlockSpec((feats, tokens), lambda i, p, k=k: (p[0] ^ k, 0)),
                    pl.BlockSpec((tokens, quarter // 2), lambda i, p: (0, i)),
                    ANY,
                ],
                out_specs=pl.BlockSpec((feats, quarter // 2), lambda i, p: (0, i)),
            ),
            out_shape=shape(feats, quarter),
        )(place, grad_t, gated_all, token)

    def hold(value, after):
        return call(
            wait_body, "hold", 0, 0,
            in_specs=[ANY] * 2, out_specs=ANY,
            out_shape=shape(*value.shape), input_output_aliases={0: 0},
        )(value, after)

    weight_far = [pieces[0]] + [
        swap(pieces[k] if k == n_dp - 1 else hold(pieces[k], delta_far), "dp", k)
        for k in range(1, n_dp)
    ]

    seed, starts, gate_grad = call(
        seed_body, "seed", 2 * rows * 128 * width, rows * width * 10,
        grid=(steps,),
        in_specs=[
            pl.BlockSpec((1, rows, block), lambda i: (i, 0, 0)),
            wide(rows, block), wide(rows, block), tall(block, rows),
        ],
        out_specs=[wide(rows, block), wide(ORDER, block), wide(rows, block)],
        out_shape=[shape(rows, width), shape(ORDER, width), shape(rows, width)],
    )(delta_far, gate, long_out, starts_coef)
    starts_far = [shift(starts, -k) for k in range(1, n_ctx)]
    local_bwd = local(True, kernel, seed)
    query_grad, conv_grad = call(
        functools.partial(back_body, n_ctx - 1), "back", 2 * rows * 128 * width, rows * width * 12,
        grid=(steps,),
        in_specs=[wide(rows, block), wide((n_ctx - 1) * rows, block)] + [wide(rows, block)] * 2
        + [wide(ORDER, block)] * (n_ctx - 1),
        out_specs=[wide(rows, block)] * 2,
        out_shape=[shape(rows, width)] * 2,
    )(local_bwd, back_coef, conv, query, *starts_far)

    cut = feats // n_dp
    weight_grad = call(
        lay_body, "lay", 0, 4 * feats * width,
        grid_spec=pltpu.PrefetchScalarGridSpec(
            num_scalar_prefetch=1, grid=(n_dp,),
            in_specs=[pl.BlockSpec((cut, quarter), lambda i, p: (i, 0))] * n_dp + [ANY],
            out_specs=pl.BlockSpec((cut, width), lambda i, p: (i, 0)),
        ),
        out_shape=shape(feats, width),
    )(place, *weight_far, query_grad)
    return query_grad, conv_grad, gate_grad, weight_grad


def solution(mesh):
    rows = P(("dp", "ctx"), "tp")
    return jax.shard_map(
        on_device,
        mesh=mesh,
        in_specs=(rows, rows, rows, rows, P(("dp", "ctx"), None), P("tp", ("dp", "ctx")),
                  P("tp", None), P("tp", None), P("tp", None)),
        out_specs=(rows, rows, rows, rows),
        check_vma=False,
    )
```

```python
import functools

import jax
import jax.numpy as jnp
from jax import lax
from jax.experimental import pallas as pl
from jax.experimental.pallas import tpu as pltpu
from jax.sharding import PartitionSpec as P

GROUP = 16
TAPS = 128
ORDER = 16
LANES = 128
PER_SLAB = LANES // GROUP
BF16 = jnp.bfloat16
F32 = jnp.float32
VMEM = 50 * 2**20
ANY = pl.BlockSpec(memory_space=pl.ANY)


def call(body, name, flops, nbytes, **kwargs):
    return pl.pallas_call(
        body,
        name=name,
        cost_estimate=pl.CostEstimate(flops=flops, bytes_accessed=nbytes, transcendentals=0),
        compiler_params=pltpu.CompilerParams(vmem_limit_bytes=VMEM),
        **kwargs,
    )


def circulants(rows_ref, base):
    out = []
    for j in range(PER_SLAB):
        row = rows_ref[base + j : base + j + 1, :]
        out.append(
            pltpu.roll(jnp.broadcast_to(row, (LANES, LANES)), 0, 1, stride=1, stride_axis=0)
        )
    return out


def lower_mask():
    t = lax.broadcasted_iota(jnp.int32, (LANES, LANES), 0)
    u = lax.broadcasted_iota(jnp.int32, (LANES, LANES), 1)
    return u <= t


def pick_groups(stacked, rows):
    lane_group = lax.broadcasted_iota(jnp.int32, (rows, LANES), 1) // GROUP
    out = stacked[:rows]
    for j in range(1, PER_SLAB):
        out = jnp.where(lane_group == j, stacked[j * rows : (j + 1) * rows], out)
    return out


def spread_groups(state):
    tiled = jnp.concatenate([state] * PER_SLAB, axis=0)
    row_group = lax.broadcasted_iota(jnp.int32, (LANES, LANES), 0) // ORDER
    lane_group = lax.broadcasted_iota(jnp.int32, (LANES, LANES), 1) // GROUP
    return jnp.where(row_group == lane_group, tiled, jnp.zeros_like(tiled))


def dot(a, b):
    return jnp.dot(a, b, preferred_element_type=F32)


def conv_body(rim, own_part, query, taps, ends_coef, *refs):
    conv, mixed, ends = refs[-3:]
    lower = lower_mask()
    for s in range(rim.shape[1] // LANES):
        cols = slice(s * LANES, (s + 1) * LANES)
        blocks = [
            jnp.where(lower, jnp.zeros_like(circ), circ).astype(BF16)
            for circ in circulants(taps, s * PER_SLAB)
        ]
        out = own_part[:, cols] + pick_groups(
            dot(jnp.concatenate(blocks, axis=0), rim[:, cols]), LANES
        )
        conv[:, cols] = out.astype(conv.dtype)
        mixed[:, cols] = (query[:, cols].astype(F32) * out).astype(BF16)
    for s in range(rim.shape[1] // LANES):
        cols = slice(s * LANES, (s + 1) * LANES)
        ends[:, cols] = pick_groups(
            dot(ends_coef[s * LANES : (s + 1) * LANES, :], mixed[:, cols]), ORDER
        ).astype(ends.dtype)


def local_body(transposed, rows, x, *refs):
    out = refs[-1]
    lower = lower_mask()
    keep = ~lower | (lax.broadcasted_iota(jnp.int32, (LANES, LANES), 0)
                     == lax.broadcasted_iota(jnp.int32, (LANES, LANES), 1)) if transposed else lower
    for s in range(x.shape[1] // LANES):
        cols = slice(s * LANES, (s + 1) * LANES)
        blocks = [
            jnp.where(keep, circ, jnp.zeros_like(circ)).astype(BF16)
            for circ in circulants(rows, s * PER_SLAB)
        ]
        out[:, cols] = pick_groups(
            dot(jnp.concatenate(blocks, axis=0), x[:, cols]), LANES
        ).astype(out.dtype)


def carried(states, coef, cols):
    wide_states = jnp.concatenate([spread_groups(ref[:, cols]) for ref in states], axis=0)
    count = len(states)
    rows = coef.shape[0] // count
    parts = [coef[k * rows : (k + 1) * rows, cols] for k in range(count)]
    return dot(jnp.concatenate(parts, axis=1), wide_states)


def long_body(count, local, coef, gate, *refs):
    states, (long_out, gated) = refs[:count], refs[-2:]
    for s in range(local.shape[1] // LANES):
        cols = slice(s * LANES, (s + 1) * LANES)
        out = local[:, cols].astype(F32) + carried(states, coef, cols)
        long_out[:, cols] = out.astype(long_out.dtype)
        gated[0, :, cols] = (gate[:, cols].astype(F32) * out).astype(BF16)


def seed_body(delta, gate, long_out, starts_coef, after, seed, starts, gate_grad):
    for s in range(gate.shape[1] // LANES):
        cols = slice(s * LANES, (s + 1) * LANES)
        out = delta[0, :, cols].astype(F32)
        seed[:, cols] = (out * gate[:, cols].astype(F32)).astype(BF16)
        gate_grad[:, cols] = (out * long_out[:, cols].astype(F32)).astype(BF16)
    for s in range(gate.shape[1] // LANES):
        cols = slice(s * LANES, (s + 1) * LANES)
        starts[:, cols] = pick_groups(
            dot(starts_coef[s * LANES : (s + 1) * LANES, :], seed[:, cols]), ORDER
        ).astype(starts.dtype)


def back_body(count, local, coef, conv, query, *refs):
    states, (query_grad, conv_grad) = refs[:count], refs[-2:]
    for s in range(local.shape[1] // LANES):
        cols = slice(s * LANES, (s + 1) * LANES)
        out = local[:, cols].astype(F32) + carried(states, coef, cols)
        query_grad[:, cols] = (out * conv[:, cols].astype(F32)).astype(BF16)
        conv_grad[:, cols] = (out * query[:, cols].astype(F32)).astype(BF16)


def pack_body(place, *refs):
    count = len(refs) // 2
    for source, target in zip(refs[:count], refs[-count:]):
        target[...] = source[...]


def join_body(*refs):
    out = refs[-1]
    for k in range(out.shape[0]):
        out[k] = refs[k][...]


def delta_body(whole, place, dest, grad, weights, *refs):
    depth, out = weights.shape[2], refs[-1]

    def multiply():
        total = None
        for k in range(weights.shape[0]):
            rows = grad[:, :, :, :, k * depth : (k + 1) * depth].reshape(-1, depth)
            term = lax.dot_general(
                rows, weights[k], (((1,), (1,)), ((), ())), preferred_element_type=F32
            )
            total = term if total is None else total + term
        out[...] = total.astype(BF16).reshape(out.shape)

    if not whole:
        return multiply()
    is_last = pl.program_id(0) == pl.num_programs(0) - 1
    pl.when(jnp.logical_not(is_last))(multiply)

    @pl.when(is_last)
    def _():
        out[...] = refs[0][...]


def flip_body(place, grad, after, out):
    out[...] = grad[...].reshape(-1, grad.shape[-1]).T


def lay_body(place, *refs):
    sources, out = refs[:-2], refs[-1]
    for k, source in enumerate(sources):
        lanes = source.shape[1]
        out[:, pl.ds(pl.multiple_of((place[0] ^ k) * lanes, lanes), lanes)] = source[...]


def wait_body(*refs):
    pass


def add_body(dests, partial_right, partial_left, right, left, *refs):
    out_right, out_left = refs[-2:]
    out_right[...] = (partial_right[...].astype(F32) + right[...].astype(F32)).astype(BF16)
    out_left[...] = (partial_left[...].astype(F32) + left[...].astype(F32)).astype(BF16)


def merge_body(own, *refs):
    out = refs[-1]
    count = out.shape[0] - 1
    out[0] = own[...]
    for k in range(count):
        out[k + 1] = refs[k][...] + refs[count + k][...]


def sum_body(dest, partial, right, left, after, out):
    total = partial[0].astype(F32) + right[0].astype(F32) + left[0].astype(F32)
    out[...] = total.astype(BF16)


def weight_body(place, grad_t, gated, after, out):
    out[...] = dot(grad_t[...], gated[...]).astype(out.dtype)


def wide(rows, lanes):
    return pl.BlockSpec((rows, lanes), lambda i: (0, i))


def tall(rows, cols):
    return pl.BlockSpec((rows, cols), lambda i: (i, 0))


def deep(count, rows, lanes):
    return pl.BlockSpec((count, rows, lanes), lambda i: (0, 0, i))


def shape(*dims, dtype=BF16):
    return jax.ShapeDtypeStruct(dims, dtype)


def on_device(query, key_in, value_in, gate, out_grad, proj_weight, mr_filter, lr_rate, lr_residue):
    rows, width = query.shape
    groups = width // GROUP
    n_dp, n_ctx, n_tp = (lax.axis_size(a) for a in ("dp", "ctx", "tp"))
    feats = proj_weight.shape[1]
    quarter = width // n_dp
    depth = n_dp * feats
    block = quarter
    steps = width // block
    part = rows // n_tp

    place = jnp.stack([lax.axis_index(a) for a in ("dp", "ctx", "tp")]).astype(jnp.int32)

    def swap(value, axis, k):
        return lax.ppermute(value, axis, [(i, i ^ k) for i in range(lax.axis_size(axis))])

    def shift(value, k, senders=None):
        ends = [(i, i + k) for i in senders or range(n_ctx) if 0 <= i + k < n_ctx]
        return lax.ppermute(value, "ctx", ends)

    def piece(k):
        return pl.BlockSpec((part, feats), lambda j, p: (p[2], j * n_ctx + (p[1] ^ k)))

    weights = lax.all_to_all(proj_weight.reshape(n_dp, quarter, feats), "dp", 0, 0, tiled=True)
    mine = call(
        pack_body, "pack", 0, 4 * part * depth * n_ctx,
        grid_spec=pltpu.PrefetchScalarGridSpec(
            num_scalar_prefetch=1, grid=(n_dp,),
            in_specs=[piece(k) for k in range(n_ctx)],
            out_specs=[pl.BlockSpec((part, feats), lambda j, p: (0, j))] * n_ctx,
        ),
        out_shape=[shape(part, depth)] * n_ctx,
    )(place, *[out_grad] * n_ctx)
    mine = [mine[0]] + [swap(mine[k], "ctx", k) for k in range(1, n_ctx)]
    product = (key_in.astype(F32) * value_in.astype(F32)).astype(BF16)
    rim = shift(product, 1)
    rate = lr_rate.reshape(-1, 1)
    residue = lr_residue.reshape(-1, 1)
    counts = jnp.arange(rows, dtype=F32)[None, :]
    ends_coef = jnp.exp(-rate * (rows - 1 - counts)).astype(BF16)
    starts_coef = jnp.exp(-rate * counts).astype(BF16)
    away = jnp.arange((n_ctx - 1) * rows, dtype=F32)[:, None]
    inside = away % rows
    carry_coef = (residue.T * jnp.exp(-rate.T * (away + 1))).astype(BF16)
    back_coef = (residue.T * jnp.exp(-rate.T * (away + rows - 2 * inside))).astype(BF16)
    kernel = jnp.sum(
        lr_residue[:, :, None] * jnp.exp(-lr_rate[:, :, None] * counts[:, None, :]), axis=1
    )

    def reversed_row(values):
        return jnp.roll(values[:, ::-1], 1, axis=1)

    taps = reversed_row(mr_filter.astype(F32))
    kernel_rev = reversed_row(kernel)
    def local(transposed, table, x, *after):
        return call(
            functools.partial(local_body, transposed),
            "local_t" if transposed else "local",
            2 * rows * 128 * width * 8, rows * width * 6,
            grid=(steps,),
            in_specs=[tall(block // GROUP, rows), wide(rows, block)] + [ANY] * len(after),
            out_specs=wide(rows, block),
            out_shape=shape(rows, width, dtype=F32),
        )(table, x, *after)

    conv_own = local(
        False, taps, product, ends_coef, starts_coef, carry_coef, back_coef, kernel_rev, kernel
    )
    conv, mixed, ends = call(
        conv_body, "conv", 2 * rows * 128 * width * 8, rows * width * 14,
        grid=(steps,),
        in_specs=[wide(rows, block)] * 3 + [tall(block // GROUP, TAPS), tall(block, rows)],
        out_specs=[wide(rows, block), wide(rows, block), wide(ORDER, block)],
        out_shape=[shape(rows, width), shape(rows, width), shape(ORDER, width)],
    )(rim, conv_own, query, taps, ends_coef)
    ends_far = [shift(ends, k) for k in range(1, n_ctx)]


    local_fwd = local(False, kernel_rev, mixed)
    mine = call(
        join_body, "join", 0, 4 * part * depth * n_ctx,
        grid=(n_dp,),
        in_specs=[wide(part, feats)] * n_ctx + [ANY] * (n_ctx + 1),
        out_specs=deep(n_ctx, part, feats),
        out_shape=shape(n_ctx, part, depth),
    )(*mine, weights, local_fwd, *ends_far)
    grad = lax.all_gather(mine, ("dp", "tp"), axis=0, tiled=False)
    grad = grad.reshape(n_dp, n_tp, n_ctx, part, depth)
    long_out, gated = call(
        functools.partial(long_body, n_ctx - 1), "long", 2 * rows * 128 * width, rows * width * 10,
        grid=(steps,),
        in_specs=[wide(rows, block), wide((n_ctx - 1) * rows, block), wide(rows, block)] + [wide(ORDER, block)] * (n_ctx - 1) + [ANY],
        out_specs=[wide(rows, block), pl.BlockSpec((1, rows, block), lambda i: (i, 0, 0))],
        out_shape=[shape(rows, width), shape(n_dp, rows, quarter)],
    )(local_fwd, carry_coef, gate, *ends_far, mine)
    gated_far = lax.all_to_all(gated, "dp", 0, 0, tiled=True)
    tokens = n_ctx * n_dp * rows
    last = n_ctx - 1
    from_left, from_right = [], []
    right = left = gated_far
    for t in range(last):
        right = shift(right, 1, range(t, last))
        left = shift(left, -1, range(1, n_ctx - t))
        from_left.append(right)
        from_right.append(left)

    first_dest = jnp.where(place[1] < n_ctx // 2, last, 0)
    chunk = (1, n_dp, rows, quarter)

    def project(dests, *after):
        count = dests.shape[0]
        whole = count > 1
        return call(
            functools.partial(delta_body, whole), "delta",
            2 * max(count - 1, 1) * n_dp * rows * depth * quarter,
            2 * tokens * depth + 2 * depth * quarter + 2 * count * n_dp * rows * quarter,
            grid_spec=pltpu.PrefetchScalarGridSpec(
                num_scalar_prefetch=2, grid=(count,),
                in_specs=[
                    pl.BlockSpec(
                        (n_dp, n_tp, 1, part, depth), lambda i, p, q: (0, 0, p[1] ^ q[i], 0, 0)
                    ),
                    pl.BlockSpec((n_dp, quarter, feats), lambda i, p, q: (0, 0, 0)),
                ] + ([pl.BlockSpec(chunk, lambda i, p, q: (0, 0, 0, 0))] if whole
                     else [ANY] * len(after)),
                out_specs=pl.BlockSpec(
                    chunk, lambda i, p, q: (q[i] if whole else 0, 0, 0, 0)
                ),
            ),
            out_shape=shape(count, n_dp, rows, quarter),
        )(place, dests, grad, weights, *after)

    first = project(first_dest[None], from_left[0], from_right[0])
    others = (first_dest + 1 + jnp.arange(n_ctx, dtype=jnp.int32)) % n_ctx
    partial = project(others.astype(jnp.int32), first)
    grad_t = call(
        flip_body, "flip", 0, 4 * tokens * depth,
        grid_spec=pltpu.PrefetchScalarGridSpec(
            num_scalar_prefetch=1, grid=(n_ctx, n_dp),
            in_specs=[
                pl.BlockSpec(
                    (1, n_tp, 1, part, depth),
                    lambda i, j, p: (j, 0, p[1] ^ ((p[1] + n_ctx - i) % n_ctx), 0, 0),
                ),
                ANY,
            ],
            out_specs=pl.BlockSpec((depth, rows), lambda i, j, p: (0, i * n_dp + j)),
        ),
        out_shape=shape(depth, tokens),
    )(place, grad, partial)
    right, left = shift(first, 1, [0]), shift(first, -1, [last])

    def pick(ahead):
        return pl.BlockSpec(
            (1, 1, rows, quarter), lambda i, q: (q[ahead], i, 0, 0)
        )

    piece_of = pl.BlockSpec((1, 1, rows, quarter), lambda i, q: (0, i, 0, 0))
    for t in range(1, last):
        after = (from_left[t], from_right[t]) + ((grad_t,) if t == last - 1 else ())
        dests = jnp.clip(jnp.stack([last - t + place[1], t - last + place[1]]), 0, last)
        right, left = call(
            add_body, "add", 0, 12 * n_dp * rows * quarter,
            grid_spec=pltpu.PrefetchScalarGridSpec(
                num_scalar_prefetch=1, grid=(n_dp,),
                in_specs=[pick(0), pick(1), piece_of, piece_of] + [ANY] * len(after),
                out_specs=[piece_of] * 2,
            ),
            out_shape=[shape(*chunk)] * 2,
        )(dests, partial, partial, right, left, *after)
        token = right
        right = shift(right, 1, range(t + 1))
        left = shift(left, -1, range(last - t, n_ctx))
    gated_all = call(
        merge_body, "merge", 0, 2 * (2 * n_ctx + last) * n_dp * rows * quarter,
        grid=(n_dp,),
        in_specs=[pl.BlockSpec((1, rows, quarter), lambda i: (i, 0, 0))] * (1 + 2 * last) + [ANY],
        out_specs=pl.BlockSpec((n_ctx, 1, rows, quarter), lambda i: (0, i, 0, 0)),
        out_shape=shape(n_ctx, n_dp, rows, quarter),
    )(gated_far, *from_left, *from_right[::-1], token).reshape(tokens, quarter)
    pieces = {}
    for k in list(range(n_dp - 1, -1, -1)):
        token = pieces[k] = call(
            weight_body, "weight", 2 * tokens * feats * quarter, 2 * tokens * (feats + quarter),
            grid_spec=pltpu.PrefetchScalarGridSpec(
                num_scalar_prefetch=1, grid=(2,),
                in_specs=[
                    pl.BlockSpec((feats, tokens), lambda i, p, k=k: (p[0] ^ k, 0)),
                    pl.BlockSpec((tokens, quarter // 2), lambda i, p: (0, i)),
                    ANY,
                ],
                out_specs=pl.BlockSpec((feats, quarter // 2), lambda i, p: (0, i)),
            ),
            out_shape=shape(feats, quarter),
        )(place, grad_t, gated_all, token)

    delta = call(
        sum_body, "sum", 0, 8 * n_dp * rows * quarter,
        grid_spec=pltpu.PrefetchScalarGridSpec(
            num_scalar_prefetch=1, grid=(n_dp,),
            in_specs=[pick(0), piece_of, piece_of, ANY],
            out_specs=pl.BlockSpec((1, rows, quarter), lambda i, q: (i, 0, 0)),
        ),
        out_shape=shape(n_dp, rows, quarter),
    )(place[1:2], partial, right, left, pieces[n_dp // 2])
    delta_far = lax.all_to_all(delta, "dp", 0, 0, tiled=True)

    def hold(value, after):
        return call(
            wait_body, "hold", 0, 0,
            in_specs=[ANY] * 2, out_specs=ANY,
            out_shape=shape(*value.shape), input_output_aliases={0: 0},
        )(value, after)

    weight_far = [pieces[0]] + [
        swap(pieces[k] if k == n_dp - 1 else hold(pieces[k], delta_far), "dp", k)
        for k in range(1, n_dp)
    ]

    seed, starts, gate_grad = call(
        seed_body, "seed", 2 * rows * 128 * width, rows * width * 10,
        grid=(steps,),
        in_specs=[
            pl.BlockSpec((1, rows, block), lambda i: (i, 0, 0)),
            wide(rows, block), wide(rows, block), tall(block, rows), ANY,
        ],
        out_specs=[wide(rows, block), wide(ORDER, block), wide(rows, block)],
        out_shape=[shape(rows, width), shape(ORDER, width), shape(rows, width)],
    )(delta_far, gate, long_out, starts_coef, weight_far[-1])
    starts_far = [shift(starts, -k) for k in range(1, n_ctx)]
    local_bwd = local(True, kernel, seed)
    query_grad, conv_grad = call(
        functools.partial(back_body, n_ctx - 1), "back", 2 * rows * 128 * width, rows * width * 12,
        grid=(steps,),
        in_specs=[wide(rows, block), wide((n_ctx - 1) * rows, block)] + [wide(rows, block)] * 2
        + [wide(ORDER, block)] * (n_ctx - 1),
        out_specs=[wide(rows, block)] * 2,
        out_shape=[shape(rows, width)] * 2,
    )(local_bwd, back_coef, conv, query, *starts_far)

    cut = feats // n_dp
    weight_grad = call(
        lay_body, "lay", 0, 4 * feats * width,
        grid_spec=pltpu.PrefetchScalarGridSpec(
            num_scalar_prefetch=1, grid=(n_dp,),
            in_specs=[pl.BlockSpec((cut, quarter), lambda i, p: (i, 0))] * n_dp + [ANY],
            out_specs=pl.BlockSpec((cut, width), lambda i, p: (i, 0)),
        ),
        out_shape=shape(feats, width),
    )(place, *weight_far, query_grad)
    return query_grad, conv_grad, gate_grad, weight_grad


def solution(mesh):
    rows = P(("dp", "ctx"), "tp")
    return jax.shard_map(
        on_device,
        mesh=mesh,
        in_specs=(rows, rows, rows, rows, P(("dp", "ctx"), None), P("tp", ("dp", "ctx")),
                  P("tp", None), P("tp", None), P("tp", None)),
        out_specs=(rows, rows, rows, rows),
        check_vma=False,
    )
```

```python
import functools

import jax
import jax.numpy as jnp
from jax import lax
from jax.experimental import pallas as pl
from jax.experimental.pallas import tpu as pltpu
from jax.sharding import PartitionSpec as P

GROUP = 16
TAPS = 128
ORDER = 16
LANES = 128
PER_SLAB = LANES // GROUP
BF16 = jnp.bfloat16
F32 = jnp.float32
VMEM = 50 * 2**20
ANY = pl.BlockSpec(memory_space=pl.ANY)


def call(body, name, flops, nbytes, **kwargs):
    return pl.pallas_call(
        body,
        name=name,
        cost_estimate=pl.CostEstimate(flops=flops, bytes_accessed=nbytes, transcendentals=0),
        compiler_params=pltpu.CompilerParams(vmem_limit_bytes=VMEM),
        **kwargs,
    )


def circulants(rows_ref, base):
    out = []
    for j in range(PER_SLAB):
        row = rows_ref[base + j : base + j + 1, :]
        out.append(
            pltpu.roll(jnp.broadcast_to(row, (LANES, LANES)), 0, 1, stride=1, stride_axis=0)
        )
    return out


def lower_mask():
    t = lax.broadcasted_iota(jnp.int32, (LANES, LANES), 0)
    u = lax.broadcasted_iota(jnp.int32, (LANES, LANES), 1)
    return u <= t


def pick_groups(stacked, rows):
    lane_group = lax.broadcasted_iota(jnp.int32, (rows, LANES), 1) // GROUP
    out = stacked[:rows]
    for j in range(1, PER_SLAB):
        out = jnp.where(lane_group == j, stacked[j * rows : (j + 1) * rows], out)
    return out


def spread_groups(state):
    tiled = jnp.concatenate([state] * PER_SLAB, axis=0)
    row_group = lax.broadcasted_iota(jnp.int32, (LANES, LANES), 0) // ORDER
    lane_group = lax.broadcasted_iota(jnp.int32, (LANES, LANES), 1) // GROUP
    return jnp.where(row_group == lane_group, tiled, jnp.zeros_like(tiled))


def dot(a, b):
    return jnp.dot(a, b, preferred_element_type=F32)


def conv_body(rim, own_part, query, taps, ends_coef, *refs):
    conv, mixed, ends = refs[-3:]
    lower = lower_mask()
    for s in range(rim.shape[1] // LANES):
        cols = slice(s * LANES, (s + 1) * LANES)
        blocks = [
            jnp.where(lower, jnp.zeros_like(circ), circ).astype(BF16)
            for circ in circulants(taps, s * PER_SLAB)
        ]
        out = own_part[:, cols] + pick_groups(
            dot(jnp.concatenate(blocks, axis=0), rim[:, cols]), LANES
        )
        conv[:, cols] = out.astype(conv.dtype)
        mixed[:, cols] = (query[:, cols].astype(F32) * out).astype(BF16)
    for s in range(rim.shape[1] // LANES):
        cols = slice(s * LANES, (s + 1) * LANES)
        ends[:, cols] = pick_groups(
            dot(ends_coef[s * LANES : (s + 1) * LANES, :], mixed[:, cols]), ORDER
        ).astype(ends.dtype)


def local_body(transposed, rows, x, *refs):
    out = refs[-1]
    lower = lower_mask()
    keep = ~lower | (lax.broadcasted_iota(jnp.int32, (LANES, LANES), 0)
                     == lax.broadcasted_iota(jnp.int32, (LANES, LANES), 1)) if transposed else lower
    for s in range(x.shape[1] // LANES):
        cols = slice(s * LANES, (s + 1) * LANES)
        blocks = [
            jnp.where(keep, circ, jnp.zeros_like(circ)).astype(BF16)
            for circ in circulants(rows, s * PER_SLAB)
        ]
        out[:, cols] = pick_groups(
            dot(jnp.concatenate(blocks, axis=0), x[:, cols]), LANES
        ).astype(out.dtype)


def carried(states, coef, cols):
    wide_states = jnp.concatenate([spread_groups(ref[:, cols]) for ref in states], axis=0)
    count = len(states)
    rows = coef.shape[0] // count
    parts = [coef[k * rows : (k + 1) * rows, cols] for k in range(count)]
    return dot(jnp.concatenate(parts, axis=1), wide_states)


def long_body(count, local, coef, gate, *refs):
    states, (long_out, gated) = refs[:count], refs[-2:]
    for s in range(local.shape[1] // LANES):
        cols = slice(s * LANES, (s + 1) * LANES)
        out = local[:, cols].astype(F32) + carried(states, coef, cols)
        long_out[:, cols] = out.astype(long_out.dtype)
        gated[0, :, cols] = (gate[:, cols].astype(F32) * out).astype(BF16)


def seed_body(delta, gate, long_out, starts_coef, after, seed, starts, gate_grad):
    for s in range(gate.shape[1] // LANES):
        cols = slice(s * LANES, (s + 1) * LANES)
        out = delta[0, :, cols].astype(F32)
        seed[:, cols] = (out * gate[:, cols].astype(F32)).astype(BF16)
        gate_grad[:, cols] = (out * long_out[:, cols].astype(F32)).astype(BF16)
    for s in range(gate.shape[1] // LANES):
        cols = slice(s * LANES, (s + 1) * LANES)
        starts[:, cols] = pick_groups(
            dot(starts_coef[s * LANES : (s + 1) * LANES, :], seed[:, cols]), ORDER
        ).astype(starts.dtype)


def back_body(count, local, coef, conv, query, *refs):
    states, (query_grad, conv_grad) = refs[:count], refs[-2:]
    for s in range(local.shape[1] // LANES):
        cols = slice(s * LANES, (s + 1) * LANES)
        out = local[:, cols].astype(F32) + carried(states, coef, cols)
        query_grad[:, cols] = (out * conv[:, cols].astype(F32)).astype(BF16)
        conv_grad[:, cols] = (out * query[:, cols].astype(F32)).astype(BF16)


def pack_body(place, *refs):
    count = len(refs) // 2
    for source, target in zip(refs[:count], refs[count + 1 :]):
        target[...] = source[...]


def join_body(*refs):
    out = refs[-1]
    for k in range(out.shape[0]):
        out[k] = refs[k][...]


def delta_body(computed, grad, weights, *refs):
    depth, out = weights.shape[2], refs[-1]

    def multiply():
        total = None
        for k in range(weights.shape[0]):
            rows = grad[:, :, :, :, k * depth : (k + 1) * depth].reshape(-1, depth)
            term = lax.dot_general(
                rows, weights[k], (((1,), (1,)), ((), ())), preferred_element_type=F32
            )
            total = term if total is None else total + term
        out[...] = total.astype(BF16).reshape(out.shape)

    if computed is None:
        return multiply()
    pl.when(pl.program_id(0) < computed)(multiply)

    @pl.when(pl.program_id(0) >= computed)
    def _():
        out[...] = refs[0][...]


def flip_body(place_of, side, place, far, near, after, out):
    is_far = place_of(pl.program_id(0), place) >= side

    @pl.when(is_far)
    def _():
        out[...] = far[...].reshape(-1, far.shape[-1]).T

    @pl.when(jnp.logical_not(is_far))
    def _():
        out[...] = near[...].reshape(-1, near.shape[-1]).T


def lay_body(place, *refs):
    sources, out = refs[:-2], refs[-1]
    for k, source in enumerate(sources):
        lanes = source.shape[1]
        out[:, pl.ds(pl.multiple_of((place[0] ^ k) * lanes, lanes), lanes)] = source[...]


def wait_body(*refs):
    pass


def add_body(dests, partial_right, partial_left, right, left, *refs):
    out_right, out_left = refs[-2:]
    out_right[...] = (partial_right[...].astype(F32) + right[...].astype(F32)).astype(BF16)
    out_left[...] = (partial_left[...].astype(F32) + left[...].astype(F32)).astype(BF16)


def merge_body(own, *refs):
    out = refs[-1]
    count = out.shape[0] - 1
    out[0] = own[...]
    for k in range(count):
        out[k + 1] = refs[k][...] + refs[count + k][...]


def sum_body(dest, partial, right, left, after, out):
    total = partial[0].astype(F32) + right[0].astype(F32) + left[0].astype(F32)
    out[...] = total.astype(BF16)


def weight_body(place, grad_t, gated, after, out):
    out[...] = dot(grad_t[...], gated[...]).astype(out.dtype)


def wide(rows, lanes):
    return pl.BlockSpec((rows, lanes), lambda i: (0, i))


def tall(rows, cols):
    return pl.BlockSpec((rows, cols), lambda i: (i, 0))


def deep(count, rows, lanes):
    return pl.BlockSpec((count, rows, lanes), lambda i: (0, 0, i))


def shape(*dims, dtype=BF16):
    return jax.ShapeDtypeStruct(dims, dtype)


def on_device(query, key_in, value_in, gate, out_grad, proj_weight, mr_filter, lr_rate, lr_residue):
    rows, width = query.shape
    groups = width // GROUP
    n_dp, n_ctx, n_tp = (lax.axis_size(a) for a in ("dp", "ctx", "tp"))
    feats = proj_weight.shape[1]
    quarter = width // n_dp
    depth = n_dp * feats
    block = quarter
    steps = width // block
    part = rows // n_tp

    place = jnp.stack([lax.axis_index(a) for a in ("dp", "ctx", "tp")]).astype(jnp.int32)

    def swap(value, axis, k):
        return lax.ppermute(value, axis, [(i, i ^ k) for i in range(lax.axis_size(axis))])

    def shift(value, k, senders=None):
        ends = [(i, i + k) for i in senders or range(n_ctx) if 0 <= i + k < n_ctx]
        return lax.ppermute(value, "ctx", ends)

    def piece(k):
        return pl.BlockSpec((part, feats), lambda j, p: (p[2], j * n_ctx + (p[1] ^ k)))

    weights = lax.all_to_all(proj_weight.reshape(n_dp, quarter, feats), "dp", 0, 0, tiled=True)
    product = (key_in.astype(F32) * value_in.astype(F32)).astype(BF16)
    rim = shift(product, 1)
    mine = call(
        pack_body, "pack", 0, 4 * part * depth * n_ctx,
        grid_spec=pltpu.PrefetchScalarGridSpec(
            num_scalar_prefetch=1, grid=(n_dp,),
            in_specs=[piece(k) for k in range(n_ctx)] + [ANY],
            out_specs=[pl.BlockSpec((part, feats), lambda j, p: (0, j))] * n_ctx,
        ),
        out_shape=[shape(part, depth)] * n_ctx,
    )(place, *[out_grad] * n_ctx, rim)
    mine = [mine[0]] + [swap(mine[k], "ctx", k) for k in range(1, n_ctx)]

    rate = lr_rate.reshape(-1, 1)
    residue = lr_residue.reshape(-1, 1)
    counts = jnp.arange(rows, dtype=F32)[None, :]
    ends_coef = jnp.exp(-rate * (rows - 1 - counts)).astype(BF16)
    starts_coef = jnp.exp(-rate * counts).astype(BF16)
    away = jnp.arange((n_ctx - 1) * rows, dtype=F32)[:, None]
    inside = away % rows
    carry_coef = (residue.T * jnp.exp(-rate.T * (away + 1))).astype(BF16)
    back_coef = (residue.T * jnp.exp(-rate.T * (away + rows - 2 * inside))).astype(BF16)
    kernel = jnp.sum(
        lr_residue[:, :, None] * jnp.exp(-lr_rate[:, :, None] * counts[:, None, :]), axis=1
    )

    def reversed_row(values):
        return jnp.roll(values[:, ::-1], 1, axis=1)

    taps = reversed_row(mr_filter.astype(F32))
    kernel_rev = reversed_row(kernel)
    def local(transposed, table, x, *after):
        return call(
            functools.partial(local_body, transposed),
            "local_t" if transposed else "local",
            2 * rows * 128 * width * 8, rows * width * 6,
            grid=(steps,),
            in_specs=[tall(block // GROUP, rows), wide(rows, block)] + [ANY] * len(after),
            out_specs=wide(rows, block),
            out_shape=shape(rows, width, dtype=F32),
        )(table, x, *after)

    conv_own = local(
        False, taps, product, ends_coef, starts_coef, carry_coef, back_coef, kernel_rev, kernel
    )
    conv, mixed, ends = call(
        conv_body, "conv", 2 * rows * 128 * width * 8, rows * width * 14,
        grid=(steps,),
        in_specs=[wide(rows, block)] * 3 + [tall(block // GROUP, TAPS), tall(block, rows)],
        out_specs=[wide(rows, block), wide(rows, block), wide(ORDER, block)],
        out_shape=[shape(rows, width), shape(rows, width), shape(ORDER, width)],
    )(rim, conv_own, query, taps, ends_coef)
    ends_far = [shift(ends, k) for k in range(1, n_ctx)]


    local_fwd = local(False, kernel_rev, mixed)
    side = n_ctx // 2

    def join(pieces, *after):
        return call(
            join_body, "join", 0, 4 * part * depth * side,
            grid=(n_dp,),
            in_specs=[wide(part, feats)] * side + [ANY] * len(after),
            out_specs=deep(side, part, feats),
            out_shape=shape(side, part, depth),
        )(*pieces, *after)

    def gather(value):
        value = lax.all_gather(value, ("dp", "tp"), axis=0, tiled=False)
        return value.reshape(n_dp, n_tp, side, part, depth)

    far = join(mine[side:], weights, local_fwd, *ends_far, *mine[1:side])
    near = join(mine[:side], far)
    grad_far, grad_near = gather(far), gather(near)
    long_out, gated = call(
        functools.partial(long_body, n_ctx - 1), "long", 2 * rows * 128 * width, rows * width * 10,
        grid=(steps,),
        in_specs=[wide(rows, block), wide((n_ctx - 1) * rows, block), wide(rows, block)] + [wide(ORDER, block)] * (n_ctx - 1) + [ANY] * 2,
        out_specs=[wide(rows, block), pl.BlockSpec((1, rows, block), lambda i: (i, 0, 0))],
        out_shape=[shape(rows, width), shape(n_dp, rows, quarter)],
    )(local_fwd, carry_coef, gate, *ends_far, far, near)
    gated_far = lax.all_to_all(gated, "dp", 0, 0, tiled=True)
    tokens = n_ctx * n_dp * rows
    last = n_ctx - 1
    from_left, from_right = [], []
    right = left = gated_far
    for t in range(last):
        right = shift(right, 1, range(t, last))
        left = shift(left, -1, range(1, n_ctx - t))
        from_left.append(right)
        from_right.append(left)

    chunk = (1, n_dp, rows, quarter)
    grad_block = (n_dp, n_tp, 1, part, depth)
    all_weights = pl.BlockSpec((n_dp, quarter, feats), lambda i: (0, 0, 0))
    far_part = call(
        functools.partial(delta_body, None), "delta", tokens * depth * quarter,
        tokens * depth + 2 * depth * quarter + tokens * quarter,
        grid=(side,),
        in_specs=[pl.BlockSpec(grad_block, lambda i: (0, 0, i, 0, 0)), all_weights, ANY, ANY],
        out_specs=pl.BlockSpec(chunk, lambda i: (i, 0, 0, 0)),
        out_shape=shape(side, n_dp, rows, quarter),
    )(grad_far, weights, from_left[0], from_right[0])
    partial = call(
        functools.partial(delta_body, side), "delta", tokens * depth * quarter,
        tokens * depth + 2 * depth * quarter + 3 * tokens * quarter,
        grid=(n_ctx,),
        in_specs=[
            pl.BlockSpec(grad_block, lambda i: (0, 0, jnp.minimum(i, side - 1), 0, 0)),
            all_weights,
            pl.BlockSpec(chunk, lambda i: (jnp.maximum(i - side, 0), 0, 0, 0)),
        ],
        out_specs=pl.BlockSpec(chunk, lambda i: (i, 0, 0, 0)),
        out_shape=shape(n_ctx, n_dp, rows, quarter),
    )(grad_near, weights, far_part)
    def place_of(i, p):
        return p[1] ^ ((p[1] + n_ctx - i) % n_ctx)

    grad_t = call(
        functools.partial(flip_body, place_of, side), "flip", 0, 6 * tokens * depth,
        grid_spec=pltpu.PrefetchScalarGridSpec(
            num_scalar_prefetch=1, grid=(n_ctx, n_dp),
            in_specs=[
                pl.BlockSpec(
                    (1, n_tp, 1, part, depth),
                    lambda i, j, p: (j, 0, jnp.maximum(place_of(i, p) - side, 0), 0, 0),
                ),
                pl.BlockSpec(
                    (1, n_tp, 1, part, depth),
                    lambda i, j, p: (j, 0, jnp.minimum(place_of(i, p), side - 1), 0, 0),
                ),
                ANY,
            ],
            out_specs=pl.BlockSpec((depth, rows), lambda i, j, p: (0, i * n_dp + j)),
        ),
        out_shape=shape(depth, tokens),
    )(place, grad_far, grad_near, partial)
    own = place[1]
    start = jnp.where(own < side, own ^ last, own) - side
    first = lax.dynamic_slice_in_dim(far_part, start, 1)
    right, left = shift(first, 1, [0]), shift(first, -1, [last])

    def pick(ahead):
        return pl.BlockSpec(
            (1, 1, rows, quarter), lambda i, q: (q[ahead], i, 0, 0)
        )

    piece_of = pl.BlockSpec((1, 1, rows, quarter), lambda i, q: (0, i, 0, 0))
    for t in range(1, last):
        after = (from_left[t], from_right[t]) + ((grad_t,) if t == last - 1 else ())
        dests = jnp.clip(jnp.stack([last - t + own, t - last + own]), 0, last) ^ own
        if t < side:
            table, dests = far_part, jnp.maximum(dests - side, 0)
        else:
            table = partial
        right, left = call(
            add_body, "add", 0, 12 * n_dp * rows * quarter,
            grid_spec=pltpu.PrefetchScalarGridSpec(
                num_scalar_prefetch=1, grid=(n_dp,),
                in_specs=[pick(0), pick(1), piece_of, piece_of] + [ANY] * len(after),
                out_specs=[piece_of] * 2,
            ),
            out_shape=[shape(*chunk)] * 2,
        )(dests, table, table, right, left, *after)
        token = right
        right = shift(right, 1, range(t + 1))
        left = shift(left, -1, range(last - t, n_ctx))
    gated_all = call(
        merge_body, "merge", 0, 2 * (2 * n_ctx + last) * n_dp * rows * quarter,
        grid=(n_dp,),
        in_specs=[pl.BlockSpec((1, rows, quarter), lambda i: (i, 0, 0))] * (1 + 2 * last) + [ANY],
        out_specs=pl.BlockSpec((n_ctx, 1, rows, quarter), lambda i: (0, i, 0, 0)),
        out_shape=shape(n_ctx, n_dp, rows, quarter),
    )(gated_far, *from_left, *from_right[::-1], token).reshape(tokens, quarter)
    pieces = {}
    for k in list(range(n_dp - 1, -1, -1)):
        token = pieces[k] = call(
            weight_body, "weight", 2 * tokens * feats * quarter, 2 * tokens * (feats + quarter),
            grid_spec=pltpu.PrefetchScalarGridSpec(
                num_scalar_prefetch=1, grid=(2,),
                in_specs=[
                    pl.BlockSpec((feats, tokens), lambda i, p, k=k: (p[0] ^ k, 0)),
                    pl.BlockSpec((tokens, quarter // 2), lambda i, p: (0, i)),
                    ANY,
                ],
                out_specs=pl.BlockSpec((feats, quarter // 2), lambda i, p: (0, i)),
            ),
            out_shape=shape(feats, quarter),
        )(place, grad_t, gated_all, token)

    delta = call(
        sum_body, "sum", 0, 8 * n_dp * rows * quarter,
        grid_spec=pltpu.PrefetchScalarGridSpec(
            num_scalar_prefetch=1, grid=(n_dp,),
            in_specs=[pick(0), piece_of, piece_of, ANY],
            out_specs=pl.BlockSpec((1, rows, quarter), lambda i, q: (i, 0, 0)),
        ),
        out_shape=shape(n_dp, rows, quarter),
    )(own[None] * 0, partial, right, left, pieces[n_dp // 2])
    delta_far = lax.all_to_all(delta, "dp", 0, 0, tiled=True)

    def hold(value, after):
        return call(
            wait_body, "hold", 0, 0,
            in_specs=[ANY] * 2, out_specs=ANY,
            out_shape=shape(*value.shape), input_output_aliases={0: 0},
        )(value, after)

    weight_far = [pieces[0]] + [
        swap(pieces[k] if k == n_dp - 1 else hold(pieces[k], delta_far), "dp", k)
        for k in range(1, n_dp)
    ]

    seed, starts, gate_grad = call(
        seed_body, "seed", 2 * rows * 128 * width, rows * width * 10,
        grid=(steps,),
        in_specs=[
            pl.BlockSpec((1, rows, block), lambda i: (i, 0, 0)),
            wide(rows, block), wide(rows, block), tall(block, rows), ANY,
        ],
        out_specs=[wide(rows, block), wide(ORDER, block), wide(rows, block)],
        out_shape=[shape(rows, width), shape(ORDER, width), shape(rows, width)],
    )(delta_far, gate, long_out, starts_coef, delta)
    starts_far = [shift(starts, -k) for k in range(1, n_ctx)]
    local_bwd = local(True, kernel, seed)
    query_grad, conv_grad = call(
        functools.partial(back_body, n_ctx - 1), "back", 2 * rows * 128 * width, rows * width * 12,
        grid=(steps,),
        in_specs=[wide(rows, block), wide((n_ctx - 1) * rows, block)] + [wide(rows, block)] * 2
        + [wide(ORDER, block)] * (n_ctx - 1),
        out_specs=[wide(rows, block)] * 2,
        out_shape=[shape(rows, width)] * 2,
    )(local_bwd, back_coef, conv, query, *starts_far)

    cut = feats // n_dp
    weight_grad = call(
        lay_body, "lay", 0, 4 * feats * width,
        grid_spec=pltpu.PrefetchScalarGridSpec(
            num_scalar_prefetch=1, grid=(n_dp,),
            in_specs=[pl.BlockSpec((cut, quarter), lambda i, p: (i, 0))] * n_dp + [ANY],
            out_specs=pl.BlockSpec((cut, width), lambda i, p: (i, 0)),
        ),
        out_shape=shape(feats, width),
    )(place, *weight_far, query_grad)
    return query_grad, conv_grad, gate_grad, weight_grad


def solution(mesh):
    rows = P(("dp", "ctx"), "tp")
    return jax.shard_map(
        on_device,
        mesh=mesh,
        in_specs=(rows, rows, rows, rows, P(("dp", "ctx"), None), P("tp", ("dp", "ctx")),
                  P("tp", None), P("tp", None), P("tp", None)),
        out_specs=(rows, rows, rows, rows),
        check_vma=False,
    )
```

```python
import functools

import jax
import jax.numpy as jnp
from jax import lax
from jax.experimental import pallas as pl
from jax.experimental.pallas import tpu as pltpu
from jax.sharding import PartitionSpec as P

GROUP = 16
TAPS = 128
ORDER = 16
LANES = 128
PER_SLAB = LANES // GROUP
BF16 = jnp.bfloat16
F32 = jnp.float32
VMEM = 50 * 2**20
ANY = pl.BlockSpec(memory_space=pl.ANY)


def call(body, name, flops, nbytes, **kwargs):
    return pl.pallas_call(
        body,
        name=name,
        cost_estimate=pl.CostEstimate(flops=flops, bytes_accessed=nbytes, transcendentals=0),
        compiler_params=pltpu.CompilerParams(vmem_limit_bytes=VMEM),
        **kwargs,
    )


def circulants(rows_ref, base):
    out = []
    for j in range(PER_SLAB):
        row = rows_ref[base + j : base + j + 1, :]
        out.append(
            pltpu.roll(jnp.broadcast_to(row, (LANES, LANES)), 0, 1, stride=1, stride_axis=0)
        )
    return out


def lower_mask():
    t = lax.broadcasted_iota(jnp.int32, (LANES, LANES), 0)
    u = lax.broadcasted_iota(jnp.int32, (LANES, LANES), 1)
    return u <= t


def pick_groups(stacked, rows):
    lane_group = lax.broadcasted_iota(jnp.int32, (rows, LANES), 1) // GROUP
    out = stacked[:rows]
    for j in range(1, PER_SLAB):
        out = jnp.where(lane_group == j, stacked[j * rows : (j + 1) * rows], out)
    return out


def spread_groups(state):
    tiled = jnp.concatenate([state] * PER_SLAB, axis=0)
    row_group = lax.broadcasted_iota(jnp.int32, (LANES, LANES), 0) // ORDER
    lane_group = lax.broadcasted_iota(jnp.int32, (LANES, LANES), 1) // GROUP
    return jnp.where(row_group == lane_group, tiled, jnp.zeros_like(tiled))


def dot(a, b):
    return jnp.dot(a, b, preferred_element_type=F32)


def conv_body(rim, own_part, query, taps, ends_coef, *refs):
    conv, mixed, ends = refs[-3:]
    lower = lower_mask()
    for s in range(rim.shape[1] // LANES):
        cols = slice(s * LANES, (s + 1) * LANES)
        blocks = [
            jnp.where(lower, jnp.zeros_like(circ), circ).astype(BF16)
            for circ in circulants(taps, s * PER_SLAB)
        ]
        out = own_part[:, cols] + pick_groups(
            dot(jnp.concatenate(blocks, axis=0), rim[:, cols]), LANES
        )
        conv[:, cols] = out.astype(conv.dtype)
        mixed[:, cols] = (query[:, cols].astype(F32) * out).astype(BF16)
    for s in range(rim.shape[1] // LANES):
        cols = slice(s * LANES, (s + 1) * LANES)
        ends[:, cols] = pick_groups(
            dot(ends_coef[s * LANES : (s + 1) * LANES, :], mixed[:, cols]), ORDER
        ).astype(ends.dtype)


def local_body(transposed, rows, x, *refs):
    out = refs[-1]
    lower = lower_mask()
    keep = ~lower | (lax.broadcasted_iota(jnp.int32, (LANES, LANES), 0)
                     == lax.broadcasted_iota(jnp.int32, (LANES, LANES), 1)) if transposed else lower
    for s in range(x.shape[1] // LANES):
        cols = slice(s * LANES, (s + 1) * LANES)
        blocks = [
            jnp.where(keep, circ, jnp.zeros_like(circ)).astype(BF16)
            for circ in circulants(rows, s * PER_SLAB)
        ]
        out[:, cols] = pick_groups(
            dot(jnp.concatenate(blocks, axis=0), x[:, cols]), LANES
        ).astype(out.dtype)


def carried(states, coef, cols):
    wide_states = jnp.concatenate([spread_groups(ref[:, cols]) for ref in states], axis=0)
    count = len(states)
    rows = coef.shape[0] // count
    parts = [coef[k * rows : (k + 1) * rows, cols] for k in range(count)]
    return dot(jnp.concatenate(parts, axis=1), wide_states)


def long_body(count, local, coef, gate, *refs):
    states, (long_out, gated) = refs[:count], refs[-2:]
    for s in range(local.shape[1] // LANES):
        cols = slice(s * LANES, (s + 1) * LANES)
        out = local[:, cols].astype(F32) + carried(states, coef, cols)
        long_out[:, cols] = out.astype(long_out.dtype)
        gated[0, :, cols] = (gate[:, cols].astype(F32) * out).astype(BF16)


def seed_body(delta, gate, long_out, starts_coef, after, seed, starts, gate_grad):
    for s in range(gate.shape[1] // LANES):
        cols = slice(s * LANES, (s + 1) * LANES)
        out = delta[0, :, cols].astype(F32)
        seed[:, cols] = (out * gate[:, cols].astype(F32)).astype(BF16)
        gate_grad[:, cols] = (out * long_out[:, cols].astype(F32)).astype(BF16)
    for s in range(gate.shape[1] // LANES):
        cols = slice(s * LANES, (s + 1) * LANES)
        starts[:, cols] = pick_groups(
            dot(starts_coef[s * LANES : (s + 1) * LANES, :], seed[:, cols]), ORDER
        ).astype(starts.dtype)


def back_body(count, local, coef, conv, query, *refs):
    states, (query_grad, conv_grad) = refs[:count], refs[-2:]
    for s in range(local.shape[1] // LANES):
        cols = slice(s * LANES, (s + 1) * LANES)
        out = local[:, cols].astype(F32) + carried(states, coef, cols)
        query_grad[:, cols] = (out * conv[:, cols].astype(F32)).astype(BF16)
        conv_grad[:, cols] = (out * query[:, cols].astype(F32)).astype(BF16)


def pack_body(count, place, *refs):
    for source, target in zip(refs[:count], refs[-count:]):
        target[...] = source[...]


def join_body(*refs):
    out = refs[-1]
    for k in range(out.shape[0]):
        out[k] = refs[k][...]


def delta_body(computed, grad, weights, *refs):
    depth, out = weights.shape[2], refs[-1]

    def multiply():
        total = None
        for k in range(weights.shape[0]):
            rows = grad[:, :, :, :, k * depth : (k + 1) * depth].reshape(-1, depth)
            term = lax.dot_general(
                rows, weights[k], (((1,), (1,)), ((), ())), preferred_element_type=F32
            )
            total = term if total is None else total + term
        out[...] = total.astype(BF16).reshape(out.shape)

    if computed is None:
        return multiply()
    pl.when(pl.program_id(0) < computed)(multiply)

    @pl.when(pl.program_id(0) >= computed)
    def _():
        out[...] = refs[0][...]


def flip_body(place_of, side, place, far, near, after, out):
    is_far = place_of(pl.program_id(0), place) >= side

    @pl.when(is_far)
    def _():
        out[...] = far[...].reshape(-1, far.shape[-1]).T

    @pl.when(jnp.logical_not(is_far))
    def _():
        out[...] = near[...].reshape(-1, near.shape[-1]).T


def lay_body(place, *refs):
    sources, out = refs[:-2], refs[-1]
    for k, source in enumerate(sources):
        lanes = source.shape[1]
        out[:, pl.ds(pl.multiple_of((place[0] ^ k) * lanes, lanes), lanes)] = source[...]


def wait_body(*refs):
    pass


def add_body(dests, partial_right, partial_left, right, left, *refs):
    out_right, out_left = refs[-2:]
    out_right[...] = (partial_right[...].astype(F32) + right[...].astype(F32)).astype(BF16)
    out_left[...] = (partial_left[...].astype(F32) + left[...].astype(F32)).astype(BF16)


def merge_body(own, *refs):
    out = refs[-1]
    count = out.shape[0] - 1
    out[0] = own[...]
    for k in range(count):
        out[k + 1] = refs[k][...] + refs[count + k][...]


def sum_body(dest, partial, right, left, after, out):
    total = partial[0].astype(F32) + right[0].astype(F32) + left[0].astype(F32)
    out[...] = total.astype(BF16)


def weight_body(place, grad_t, gated, after, out):
    out[...] = dot(grad_t[...], gated[...]).astype(out.dtype)


def wide(rows, lanes):
    return pl.BlockSpec((rows, lanes), lambda i: (0, i))


def tall(rows, cols):
    return pl.BlockSpec((rows, cols), lambda i: (i, 0))


def deep(count, rows, lanes):
    return pl.BlockSpec((count, rows, lanes), lambda i: (0, 0, i))


def shape(*dims, dtype=BF16):
    return jax.ShapeDtypeStruct(dims, dtype)


def on_device(query, key_in, value_in, gate, out_grad, proj_weight, mr_filter, lr_rate, lr_residue):
    rows, width = query.shape
    groups = width // GROUP
    n_dp, n_ctx, n_tp = (lax.axis_size(a) for a in ("dp", "ctx", "tp"))
    feats = proj_weight.shape[1]
    quarter = width // n_dp
    depth = n_dp * feats
    block = quarter
    steps = width // block
    part = rows // n_tp

    place = jnp.stack([lax.axis_index(a) for a in ("dp", "ctx", "tp")]).astype(jnp.int32)

    def swap(value, axis, k):
        return lax.ppermute(value, axis, [(i, i ^ k) for i in range(lax.axis_size(axis))])

    def shift(value, k, senders=None):
        ends = [(i, i + k) for i in senders or range(n_ctx) if 0 <= i + k < n_ctx]
        return lax.ppermute(value, "ctx", ends)

    def piece(k):
        return pl.BlockSpec((part, feats), lambda j, p: (p[2], j * n_ctx + (p[1] ^ k)))

    weights = lax.all_to_all(proj_weight.reshape(n_dp, quarter, feats), "dp", 0, 0, tiled=True)
    product = (key_in.astype(F32) * value_in.astype(F32)).astype(BF16)
    rim = shift(product, 1)

    rate = lr_rate.reshape(-1, 1)
    residue = lr_residue.reshape(-1, 1)
    counts = jnp.arange(rows, dtype=F32)[None, :]
    ends_coef = jnp.exp(-rate * (rows - 1 - counts)).astype(BF16)
    starts_coef = jnp.exp(-rate * counts).astype(BF16)
    away = jnp.arange((n_ctx - 1) * rows, dtype=F32)[:, None]
    inside = away % rows
    carry_coef = (residue.T * jnp.exp(-rate.T * (away + 1))).astype(BF16)
    back_coef = (residue.T * jnp.exp(-rate.T * (away + rows - 2 * inside))).astype(BF16)
    kernel = jnp.sum(
        lr_residue[:, :, None] * jnp.exp(-lr_rate[:, :, None] * counts[:, None, :]), axis=1
    )

    def reversed_row(values):
        return jnp.roll(values[:, ::-1], 1, axis=1)

    taps = reversed_row(mr_filter.astype(F32))
    kernel_rev = reversed_row(kernel)
    def local(transposed, table, x, *after):
        return call(
            functools.partial(local_body, transposed),
            "local_t" if transposed else "local",
            2 * rows * 128 * width * 8, rows * width * 6,
            grid=(steps,),
            in_specs=[tall(block // GROUP, rows), wide(rows, block)] + [ANY] * len(after),
            out_specs=wide(rows, block),
            out_shape=shape(rows, width, dtype=F32),
        )(table, x, *after)

    conv_own = local(
        False, taps, product, ends_coef, starts_coef, carry_coef, back_coef, kernel_rev, kernel
    )
    conv, mixed, ends = call(
        conv_body, "conv", 2 * rows * 128 * width * 8, rows * width * 14,
        grid=(steps,),
        in_specs=[wide(rows, block)] * 3 + [tall(block // GROUP, TAPS), tall(block, rows)],
        out_specs=[wide(rows, block), wide(rows, block), wide(ORDER, block)],
        out_shape=[shape(rows, width), shape(rows, width), shape(ORDER, width)],
    )(rim, conv_own, query, taps, ends_coef)
    ends_far = [shift(ends, k) for k in range(1, n_ctx)]


    local_fwd = local(False, kernel_rev, mixed)
    mine = call(
        functools.partial(pack_body, n_ctx), "pack", 0, 4 * part * depth * n_ctx,
        grid_spec=pltpu.PrefetchScalarGridSpec(
            num_scalar_prefetch=1, grid=(n_dp,),
            in_specs=[piece(k) for k in range(n_ctx)] + [ANY] * (n_ctx - 1),
            out_specs=[pl.BlockSpec((part, feats), lambda j, p: (0, j))] * n_ctx,
        ),
        out_shape=[shape(part, depth)] * n_ctx,
    )(place, *[out_grad] * n_ctx, *ends_far)
    mine = [mine[0]] + [swap(mine[k], "ctx", k) for k in range(1, n_ctx)]
    long_out, gated = call(
        functools.partial(long_body, n_ctx - 1), "long", 2 * rows * 128 * width, rows * width * 10,
        grid=(steps,),
        in_specs=[wide(rows, block), wide((n_ctx - 1) * rows, block), wide(rows, block)] + [wide(ORDER, block)] * (n_ctx - 1),
        out_specs=[wide(rows, block), pl.BlockSpec((1, rows, block), lambda i: (i, 0, 0))],
        out_shape=[shape(rows, width), shape(n_dp, rows, quarter)],
    )(local_fwd, carry_coef, gate, *ends_far)
    gated_far = lax.all_to_all(gated, "dp", 0, 0, tiled=True)
    side = n_ctx // 2

    def join(pieces, *after):
        return call(
            join_body, "join", 0, 4 * part * depth * side,
            grid=(n_dp,),
            in_specs=[wide(part, feats)] * side + [ANY] * len(after),
            out_specs=deep(side, part, feats),
            out_shape=shape(side, part, depth),
        )(*pieces, *after)

    def gather(value):
        value = lax.all_gather(value, ("dp", "tp"), axis=0, tiled=False)
        return value.reshape(n_dp, n_tp, side, part, depth)

    far = join(mine[side:], weights, gated_far, *mine[1:side])
    near = join(mine[:side], far)
    grad_far, grad_near = gather(far), gather(near)
    tokens = n_ctx * n_dp * rows
    last = n_ctx - 1
    from_left, from_right = [], []
    right = left = gated_far
    for t in range(last):
        right = shift(right, 1, range(t, last))
        left = shift(left, -1, range(1, n_ctx - t))
        from_left.append(right)
        from_right.append(left)

    chunk = (1, n_dp, rows, quarter)
    grad_block = (n_dp, n_tp, 1, part, depth)
    all_weights = pl.BlockSpec((n_dp, quarter, feats), lambda i: (0, 0, 0))
    far_part = call(
        functools.partial(delta_body, None), "delta", tokens * depth * quarter,
        tokens * depth + 2 * depth * quarter + tokens * quarter,
        grid=(side,),
        in_specs=[pl.BlockSpec(grad_block, lambda i: (0, 0, i, 0, 0)), all_weights, ANY, ANY],
        out_specs=pl.BlockSpec(chunk, lambda i: (i, 0, 0, 0)),
        out_shape=shape(side, n_dp, rows, quarter),
    )(grad_far, weights, from_left[0], from_right[0])
    partial = call(
        functools.partial(delta_body, side), "delta", tokens * depth * quarter,
        tokens * depth + 2 * depth * quarter + 3 * tokens * quarter,
        grid=(n_ctx,),
        in_specs=[
            pl.BlockSpec(grad_block, lambda i: (0, 0, jnp.minimum(i, side - 1), 0, 0)),
            all_weights,
            pl.BlockSpec(chunk, lambda i: (jnp.maximum(i - side, 0), 0, 0, 0)),
        ],
        out_specs=pl.BlockSpec(chunk, lambda i: (i, 0, 0, 0)),
        out_shape=shape(n_ctx, n_dp, rows, quarter),
    )(grad_near, weights, far_part)
    def place_of(i, p):
        return p[1] ^ ((p[1] + n_ctx - i) % n_ctx)

    grad_t = call(
        functools.partial(flip_body, place_of, side), "flip", 0, 6 * tokens * depth,
        grid_spec=pltpu.PrefetchScalarGridSpec(
            num_scalar_prefetch=1, grid=(n_ctx, n_dp),
            in_specs=[
                pl.BlockSpec(
                    (1, n_tp, 1, part, depth),
                    lambda i, j, p: (j, 0, jnp.maximum(place_of(i, p) - side, 0), 0, 0),
                ),
                pl.BlockSpec(
                    (1, n_tp, 1, part, depth),
                    lambda i, j, p: (j, 0, jnp.minimum(place_of(i, p), side - 1), 0, 0),
                ),
                ANY,
            ],
            out_specs=pl.BlockSpec((depth, rows), lambda i, j, p: (0, i * n_dp + j)),
        ),
        out_shape=shape(depth, tokens),
    )(place, grad_far, grad_near, partial)
    own = place[1]
    start = jnp.where(own < side, own ^ last, own) - side
    first = lax.dynamic_slice_in_dim(far_part, start, 1)
    right, left = shift(first, 1, [0]), shift(first, -1, [last])

    def pick(ahead):
        return pl.BlockSpec(
            (1, 1, rows, quarter), lambda i, q: (q[ahead], i, 0, 0)
        )

    piece_of = pl.BlockSpec((1, 1, rows, quarter), lambda i, q: (0, i, 0, 0))
    for t in range(1, last):
        after = (from_left[t], from_right[t]) + ((grad_t,) if t == last - 1 else ())
        dests = jnp.clip(jnp.stack([last - t + own, t - last + own]), 0, last) ^ own
        if t < side:
            table, dests = far_part, jnp.maximum(dests - side, 0)
        else:
            table = partial
        right, left = call(
            add_body, "add", 0, 12 * n_dp * rows * quarter,
            grid_spec=pltpu.PrefetchScalarGridSpec(
                num_scalar_prefetch=1, grid=(n_dp,),
                in_specs=[pick(0), pick(1), piece_of, piece_of] + [ANY] * len(after),
                out_specs=[piece_of] * 2,
            ),
            out_shape=[shape(*chunk)] * 2,
        )(dests, table, table, right, left, *after)
        token = right
        right = shift(right, 1, range(t + 1))
        left = shift(left, -1, range(last - t, n_ctx))
    gated_all = call(
        merge_body, "merge", 0, 2 * (2 * n_ctx + last) * n_dp * rows * quarter,
        grid=(n_dp,),
        in_specs=[pl.BlockSpec((1, rows, quarter), lambda i: (i, 0, 0))] * (1 + 2 * last) + [ANY],
        out_specs=pl.BlockSpec((n_ctx, 1, rows, quarter), lambda i: (0, i, 0, 0)),
        out_shape=shape(n_ctx, n_dp, rows, quarter),
    )(gated_far, *from_left, *from_right[::-1], token).reshape(tokens, quarter)
    pieces = {}
    for k in list(range(n_dp - 1, -1, -1)):
        token = pieces[k] = call(
            weight_body, "weight", 2 * tokens * feats * quarter, 2 * tokens * (feats + quarter),
            grid_spec=pltpu.PrefetchScalarGridSpec(
                num_scalar_prefetch=1, grid=(2,),
                in_specs=[
                    pl.BlockSpec((feats, tokens), lambda i, p, k=k: (p[0] ^ k, 0)),
                    pl.BlockSpec((tokens, quarter // 2), lambda i, p: (0, i)),
                    ANY,
                ],
                out_specs=pl.BlockSpec((feats, quarter // 2), lambda i, p: (0, i)),
            ),
            out_shape=shape(feats, quarter),
        )(place, grad_t, gated_all, token)

    def hold(value, after):
        return call(
            wait_body, "hold", 0, 0,
            in_specs=[ANY] * 2, out_specs=ANY,
            out_shape=shape(*value.shape), input_output_aliases={0: 0},
        )(value, after)

    diagonal = swap(pieces[n_dp - 1], "dp", n_dp - 1)
    delta = call(
        sum_body, "sum", 0, 8 * n_dp * rows * quarter,
        grid_spec=pltpu.PrefetchScalarGridSpec(
            num_scalar_prefetch=1, grid=(n_dp,),
            in_specs=[pick(0), piece_of, piece_of, ANY],
            out_specs=pl.BlockSpec((1, rows, quarter), lambda i, q: (i, 0, 0)),
        ),
        out_shape=shape(n_dp, rows, quarter),
    )(own[None] * 0, partial, right, left, diagonal)
    delta_far = lax.all_to_all(delta, "dp", 0, 0, tiled=True)

    weight_far = [pieces[0]] + [
        swap(hold(pieces[k], delta_far), "dp", k) for k in range(1, n_dp - 1)
    ] + [diagonal]

    seed, starts, gate_grad = call(
        seed_body, "seed", 2 * rows * 128 * width, rows * width * 10,
        grid=(steps,),
        in_specs=[
            pl.BlockSpec((1, rows, block), lambda i: (i, 0, 0)),
            wide(rows, block), wide(rows, block), tall(block, rows), ANY,
        ],
        out_specs=[wide(rows, block), wide(ORDER, block), wide(rows, block)],
        out_shape=[shape(rows, width), shape(ORDER, width), shape(rows, width)],
    )(delta_far, gate, long_out, starts_coef, delta)
    starts_far = [shift(starts, -k) for k in range(1, n_ctx)]
    local_bwd = local(True, kernel, seed)
    query_grad, conv_grad = call(
        functools.partial(back_body, n_ctx - 1), "back", 2 * rows * 128 * width, rows * width * 12,
        grid=(steps,),
        in_specs=[wide(rows, block), wide((n_ctx - 1) * rows, block)] + [wide(rows, block)] * 2
        + [wide(ORDER, block)] * (n_ctx - 1),
        out_specs=[wide(rows, block)] * 2,
        out_shape=[shape(rows, width)] * 2,
    )(local_bwd, back_coef, conv, query, *starts_far)

    cut = feats // n_dp
    weight_grad = call(
        lay_body, "lay", 0, 4 * feats * width,
        grid_spec=pltpu.PrefetchScalarGridSpec(
            num_scalar_prefetch=1, grid=(n_dp,),
            in_specs=[pl.BlockSpec((cut, quarter), lambda i, p: (i, 0))] * n_dp + [ANY],
            out_specs=pl.BlockSpec((cut, width), lambda i, p: (i, 0)),
        ),
        out_shape=shape(feats, width),
    )(place, *weight_far, query_grad)
    return query_grad, conv_grad, gate_grad, weight_grad


def solution(mesh):
    rows = P(("dp", "ctx"), "tp")
    return jax.shard_map(
        on_device,
        mesh=mesh,
        in_specs=(rows, rows, rows, rows, P(("dp", "ctx"), None), P("tp", ("dp", "ctx")),
                  P("tp", None), P("tp", None), P("tp", None)),
        out_specs=(rows, rows, rows, rows),
        check_vma=False,
    )
```

```python
import functools

import jax
import jax.numpy as jnp
from jax import lax
from jax.experimental import pallas as pl
from jax.experimental.pallas import tpu as pltpu
from jax.sharding import PartitionSpec as P

GROUP = 16
TAPS = 128
ORDER = 16
LANES = 128
PER_SLAB = LANES // GROUP
BF16 = jnp.bfloat16
F32 = jnp.float32
VMEM = 50 * 2**20
ANY = pl.BlockSpec(memory_space=pl.ANY)


def call(body, name, flops, nbytes, **kwargs):
    return pl.pallas_call(
        body,
        name=name,
        cost_estimate=pl.CostEstimate(flops=flops, bytes_accessed=nbytes, transcendentals=0),
        compiler_params=pltpu.CompilerParams(vmem_limit_bytes=VMEM),
        **kwargs,
    )


def circulants(rows_ref, base):
    out = []
    for j in range(PER_SLAB):
        row = rows_ref[base + j : base + j + 1, :]
        out.append(
            pltpu.roll(jnp.broadcast_to(row, (LANES, LANES)), 0, 1, stride=1, stride_axis=0)
        )
    return out


def lower_mask():
    t = lax.broadcasted_iota(jnp.int32, (LANES, LANES), 0)
    u = lax.broadcasted_iota(jnp.int32, (LANES, LANES), 1)
    return u <= t


def pick_groups(stacked, rows):
    lane_group = lax.broadcasted_iota(jnp.int32, (rows, LANES), 1) // GROUP
    out = stacked[:rows]
    for j in range(1, PER_SLAB):
        out = jnp.where(lane_group == j, stacked[j * rows : (j + 1) * rows], out)
    return out


def spread_groups(state):
    tiled = jnp.concatenate([state] * PER_SLAB, axis=0)
    row_group = lax.broadcasted_iota(jnp.int32, (LANES, LANES), 0) // ORDER
    lane_group = lax.broadcasted_iota(jnp.int32, (LANES, LANES), 1) // GROUP
    return jnp.where(row_group == lane_group, tiled, jnp.zeros_like(tiled))


def dot(a, b):
    return jnp.dot(a, b, preferred_element_type=F32)


def conv_body(rim, own_part, query, taps, ends_coef, *refs):
    conv, mixed, ends = refs[-3:]
    lower = lower_mask()
    for s in range(rim.shape[1] // LANES):
        cols = slice(s * LANES, (s + 1) * LANES)
        blocks = [
            jnp.where(lower, jnp.zeros_like(circ), circ).astype(BF16)
            for circ in circulants(taps, s * PER_SLAB)
        ]
        out = own_part[:, cols] + pick_groups(
            dot(jnp.concatenate(blocks, axis=0), rim[:, cols]), LANES
        )
        conv[:, cols] = out.astype(conv.dtype)
        mixed[:, cols] = (query[:, cols].astype(F32) * out).astype(BF16)
    for s in range(rim.shape[1] // LANES):
        cols = slice(s * LANES, (s + 1) * LANES)
        ends[:, cols] = pick_groups(
            dot(ends_coef[s * LANES : (s + 1) * LANES, :], mixed[:, cols]), ORDER
        ).astype(ends.dtype)


def local_body(transposed, rows, x, *refs):
    out = refs[-1]
    lower = lower_mask()
    keep = ~lower | (lax.broadcasted_iota(jnp.int32, (LANES, LANES), 0)
                     == lax.broadcasted_iota(jnp.int32, (LANES, LANES), 1)) if transposed else lower
    for s in range(x.shape[1] // LANES):
        cols = slice(s * LANES, (s + 1) * LANES)
        blocks = [
            jnp.where(keep, circ, jnp.zeros_like(circ)).astype(BF16)
            for circ in circulants(rows, s * PER_SLAB)
        ]
        out[:, cols] = pick_groups(
            dot(jnp.concatenate(blocks, axis=0), x[:, cols]), LANES
        ).astype(out.dtype)


def carried(states, coef, cols):
    wide_states = jnp.concatenate([spread_groups(ref[:, cols]) for ref in states], axis=0)
    count = len(states)
    rows = coef.shape[0] // count
    parts = [coef[k * rows : (k + 1) * rows, cols] for k in range(count)]
    return dot(jnp.concatenate(parts, axis=1), wide_states)


def long_body(count, local, coef, gate, *refs):
    states, (long_out, gated) = refs[:count], refs[-2:]
    for s in range(local.shape[1] // LANES):
        cols = slice(s * LANES, (s + 1) * LANES)
        out = local[:, cols].astype(F32) + carried(states, coef, cols)
        long_out[:, cols] = out.astype(long_out.dtype)
        gated[0, :, cols] = (gate[:, cols].astype(F32) * out).astype(BF16)


def seed_body(count, place, *refs):
    sources = refs[:count]
    gate, long_out, starts_coef, seed, starts, gate_grad, delta = refs[count:]
    for k, source in enumerate(sources):

        @pl.when(pl.program_id(0) == k)
        def _(source=source):
            delta[...] = source[...]

    for s in range(gate.shape[1] // LANES):
        cols = slice(s * LANES, (s + 1) * LANES)
        out = delta[:, cols].astype(F32)
        seed[:, cols] = (out * gate[:, cols].astype(F32)).astype(BF16)
        gate_grad[:, cols] = (out * long_out[:, cols].astype(F32)).astype(BF16)
    for s in range(gate.shape[1] // LANES):
        cols = slice(s * LANES, (s + 1) * LANES)
        starts[:, cols] = pick_groups(
            dot(starts_coef[s * LANES : (s + 1) * LANES, :], seed[:, cols]), ORDER
        ).astype(starts.dtype)


def back_body(count, local, coef, conv, query, *refs):
    states, (query_grad, conv_grad) = refs[:count], refs[-2:]
    for s in range(local.shape[1] // LANES):
        cols = slice(s * LANES, (s + 1) * LANES)
        out = local[:, cols].astype(F32) + carried(states, coef, cols)
        query_grad[:, cols] = (out * conv[:, cols].astype(F32)).astype(BF16)
        conv_grad[:, cols] = (out * query[:, cols].astype(F32)).astype(BF16)


def pack_body(place, *refs):
    count = len(refs) // 2
    for source, target in zip(refs[:count], refs[-count:]):
        target[...] = source[...]


def join_body(*refs):
    out = refs[-1]
    for k in range(out.shape[0]):
        out[k] = refs[k][...]


def delta_body(whole, place, dest, grad, weights, *refs):
    depth, out = weights.shape[2], refs[-1]

    def multiply():
        total = None
        for k in range(weights.shape[0]):
            rows = grad[:, :, :, :, k * depth : (k + 1) * depth].reshape(-1, depth)
            term = lax.dot_general(
                rows, weights[k], (((1,), (1,)), ((), ())), preferred_element_type=F32
            )
            total = term if total is None else total + term
        out[...] = total.astype(BF16).reshape(out.shape)

    if not whole:
        return multiply()
    is_last = pl.program_id(0) == pl.num_programs(0) - 1
    pl.when(jnp.logical_not(is_last))(multiply)

    @pl.when(is_last)
    def _():
        out[...] = refs[0][...]


def flip_body(place, grad, after, out):
    out[...] = grad[...].reshape(-1, grad.shape[-1]).T


def lay_body(source, after, target):
    target[...] = source[0]


def add_body(dests, partial_right, partial_left, right, left, *refs):
    out_right, out_left = refs[-2:]
    out_right[...] = (partial_right[...].astype(F32) + right[...].astype(F32)).astype(BF16)
    out_left[...] = (partial_left[...].astype(F32) + left[...].astype(F32)).astype(BF16)


def merge_body(own, *refs):
    out = refs[-1]
    count = out.shape[0] - 1
    out[0] = own[...]
    for k in range(count):
        out[k + 1] = refs[k][...] + refs[count + k][...]


def sum_body(place, partial, right, left, after, *outs):
    total = partial[0, 0].astype(F32) + right[0, 0].astype(F32) + left[0, 0].astype(F32)
    for k, out in enumerate(outs):

        @pl.when(pl.program_id(0) == k)
        def _(out=out):
            out[...] = total.astype(BF16)


def weight_body(grad_t, gated, after, out):
    out[0] = dot(grad_t[...], gated[...]).astype(out.dtype)


def wide(rows, lanes):
    return pl.BlockSpec((rows, lanes), lambda i: (0, i))


def tall(rows, cols):
    return pl.BlockSpec((rows, cols), lambda i: (i, 0))


def deep(count, rows, lanes):
    return pl.BlockSpec((count, rows, lanes), lambda i: (0, 0, i))


def shape(*dims, dtype=BF16):
    return jax.ShapeDtypeStruct(dims, dtype)


def on_device(query, key_in, value_in, gate, out_grad, proj_weight, mr_filter, lr_rate, lr_residue):
    rows, width = query.shape
    groups = width // GROUP
    n_dp, n_ctx, n_tp = (lax.axis_size(a) for a in ("dp", "ctx", "tp"))
    feats = proj_weight.shape[1]
    quarter = width // n_dp
    depth = n_dp * feats
    block = quarter
    steps = width // block
    part = rows // n_tp

    place = jnp.stack([lax.axis_index(a) for a in ("dp", "ctx", "tp")]).astype(jnp.int32)

    def swap(value, axis, k):
        return lax.ppermute(value, axis, [(i, i ^ k) for i in range(lax.axis_size(axis))])

    def shift(value, k, senders=None):
        ends = [(i, i + k) for i in senders or range(n_ctx) if 0 <= i + k < n_ctx]
        return lax.ppermute(value, "ctx", ends)

    def piece(k):
        return pl.BlockSpec((part, feats), lambda j, p: (p[2], j * n_ctx + (p[1] ^ k)))

    weights = lax.all_to_all(proj_weight.reshape(n_dp, quarter, feats), "dp", 0, 0, tiled=True)
    mine = call(
        pack_body, "pack", 0, 4 * part * depth * n_ctx,
        grid_spec=pltpu.PrefetchScalarGridSpec(
            num_scalar_prefetch=1, grid=(n_dp,),
            in_specs=[piece(k) for k in range(n_ctx)],
            out_specs=[pl.BlockSpec((part, feats), lambda j, p: (0, j))] * n_ctx,
        ),
        out_shape=[shape(part, depth)] * n_ctx,
    )(place, *[out_grad] * n_ctx)
    mine = [mine[0]] + [swap(mine[k], "ctx", k) for k in range(1, n_ctx)]
    product = (key_in.astype(F32) * value_in.astype(F32)).astype(BF16)
    rim = shift(product, 1)
    rate = lr_rate.reshape(-1, 1)
    residue = lr_residue.reshape(-1, 1)
    counts = jnp.arange(rows, dtype=F32)[None, :]
    ends_coef = jnp.exp(-rate * (rows - 1 - counts)).astype(BF16)
    starts_coef = jnp.exp(-rate * counts).astype(BF16)
    away = jnp.arange((n_ctx - 1) * rows, dtype=F32)[:, None]
    inside = away % rows
    carry_coef = (residue.T * jnp.exp(-rate.T * (away + 1))).astype(BF16)
    back_coef = (residue.T * jnp.exp(-rate.T * (away + rows - 2 * inside))).astype(BF16)
    kernel = jnp.sum(
        lr_residue[:, :, None] * jnp.exp(-lr_rate[:, :, None] * counts[:, None, :]), axis=1
    )

    def reversed_row(values):
        return jnp.roll(values[:, ::-1], 1, axis=1)

    taps = reversed_row(mr_filter.astype(F32))
    kernel_rev = reversed_row(kernel)
    def local(transposed, table, x, *after):
        return call(
            functools.partial(local_body, transposed),
            "local_t" if transposed else "local",
            2 * rows * 128 * width * 8, rows * width * 6,
            grid=(steps,),
            in_specs=[tall(block // GROUP, rows), wide(rows, block)] + [ANY] * len(after),
            out_specs=wide(rows, block),
            out_shape=shape(rows, width, dtype=F32),
        )(table, x, *after)

    conv_own = local(
        False, taps, product, ends_coef, starts_coef, carry_coef, back_coef, kernel_rev, kernel
    )
    conv, mixed, ends = call(
        conv_body, "conv", 2 * rows * 128 * width * 8, rows * width * 14,
        grid=(steps,),
        in_specs=[wide(rows, block)] * 3 + [tall(block // GROUP, TAPS), tall(block, rows)],
        out_specs=[wide(rows, block), wide(rows, block), wide(ORDER, block)],
        out_shape=[shape(rows, width), shape(rows, width), shape(ORDER, width)],
    )(rim, conv_own, query, taps, ends_coef)
    ends_far = [shift(ends, k) for k in range(1, n_ctx)]


    local_fwd = local(False, kernel_rev, mixed)
    mine = call(
        join_body, "join", 0, 4 * part * depth * n_ctx,
        grid=(n_dp,),
        in_specs=[wide(part, feats)] * n_ctx + [ANY] * 2,
        out_specs=deep(n_ctx, part, feats),
        out_shape=shape(n_ctx, part, depth),
    )(*mine, weights, local_fwd)
    grad = lax.all_gather(mine, ("dp", "tp"), axis=0, tiled=False)
    grad = grad.reshape(n_dp, n_tp, n_ctx, part, depth)
    long_out, gated = call(
        functools.partial(long_body, n_ctx - 1), "long", 2 * rows * 128 * width, rows * width * 10,
        grid=(steps,),
        in_specs=[wide(rows, block), wide((n_ctx - 1) * rows, block), wide(rows, block)] + [wide(ORDER, block)] * (n_ctx - 1) + [ANY],
        out_specs=[wide(rows, block), pl.BlockSpec((1, rows, block), lambda i: (i, 0, 0))],
        out_shape=[shape(rows, width), shape(n_dp, rows, quarter)],
    )(local_fwd, carry_coef, gate, *ends_far, mine)
    gated_far = lax.all_to_all(gated, "dp", 0, 0, tiled=True)
    tokens = n_ctx * n_dp * rows
    last = n_ctx - 1
    from_left, from_right = [], []
    right = left = gated_far
    for t in range(last):
        right = shift(right, 1, range(t, last))
        left = shift(left, -1, range(1, n_ctx - t))
        from_left.append(right)
        from_right.append(left)

    first_dest = jnp.where(place[1] < n_ctx // 2, last, 0)
    chunk = (1, n_dp, rows, quarter)

    def project(dests, *after):
        count = dests.shape[0]
        whole = count > 1
        return call(
            functools.partial(delta_body, whole), "delta",
            2 * max(count - 1, 1) * n_dp * rows * depth * quarter,
            2 * tokens * depth + 2 * depth * quarter + 2 * count * n_dp * rows * quarter,
            grid_spec=pltpu.PrefetchScalarGridSpec(
                num_scalar_prefetch=2, grid=(count,),
                in_specs=[
                    pl.BlockSpec(
                        (n_dp, n_tp, 1, part, depth), lambda i, p, q: (0, 0, p[1] ^ q[i], 0, 0)
                    ),
                    pl.BlockSpec((n_dp, quarter, feats), lambda i, p, q: (0, 0, 0)),
                ] + ([pl.BlockSpec(chunk, lambda i, p, q: (0, 0, 0, 0))] if whole
                     else [ANY] * len(after)),
                out_specs=pl.BlockSpec(
                    chunk, lambda i, p, q: (q[i] if whole else 0, 0, 0, 0)
                ),
            ),
            out_shape=shape(count, n_dp, rows, quarter),
        )(place, dests, grad, weights, *after)

    first = project(first_dest[None], from_left[0], from_right[0])
    others = (first_dest + 1 + jnp.arange(n_ctx, dtype=jnp.int32)) % n_ctx
    partial = project(others.astype(jnp.int32), first)
    grad_t = call(
        flip_body, "flip", 0, 4 * tokens * depth,
        grid_spec=pltpu.PrefetchScalarGridSpec(
            num_scalar_prefetch=1, grid=(n_ctx, n_dp),
            in_specs=[
                pl.BlockSpec(
                    (1, n_tp, 1, part, depth),
                    lambda i, j, p: (j, 0, p[1] ^ ((p[1] + n_ctx - i) % n_ctx), 0, 0),
                ),
                ANY,
            ],
            out_specs=pl.BlockSpec((depth, rows), lambda i, j, p: (0, i * n_dp + j)),
        ),
        out_shape=shape(depth, tokens),
    )(place, grad, partial)
    right, left = shift(first, 1, [0]), shift(first, -1, [last])

    def pick(ahead):
        return pl.BlockSpec(
            (1, 1, rows, quarter), lambda i, q: (q[ahead], i, 0, 0)
        )

    piece_of = pl.BlockSpec((1, 1, rows, quarter), lambda i, q: (0, i, 0, 0))
    for t in range(1, last):
        after = (from_left[t], from_right[t]) + ((grad_t,) if t == last - 1 else ())
        dests = jnp.clip(jnp.stack([last - t + place[1], t - last + place[1]]), 0, last)
        right, left = call(
            add_body, "add", 0, 12 * n_dp * rows * quarter,
            grid_spec=pltpu.PrefetchScalarGridSpec(
                num_scalar_prefetch=1, grid=(n_dp,),
                in_specs=[pick(0), pick(1), piece_of, piece_of] + [ANY] * len(after),
                out_specs=[piece_of] * 2,
            ),
            out_shape=[shape(*chunk)] * 2,
        )(dests, partial, partial, right, left, *after)
        token = right
        right = shift(right, 1, range(t + 1))
        left = shift(left, -1, range(last - t, n_ctx))
    gated_all = call(
        merge_body, "merge", 0, 2 * (2 * n_ctx + last) * n_dp * rows * quarter,
        grid=(n_dp,),
        in_specs=[pl.BlockSpec((1, rows, quarter), lambda i: (i, 0, 0))] * (1 + 2 * last) + [ANY],
        out_specs=pl.BlockSpec((n_ctx, 1, rows, quarter), lambda i: (0, i, 0, 0)),
        out_shape=shape(n_ctx, n_dp, rows, quarter),
    )(gated_far, *from_left, *from_right[::-1], token).reshape(tokens, quarter)
    weight_part = call(
        weight_body, "weight", 2 * tokens * depth * quarter, 2 * tokens * (depth + quarter),
        grid=(n_dp,),
        in_specs=[
            pl.BlockSpec((feats, tokens), lambda i: (i, 0)),
            pl.BlockSpec((tokens, quarter), lambda i: (0, 0)),
            ANY,
        ],
        out_specs=pl.BlockSpec((1, feats, quarter), lambda i: (i, 0, 0)),
        out_shape=shape(n_dp, feats, quarter),
    )(grad_t, gated_all, token)
    weight_far = lax.all_to_all(weight_part, "dp", 0, 0, tiled=True)

    delta = call(
        sum_body, "sum", 0, 8 * n_dp * rows * quarter,
        grid_spec=pltpu.PrefetchScalarGridSpec(
            num_scalar_prefetch=1, grid=(n_dp,),
            in_specs=[
                pl.BlockSpec((1, 1, rows, quarter), lambda i, p: (p[1], p[0] ^ i, 0, 0)),
                pl.BlockSpec((1, 1, rows, quarter), lambda i, p: (0, p[0] ^ i, 0, 0)),
                pl.BlockSpec((1, 1, rows, quarter), lambda i, p: (0, p[0] ^ i, 0, 0)),
                ANY,
            ],
            out_specs=[pl.BlockSpec((rows, quarter), lambda i, p: (0, 0))] * n_dp,
        ),
        out_shape=[shape(rows, quarter)] * n_dp,
    )(place, partial, right, left, weight_part)
    delta = [delta[0]] + [swap(delta[k], "dp", k) for k in range(1, n_dp)]

    here = pl.BlockSpec((rows, block), lambda i, p: (0, p[0] ^ i))
    seed, starts, gate_grad = call(
        functools.partial(seed_body, n_dp), "seed", 2 * rows * 128 * width, rows * width * 10,
        grid_spec=pltpu.PrefetchScalarGridSpec(
            num_scalar_prefetch=1, grid=(n_dp,),
            in_specs=[pl.BlockSpec((rows, quarter), lambda i, p: (0, 0))] * n_dp
            + [here, here, pl.BlockSpec((block, rows), lambda i, p: (p[0] ^ i, 0))],
            out_specs=[here, pl.BlockSpec((ORDER, block), lambda i, p: (0, p[0] ^ i)), here],
            scratch_shapes=[pltpu.VMEM((rows, block), BF16)],
        ),
        out_shape=[shape(rows, width), shape(ORDER, width), shape(rows, width)],
    )(place, *delta, gate, long_out, starts_coef)
    starts_far = [shift(starts, -k) for k in range(1, n_ctx)]
    local_bwd = local(True, kernel, seed)
    query_grad, conv_grad = call(
        functools.partial(back_body, n_ctx - 1), "back", 2 * rows * 128 * width, rows * width * 12,
        grid=(steps,),
        in_specs=[wide(rows, block), wide((n_ctx - 1) * rows, block)] + [wide(rows, block)] * 2
        + [wide(ORDER, block)] * (n_ctx - 1),
        out_specs=[wide(rows, block)] * 2,
        out_shape=[shape(rows, width)] * 2,
    )(local_bwd, back_coef, conv, query, *starts_far)

    weight_grad = call(
        lay_body, "lay", 0, 4 * feats * width,
        grid=(n_dp,),
        in_specs=[pl.BlockSpec((1, feats, quarter), lambda i: (i, 0, 0)), ANY],
        out_specs=pl.BlockSpec((feats, quarter), lambda i: (0, i)),
        out_shape=shape(feats, width),
    )(weight_far, query_grad)
    return query_grad, conv_grad, gate_grad, weight_grad


def solution(mesh):
    rows = P(("dp", "ctx"), "tp")
    return jax.shard_map(
        on_device,
        mesh=mesh,
        in_specs=(rows, rows, rows, rows, P(("dp", "ctx"), None), P("tp", ("dp", "ctx")),
                  P("tp", None), P("tp", None), P("tp", None)),
        out_specs=(rows, rows, rows, rows),
        check_vma=False,
    )
```

```python
import functools

import jax
import jax.numpy as jnp
from jax import lax
from jax.experimental import pallas as pl
from jax.experimental.pallas import tpu as pltpu
from jax.sharding import PartitionSpec as P

GROUP = 16
TAPS = 128
ORDER = 16
LANES = 128
PER_SLAB = LANES // GROUP
BF16 = jnp.bfloat16
F32 = jnp.float32
VMEM = 50 * 2**20
ANY = pl.BlockSpec(memory_space=pl.ANY)


def call(body, name, flops, nbytes, **kwargs):
    return pl.pallas_call(
        body,
        name=name,
        cost_estimate=pl.CostEstimate(flops=flops, bytes_accessed=nbytes, transcendentals=0),
        compiler_params=pltpu.CompilerParams(vmem_limit_bytes=VMEM),
        **kwargs,
    )


def circulants(rows_ref, base):
    out = []
    for j in range(PER_SLAB):
        row = rows_ref[base + j : base + j + 1, :]
        out.append(
            pltpu.roll(jnp.broadcast_to(row, (LANES, LANES)), 0, 1, stride=1, stride_axis=0)
        )
    return out


def lower_mask():
    t = lax.broadcasted_iota(jnp.int32, (LANES, LANES), 0)
    u = lax.broadcasted_iota(jnp.int32, (LANES, LANES), 1)
    return u <= t


def pick_groups(stacked, rows):
    lane_group = lax.broadcasted_iota(jnp.int32, (rows, LANES), 1) // GROUP
    out = stacked[:rows]
    for j in range(1, PER_SLAB):
        out = jnp.where(lane_group == j, stacked[j * rows : (j + 1) * rows], out)
    return out


def spread_groups(state):
    tiled = jnp.concatenate([state] * PER_SLAB, axis=0)
    row_group = lax.broadcasted_iota(jnp.int32, (LANES, LANES), 0) // ORDER
    lane_group = lax.broadcasted_iota(jnp.int32, (LANES, LANES), 1) // GROUP
    return jnp.where(row_group == lane_group, tiled, jnp.zeros_like(tiled))


def dot(a, b):
    return jnp.dot(a, b, preferred_element_type=F32)


def conv_body(rim, own_part, query, taps, ends_coef, *refs):
    conv, mixed, ends = refs[-3:]
    lower = lower_mask()
    for s in range(rim.shape[1] // LANES):
        cols = slice(s * LANES, (s + 1) * LANES)
        blocks = [
            jnp.where(lower, jnp.zeros_like(circ), circ).astype(BF16)
            for circ in circulants(taps, s * PER_SLAB)
        ]
        out = own_part[:, cols] + pick_groups(
            dot(jnp.concatenate(blocks, axis=0), rim[:, cols]), LANES
        )
        conv[:, cols] = out.astype(conv.dtype)
        mixed[:, cols] = (query[:, cols].astype(F32) * out).astype(BF16)
    for s in range(rim.shape[1] // LANES):
        cols = slice(s * LANES, (s + 1) * LANES)
        ends[:, cols] = pick_groups(
            dot(ends_coef[s * LANES : (s + 1) * LANES, :], mixed[:, cols]), ORDER
        ).astype(ends.dtype)


def local_body(transposed, rows, x, *refs):
    out = refs[-1]
    lower = lower_mask()
    keep = ~lower | (lax.broadcasted_iota(jnp.int32, (LANES, LANES), 0)
                     == lax.broadcasted_iota(jnp.int32, (LANES, LANES), 1)) if transposed else lower
    for s in range(x.shape[1] // LANES):
        cols = slice(s * LANES, (s + 1) * LANES)
        blocks = [
            jnp.where(keep, circ, jnp.zeros_like(circ)).astype(BF16)
            for circ in circulants(rows, s * PER_SLAB)
        ]
        out[:, cols] = pick_groups(
            dot(jnp.concatenate(blocks, axis=0), x[:, cols]), LANES
        ).astype(out.dtype)


def carried(states, coef, cols):
    wide_states = jnp.concatenate([spread_groups(ref[:, cols]) for ref in states], axis=0)
    count = len(states)
    rows = coef.shape[0] // count
    parts = [coef[k * rows : (k + 1) * rows, cols] for k in range(count)]
    return dot(jnp.concatenate(parts, axis=1), wide_states)


def long_body(count, local, coef, gate, *refs):
    states, (long_out, gated) = refs[:count], refs[-2:]
    for s in range(local.shape[1] // LANES):
        cols = slice(s * LANES, (s + 1) * LANES)
        out = local[:, cols].astype(F32) + carried(states, coef, cols)
        long_out[:, cols] = out.astype(long_out.dtype)
        gated[0, :, cols] = (gate[:, cols].astype(F32) * out).astype(BF16)


def seed_body(count, place, *refs):
    sources = refs[:count]
    gate, long_out, starts_coef, seed, starts, gate_grad, delta = refs[count:]
    for k, source in enumerate(sources):

        @pl.when(pl.program_id(0) == k)
        def _(source=source):
            delta[...] = source[...]

    for s in range(gate.shape[1] // LANES):
        cols = slice(s * LANES, (s + 1) * LANES)
        out = delta[:, cols].astype(F32)
        seed[:, cols] = (out * gate[:, cols].astype(F32)).astype(BF16)
        gate_grad[:, cols] = (out * long_out[:, cols].astype(F32)).astype(BF16)
    for s in range(gate.shape[1] // LANES):
        cols = slice(s * LANES, (s + 1) * LANES)
        starts[:, cols] = pick_groups(
            dot(starts_coef[s * LANES : (s + 1) * LANES, :], seed[:, cols]), ORDER
        ).astype(starts.dtype)


def back_body(count, local, coef, conv, query, *refs):
    states, (query_grad, conv_grad) = refs[:count], refs[-2:]
    for s in range(local.shape[1] // LANES):
        cols = slice(s * LANES, (s + 1) * LANES)
        out = local[:, cols].astype(F32) + carried(states, coef, cols)
        query_grad[:, cols] = (out * conv[:, cols].astype(F32)).astype(BF16)
        conv_grad[:, cols] = (out * query[:, cols].astype(F32)).astype(BF16)


def pack_body(place, *refs):
    count = len(refs) // 2
    for source, target in zip(refs[:count], refs[-count:]):
        target[...] = source[...]


def join_body(*refs):
    out = refs[-1]
    for k in range(out.shape[0]):
        out[k] = refs[k][...]


def delta_body(whole, place, dest, grad, weights, *refs):
    depth, out = weights.shape[2], refs[-1]

    def multiply():
        total = None
        for k in range(weights.shape[0]):
            rows = grad[:, :, :, :, k * depth : (k + 1) * depth].reshape(-1, depth)
            term = lax.dot_general(
                rows, weights[k], (((1,), (1,)), ((), ())), preferred_element_type=F32
            )
            total = term if total is None else total + term
        out[...] = total.astype(BF16).reshape(out.shape)

    if not whole:
        return multiply()
    is_last = pl.program_id(0) == pl.num_programs(0) - 1
    pl.when(jnp.logical_not(is_last))(multiply)

    @pl.when(is_last)
    def _():
        out[...] = refs[0][...]


def flip_body(place, grad, after, out):
    out[...] = grad[...].reshape(-1, grad.shape[-1]).T


def lay_body(source, after, target):
    target[...] = source[0]


def wait_body(*refs):
    pass


def add_body(dests, partial_right, partial_left, right, left, *refs):
    out_right, out_left = refs[-2:]
    out_right[...] = (partial_right[...].astype(F32) + right[...].astype(F32)).astype(BF16)
    out_left[...] = (partial_left[...].astype(F32) + left[...].astype(F32)).astype(BF16)


def merge_body(own, *refs):
    out = refs[-1]
    count = out.shape[0] - 1
    out[0] = own[...]
    for k in range(count):
        out[k + 1] = refs[k][...] + refs[count + k][...]


def sum_body(place, partial, right, left, after, *outs):
    total = partial[0, 0].astype(F32) + right[0, 0].astype(F32) + left[0, 0].astype(F32)
    for k, out in enumerate(outs):

        @pl.when(pl.program_id(0) == k)
        def _(out=out):
            out[...] = total.astype(BF16)


def weight_body(grad_t, gated, after, out):
    out[0] = dot(grad_t[...], gated[...]).astype(out.dtype)


def wide(rows, lanes):
    return pl.BlockSpec((rows, lanes), lambda i: (0, i))


def tall(rows, cols):
    return pl.BlockSpec((rows, cols), lambda i: (i, 0))


def deep(count, rows, lanes):
    return pl.BlockSpec((count, rows, lanes), lambda i: (0, 0, i))


def shape(*dims, dtype=BF16):
    return jax.ShapeDtypeStruct(dims, dtype)


def on_device(query, key_in, value_in, gate, out_grad, proj_weight, mr_filter, lr_rate, lr_residue):
    rows, width = query.shape
    groups = width // GROUP
    n_dp, n_ctx, n_tp = (lax.axis_size(a) for a in ("dp", "ctx", "tp"))
    feats = proj_weight.shape[1]
    quarter = width // n_dp
    depth = n_dp * feats
    block = quarter
    steps = width // block
    part = rows // n_tp

    place = jnp.stack([lax.axis_index(a) for a in ("dp", "ctx", "tp")]).astype(jnp.int32)

    def swap(value, axis, k):
        return lax.ppermute(value, axis, [(i, i ^ k) for i in range(lax.axis_size(axis))])

    def shift(value, k, senders=None):
        ends = [(i, i + k) for i in senders or range(n_ctx) if 0 <= i + k < n_ctx]
        return lax.ppermute(value, "ctx", ends)

    def piece(k):
        return pl.BlockSpec((part, feats), lambda j, p: (p[2], j * n_ctx + (p[1] ^ k)))

    weights = lax.all_to_all(proj_weight.reshape(n_dp, quarter, feats), "dp", 0, 0, tiled=True)
    mine = call(
        pack_body, "pack", 0, 4 * part * depth * n_ctx,
        grid_spec=pltpu.PrefetchScalarGridSpec(
            num_scalar_prefetch=1, grid=(n_dp,),
            in_specs=[piece(k) for k in range(n_ctx)],
            out_specs=[pl.BlockSpec((part, feats), lambda j, p: (0, j))] * n_ctx,
        ),
        out_shape=[shape(part, depth)] * n_ctx,
    )(place, *[out_grad] * n_ctx)
    mine = [mine[0]] + [swap(mine[k], "ctx", k) for k in range(1, n_ctx)]
    product = (key_in.astype(F32) * value_in.astype(F32)).astype(BF16)
    rim = shift(product, 1)
    rate = lr_rate.reshape(-1, 1)
    residue = lr_residue.reshape(-1, 1)
    counts = jnp.arange(rows, dtype=F32)[None, :]
    ends_coef = jnp.exp(-rate * (rows - 1 - counts)).astype(BF16)
    starts_coef = jnp.exp(-rate * counts).astype(BF16)
    away = jnp.arange((n_ctx - 1) * rows, dtype=F32)[:, None]
    inside = away % rows
    carry_coef = (residue.T * jnp.exp(-rate.T * (away + 1))).astype(BF16)
    back_coef = (residue.T * jnp.exp(-rate.T * (away + rows - 2 * inside))).astype(BF16)
    kernel = jnp.sum(
        lr_residue[:, :, None] * jnp.exp(-lr_rate[:, :, None] * counts[:, None, :]), axis=1
    )

    def reversed_row(values):
        return jnp.roll(values[:, ::-1], 1, axis=1)

    taps = reversed_row(mr_filter.astype(F32))
    kernel_rev = reversed_row(kernel)
    def local(transposed, table, x, *after):
        return call(
            functools.partial(local_body, transposed),
            "local_t" if transposed else "local",
            2 * rows * 128 * width * 8, rows * width * 6,
            grid=(steps,),
            in_specs=[tall(block // GROUP, rows), wide(rows, block)] + [ANY] * len(after),
            out_specs=wide(rows, block),
            out_shape=shape(rows, width, dtype=F32),
        )(table, x, *after)

    conv_own = local(
        False, taps, product, ends_coef, starts_coef, carry_coef, back_coef, kernel_rev, kernel
    )
    conv, mixed, ends = call(
        conv_body, "conv", 2 * rows * 128 * width * 8, rows * width * 14,
        grid=(steps,),
        in_specs=[wide(rows, block)] * 3 + [tall(block // GROUP, TAPS), tall(block, rows)],
        out_specs=[wide(rows, block), wide(rows, block), wide(ORDER, block)],
        out_shape=[shape(rows, width), shape(rows, width), shape(ORDER, width)],
    )(rim, conv_own, query, taps, ends_coef)
    ends_far = [shift(ends, k) for k in range(1, n_ctx)]


    local_fwd = local(False, kernel_rev, mixed)
    mine = call(
        join_body, "join", 0, 4 * part * depth * n_ctx,
        grid=(n_dp,),
        in_specs=[wide(part, feats)] * n_ctx + [ANY] * 2,
        out_specs=deep(n_ctx, part, feats),
        out_shape=shape(n_ctx, part, depth),
    )(*mine, weights, local_fwd)
    grad = lax.all_gather(mine, ("dp", "tp"), axis=0, tiled=False)
    grad = grad.reshape(n_dp, n_tp, n_ctx, part, depth)
    long_out, gated = call(
        functools.partial(long_body, n_ctx - 1), "long", 2 * rows * 128 * width, rows * width * 10,
        grid=(steps,),
        in_specs=[wide(rows, block), wide((n_ctx - 1) * rows, block), wide(rows, block)] + [wide(ORDER, block)] * (n_ctx - 1) + [ANY],
        out_specs=[wide(rows, block), pl.BlockSpec((1, rows, block), lambda i: (i, 0, 0))],
        out_shape=[shape(rows, width), shape(n_dp, rows, quarter)],
    )(local_fwd, carry_coef, gate, *ends_far, mine)
    gated_far = lax.all_to_all(gated, "dp", 0, 0, tiled=True)
    tokens = n_ctx * n_dp * rows
    last = n_ctx - 1
    from_left, from_right = [], []
    right = left = gated_far
    for t in range(last):
        right = shift(right, 1, range(t, last))
        left = shift(left, -1, range(1, n_ctx - t))
        from_left.append(right)
        from_right.append(left)

    first_dest = jnp.where(place[1] < n_ctx // 2, last, 0)
    chunk = (1, n_dp, rows, quarter)

    def project(dests, *after):
        count = dests.shape[0]
        whole = count > 1
        return call(
            functools.partial(delta_body, whole), "delta",
            2 * max(count - 1, 1) * n_dp * rows * depth * quarter,
            2 * tokens * depth + 2 * depth * quarter + 2 * count * n_dp * rows * quarter,
            grid_spec=pltpu.PrefetchScalarGridSpec(
                num_scalar_prefetch=2, grid=(count,),
                in_specs=[
                    pl.BlockSpec(
                        (n_dp, n_tp, 1, part, depth), lambda i, p, q: (0, 0, p[1] ^ q[i], 0, 0)
                    ),
                    pl.BlockSpec((n_dp, quarter, feats), lambda i, p, q: (0, 0, 0)),
                ] + ([pl.BlockSpec(chunk, lambda i, p, q: (0, 0, 0, 0))] if whole
                     else [ANY] * len(after)),
                out_specs=pl.BlockSpec(
                    chunk, lambda i, p, q: (q[i] if whole else 0, 0, 0, 0)
                ),
            ),
            out_shape=shape(count, n_dp, rows, quarter),
        )(place, dests, grad, weights, *after)

    first = project(first_dest[None], from_left[0], from_right[0])
    others = (first_dest + 1 + jnp.arange(n_ctx, dtype=jnp.int32)) % n_ctx
    partial = project(others.astype(jnp.int32), first)
    grad_t = call(
        flip_body, "flip", 0, 4 * tokens * depth,
        grid_spec=pltpu.PrefetchScalarGridSpec(
            num_scalar_prefetch=1, grid=(n_ctx, n_dp),
            in_specs=[
                pl.BlockSpec(
                    (1, n_tp, 1, part, depth),
                    lambda i, j, p: (j, 0, p[1] ^ ((p[1] + n_ctx - i) % n_ctx), 0, 0),
                ),
                ANY,
            ],
            out_specs=pl.BlockSpec((depth, rows), lambda i, j, p: (0, i * n_dp + j)),
        ),
        out_shape=shape(depth, tokens),
    )(place, grad, partial)
    right, left = shift(first, 1, [0]), shift(first, -1, [last])

    def pick(ahead):
        return pl.BlockSpec(
            (1, 1, rows, quarter), lambda i, q: (q[ahead], i, 0, 0)
        )

    piece_of = pl.BlockSpec((1, 1, rows, quarter), lambda i, q: (0, i, 0, 0))
    for t in range(1, last):
        after = (from_left[t], from_right[t]) + ((grad_t,) if t == last - 1 else ())
        dests = jnp.clip(jnp.stack([last - t + place[1], t - last + place[1]]), 0, last)
        right, left = call(
            add_body, "add", 0, 12 * n_dp * rows * quarter,
            grid_spec=pltpu.PrefetchScalarGridSpec(
                num_scalar_prefetch=1, grid=(n_dp,),
                in_specs=[pick(0), pick(1), piece_of, piece_of] + [ANY] * len(after),
                out_specs=[piece_of] * 2,
            ),
            out_shape=[shape(*chunk)] * 2,
        )(dests, partial, partial, right, left, *after)
        token = right
        right = shift(right, 1, range(t + 1))
        left = shift(left, -1, range(last - t, n_ctx))
    gated_all = call(
        merge_body, "merge", 0, 2 * (2 * n_ctx + last) * n_dp * rows * quarter,
        grid=(n_dp,),
        in_specs=[pl.BlockSpec((1, rows, quarter), lambda i: (i, 0, 0))] * (1 + 2 * last) + [ANY],
        out_specs=pl.BlockSpec((n_ctx, 1, rows, quarter), lambda i: (0, i, 0, 0)),
        out_shape=shape(n_ctx, n_dp, rows, quarter),
    )(gated_far, *from_left, *from_right[::-1], token).reshape(tokens, quarter)
    weight_part = call(
        weight_body, "weight", 2 * tokens * depth * quarter, 2 * tokens * (depth + quarter),
        grid=(n_dp,),
        in_specs=[
            pl.BlockSpec((feats, tokens), lambda i: (i, 0)),
            pl.BlockSpec((tokens, quarter), lambda i: (0, 0)),
            ANY,
        ],
        out_specs=pl.BlockSpec((1, feats, quarter), lambda i: (i, 0, 0)),
        out_shape=shape(n_dp, feats, quarter),
    )(grad_t, gated_all, token)

    delta = call(
        sum_body, "sum", 0, 8 * n_dp * rows * quarter,
        grid_spec=pltpu.PrefetchScalarGridSpec(
            num_scalar_prefetch=1, grid=(n_dp,),
            in_specs=[
                pl.BlockSpec((1, 1, rows, quarter), lambda i, p: (p[1], p[0] ^ i, 0, 0)),
                pl.BlockSpec((1, 1, rows, quarter), lambda i, p: (0, p[0] ^ i, 0, 0)),
                pl.BlockSpec((1, 1, rows, quarter), lambda i, p: (0, p[0] ^ i, 0, 0)),
                ANY,
            ],
            out_specs=[pl.BlockSpec((rows, quarter), lambda i, p: (0, 0))] * n_dp,
        ),
        out_shape=[shape(rows, quarter)] * n_dp,
    )(place, partial, right, left, weight_part)
    held = call(
        wait_body, "hold", 0, 0,
        in_specs=[ANY] * 2, out_specs=ANY,
        out_shape=shape(n_dp, feats, quarter), input_output_aliases={0: 0},
    )(weight_part, delta[0])
    weight_far = lax.all_to_all(held, "dp", 0, 0, tiled=True)
    delta = [delta[0]] + [swap(delta[k], "dp", k) for k in range(1, n_dp)]

    here = pl.BlockSpec((rows, block), lambda i, p: (0, p[0] ^ i))
    seed, starts, gate_grad = call(
        functools.partial(seed_body, n_dp), "seed", 2 * rows * 128 * width, rows * width * 10,
        grid_spec=pltpu.PrefetchScalarGridSpec(
            num_scalar_prefetch=1, grid=(n_dp,),
            in_specs=[pl.BlockSpec((rows, quarter), lambda i, p: (0, 0))] * n_dp
            + [here, here, pl.BlockSpec((block, rows), lambda i, p: (p[0] ^ i, 0))],
            out_specs=[here, pl.BlockSpec((ORDER, block), lambda i, p: (0, p[0] ^ i)), here],
            scratch_shapes=[pltpu.VMEM((rows, block), BF16)],
        ),
        out_shape=[shape(rows, width), shape(ORDER, width), shape(rows, width)],
    )(place, *delta, gate, long_out, starts_coef)
    starts_far = [shift(starts, -k) for k in range(1, n_ctx)]
    local_bwd = local(True, kernel, seed)
    query_grad, conv_grad = call(
        functools.partial(back_body, n_ctx - 1), "back", 2 * rows * 128 * width, rows * width * 12,
        grid=(steps,),
        in_specs=[wide(rows, block), wide((n_ctx - 1) * rows, block)] + [wide(rows, block)] * 2
        + [wide(ORDER, block)] * (n_ctx - 1),
        out_specs=[wide(rows, block)] * 2,
        out_shape=[shape(rows, width)] * 2,
    )(local_bwd, back_coef, conv, query, *starts_far)

    weight_grad = call(
        lay_body, "lay", 0, 4 * feats * width,
        grid=(n_dp,),
        in_specs=[pl.BlockSpec((1, feats, quarter), lambda i: (i, 0, 0)), ANY],
        out_specs=pl.BlockSpec((feats, quarter), lambda i: (0, i)),
        out_shape=shape(feats, width),
    )(weight_far, query_grad)
    return query_grad, conv_grad, gate_grad, weight_grad


def solution(mesh):
    rows = P(("dp", "ctx"), "tp")
    return jax.shard_map(
        on_device,
        mesh=mesh,
        in_specs=(rows, rows, rows, rows, P(("dp", "ctx"), None), P("tp", ("dp", "ctx")),
                  P("tp", None), P("tp", None), P("tp", None)),
        out_specs=(rows, rows, rows, rows),
        check_vma=False,
    )
```

```python
import functools

import jax
import jax.numpy as jnp
from jax import lax
from jax.experimental import pallas as pl
from jax.experimental.pallas import tpu as pltpu
from jax.sharding import PartitionSpec as P

GROUP = 16
TAPS = 128
ORDER = 16
LANES = 128
PER_SLAB = LANES // GROUP
BF16 = jnp.bfloat16
F32 = jnp.float32
VMEM = 50 * 2**20
ANY = pl.BlockSpec(memory_space=pl.ANY)


def call(body, name, flops, nbytes, **kwargs):
    return pl.pallas_call(
        body,
        name=name,
        cost_estimate=pl.CostEstimate(flops=flops, bytes_accessed=nbytes, transcendentals=0),
        compiler_params=pltpu.CompilerParams(vmem_limit_bytes=VMEM),
        **kwargs,
    )


def circulants(rows_ref, base):
    out = []
    for j in range(PER_SLAB):
        row = rows_ref[base + j : base + j + 1, :]
        out.append(
            pltpu.roll(jnp.broadcast_to(row, (LANES, LANES)), 0, 1, stride=1, stride_axis=0)
        )
    return out


def lower_mask():
    t = lax.broadcasted_iota(jnp.int32, (LANES, LANES), 0)
    u = lax.broadcasted_iota(jnp.int32, (LANES, LANES), 1)
    return u <= t


def pick_groups(stacked, rows):
    lane_group = lax.broadcasted_iota(jnp.int32, (rows, LANES), 1) // GROUP
    out = stacked[:rows]
    for j in range(1, PER_SLAB):
        out = jnp.where(lane_group == j, stacked[j * rows : (j + 1) * rows], out)
    return out


def spread_groups(state):
    tiled = jnp.concatenate([state] * PER_SLAB, axis=0)
    row_group = lax.broadcasted_iota(jnp.int32, (LANES, LANES), 0) // ORDER
    lane_group = lax.broadcasted_iota(jnp.int32, (LANES, LANES), 1) // GROUP
    return jnp.where(row_group == lane_group, tiled, jnp.zeros_like(tiled))


def dot(a, b):
    return jnp.dot(a, b, preferred_element_type=F32)


def conv_body(rim, own_part, query, taps, ends_coef, *refs):
    conv, mixed, ends = refs[-3:]
    lower = lower_mask()
    for s in range(rim.shape[1] // LANES):
        cols = slice(s * LANES, (s + 1) * LANES)
        blocks = [
            jnp.where(lower, jnp.zeros_like(circ), circ).astype(BF16)
            for circ in circulants(taps, s * PER_SLAB)
        ]
        out = own_part[:, cols] + pick_groups(
            dot(jnp.concatenate(blocks, axis=0), rim[:, cols]), LANES
        )
        conv[:, cols] = out.astype(conv.dtype)
        mixed[:, cols] = (query[:, cols].astype(F32) * out).astype(BF16)
    for s in range(rim.shape[1] // LANES):
        cols = slice(s * LANES, (s + 1) * LANES)
        ends[:, cols] = pick_groups(
            dot(ends_coef[s * LANES : (s + 1) * LANES, :], mixed[:, cols]), ORDER
        ).astype(ends.dtype)


def local_body(transposed, rows, x, *refs):
    out = refs[-1]
    lower = lower_mask()
    keep = ~lower | (lax.broadcasted_iota(jnp.int32, (LANES, LANES), 0)
                     == lax.broadcasted_iota(jnp.int32, (LANES, LANES), 1)) if transposed else lower
    for s in range(x.shape[1] // LANES):
        cols = slice(s * LANES, (s + 1) * LANES)
        blocks = [
            jnp.where(keep, circ, jnp.zeros_like(circ)).astype(BF16)
            for circ in circulants(rows, s * PER_SLAB)
        ]
        out[:, cols] = pick_groups(
            dot(jnp.concatenate(blocks, axis=0), x[:, cols]), LANES
        ).astype(out.dtype)


def carried(states, coef, cols):
    wide_states = jnp.concatenate([spread_groups(ref[:, cols]) for ref in states], axis=0)
    count = len(states)
    rows = coef.shape[0] // count
    parts = [coef[k * rows : (k + 1) * rows, cols] for k in range(count)]
    return dot(jnp.concatenate(parts, axis=1), wide_states)


def long_body(count, local, coef, gate, *refs):
    states, (long_out, gated) = refs[:count], refs[-2:]
    for s in range(local.shape[1] // LANES):
        cols = slice(s * LANES, (s + 1) * LANES)
        out = local[:, cols].astype(F32) + carried(states, coef, cols)
        long_out[:, cols] = out.astype(long_out.dtype)
        gated[0, :, cols] = (gate[:, cols].astype(F32) * out).astype(BF16)


def seed_body(count, place, *refs):
    sources = refs[:count]
    gate, long_out, starts_coef, seed, starts, gate_grad, delta = refs[count:]
    for k, source in enumerate(sources):

        @pl.when(pl.program_id(0) == k)
        def _(source=source):
            delta[...] = source[...]

    for s in range(gate.shape[1] // LANES):
        cols = slice(s * LANES, (s + 1) * LANES)
        out = delta[:, cols].astype(F32)
        seed[:, cols] = (out * gate[:, cols].astype(F32)).astype(BF16)
        gate_grad[:, cols] = (out * long_out[:, cols].astype(F32)).astype(BF16)
    for s in range(gate.shape[1] // LANES):
        cols = slice(s * LANES, (s + 1) * LANES)
        starts[:, cols] = pick_groups(
            dot(starts_coef[s * LANES : (s + 1) * LANES, :], seed[:, cols]), ORDER
        ).astype(starts.dtype)


def back_body(count, local, coef, conv, query, *refs):
    states, (query_grad, conv_grad) = refs[:count], refs[-2:]
    for s in range(local.shape[1] // LANES):
        cols = slice(s * LANES, (s + 1) * LANES)
        out = local[:, cols].astype(F32) + carried(states, coef, cols)
        query_grad[:, cols] = (out * conv[:, cols].astype(F32)).astype(BF16)
        conv_grad[:, cols] = (out * query[:, cols].astype(F32)).astype(BF16)


def pack_body(place, *refs):
    count = len(refs) // 2
    for source, target in zip(refs[:count], refs[-count:]):
        target[...] = source[...]


def join_body(*refs):
    out = refs[-1]
    for k in range(out.shape[0]):
        out[k] = refs[k][...]


def delta_body(whole, place, dest, grad, weights, *refs):
    depth, out = weights.shape[2], refs[-1]

    def multiply():
        total = None
        for k in range(weights.shape[0]):
            rows = grad[:, :, :, :, k * depth : (k + 1) * depth].reshape(-1, depth)
            term = lax.dot_general(
                rows, weights[k], (((1,), (1,)), ((), ())), preferred_element_type=F32
            )
            total = term if total is None else total + term
        out[...] = total.astype(BF16).reshape(out.shape)

    if not whole:
        return multiply()
    is_last = pl.program_id(0) == pl.num_programs(0) - 1
    pl.when(jnp.logical_not(is_last))(multiply)

    @pl.when(is_last)
    def _():
        out[...] = refs[0][...]


def flip_body(place, grad, after, out):
    out[...] = grad[...].reshape(-1, grad.shape[-1]).T


def lay_body(source, after, target):
    target[...] = source[0]


def wait_body(*refs):
    pass


def add_body(dests, partial_right, partial_left, right, left, *refs):
    out_right, out_left = refs[-2:]
    out_right[...] = (partial_right[...].astype(F32) + right[...].astype(F32)).astype(BF16)
    out_left[...] = (partial_left[...].astype(F32) + left[...].astype(F32)).astype(BF16)


def merge_body(own, *refs):
    out = refs[-1]
    count = out.shape[0] - 1
    out[0] = own[...]
    for k in range(count):
        out[k + 1] = refs[k][...] + refs[count + k][...]


def sum_body(place, partial, right, left, after, *outs):
    total = partial[0, 0].astype(F32) + right[0, 0].astype(F32) + left[0, 0].astype(F32)
    for k, out in enumerate(outs):

        @pl.when(pl.program_id(0) == k)
        def _(out=out):
            out[...] = total.astype(BF16)


def weight_body(grad_t, gated, after, out):
    out[0] = dot(grad_t[...], gated[...]).astype(out.dtype)


def wide(rows, lanes):
    return pl.BlockSpec((rows, lanes), lambda i: (0, i))


def tall(rows, cols):
    return pl.BlockSpec((rows, cols), lambda i: (i, 0))


def deep(count, rows, lanes):
    return pl.BlockSpec((count, rows, lanes), lambda i: (0, 0, i))


def shape(*dims, dtype=BF16):
    return jax.ShapeDtypeStruct(dims, dtype)


def on_device(query, key_in, value_in, gate, out_grad, proj_weight, mr_filter, lr_rate, lr_residue):
    rows, width = query.shape
    groups = width // GROUP
    n_dp, n_ctx, n_tp = (lax.axis_size(a) for a in ("dp", "ctx", "tp"))
    feats = proj_weight.shape[1]
    quarter = width // n_dp
    depth = n_dp * feats
    block = quarter
    steps = width // block
    part = rows // n_tp

    place = jnp.stack([lax.axis_index(a) for a in ("dp", "ctx", "tp")]).astype(jnp.int32)

    def swap(value, axis, k):
        return lax.ppermute(value, axis, [(i, i ^ k) for i in range(lax.axis_size(axis))])

    def shift(value, k, senders=None):
        ends = [(i, i + k) for i in senders or range(n_ctx) if 0 <= i + k < n_ctx]
        return lax.ppermute(value, "ctx", ends)

    def piece(k):
        return pl.BlockSpec((part, feats), lambda j, p: (p[2], j * n_ctx + (p[1] ^ k)))

    weights = lax.all_to_all(proj_weight.reshape(n_dp, quarter, feats), "dp", 0, 0, tiled=True)
    mine = call(
        pack_body, "pack", 0, 4 * part * depth * n_ctx,
        grid_spec=pltpu.PrefetchScalarGridSpec(
            num_scalar_prefetch=1, grid=(n_dp,),
            in_specs=[piece(k) for k in range(n_ctx)],
            out_specs=[pl.BlockSpec((part, feats), lambda j, p: (0, j))] * n_ctx,
        ),
        out_shape=[shape(part, depth)] * n_ctx,
    )(place, *[out_grad] * n_ctx)
    mine = [mine[0]] + [swap(mine[k], "ctx", k) for k in range(1, n_ctx)]
    product = (key_in.astype(F32) * value_in.astype(F32)).astype(BF16)
    rim = shift(product, 1)
    rate = lr_rate.reshape(-1, 1)
    residue = lr_residue.reshape(-1, 1)
    counts = jnp.arange(rows, dtype=F32)[None, :]
    ends_coef = jnp.exp(-rate * (rows - 1 - counts)).astype(BF16)
    starts_coef = jnp.exp(-rate * counts).astype(BF16)
    away = jnp.arange((n_ctx - 1) * rows, dtype=F32)[:, None]
    inside = away % rows
    carry_coef = (residue.T * jnp.exp(-rate.T * (away + 1))).astype(BF16)
    back_coef = (residue.T * jnp.exp(-rate.T * (away + rows - 2 * inside))).astype(BF16)
    kernel = jnp.sum(
        lr_residue[:, :, None] * jnp.exp(-lr_rate[:, :, None] * counts[:, None, :]), axis=1
    )

    def reversed_row(values):
        return jnp.roll(values[:, ::-1], 1, axis=1)

    taps = reversed_row(mr_filter.astype(F32))
    kernel_rev = reversed_row(kernel)
    def local(transposed, table, x, *after):
        return call(
            functools.partial(local_body, transposed),
            "local_t" if transposed else "local",
            2 * rows * 128 * width * 8, rows * width * 6,
            grid=(steps,),
            in_specs=[tall(block // GROUP, rows), wide(rows, block)] + [ANY] * len(after),
            out_specs=wide(rows, block),
            out_shape=shape(rows, width, dtype=F32),
        )(table, x, *after)

    conv_own = local(
        False, taps, product, ends_coef, starts_coef, carry_coef, back_coef, kernel_rev, kernel
    )
    conv, mixed, ends = call(
        conv_body, "conv", 2 * rows * 128 * width * 8, rows * width * 14,
        grid=(steps,),
        in_specs=[wide(rows, block)] * 3 + [tall(block // GROUP, TAPS), tall(block, rows)],
        out_specs=[wide(rows, block), wide(rows, block), wide(ORDER, block)],
        out_shape=[shape(rows, width), shape(rows, width), shape(ORDER, width)],
    )(rim, conv_own, query, taps, ends_coef)
    ends_far = [shift(ends, k) for k in range(1, n_ctx)]


    local_fwd = local(False, kernel_rev, mixed)
    mine = call(
        join_body, "join", 0, 4 * part * depth * n_ctx,
        grid=(n_dp,),
        in_specs=[wide(part, feats)] * n_ctx + [ANY] * 2,
        out_specs=deep(n_ctx, part, feats),
        out_shape=shape(n_ctx, part, depth),
    )(*mine, weights, local_fwd)
    grad = lax.all_gather(mine, ("dp", "tp"), axis=0, tiled=False)
    grad = grad.reshape(n_dp, n_tp, n_ctx, part, depth)
    long_out, gated = call(
        functools.partial(long_body, n_ctx - 1), "long", 2 * rows * 128 * width, rows * width * 10,
        grid=(steps,),
        in_specs=[wide(rows, block), wide((n_ctx - 1) * rows, block), wide(rows, block)] + [wide(ORDER, block)] * (n_ctx - 1) + [ANY],
        out_specs=[wide(rows, block), pl.BlockSpec((1, rows, block), lambda i: (i, 0, 0))],
        out_shape=[shape(rows, width), shape(n_dp, rows, quarter)],
    )(local_fwd, carry_coef, gate, *ends_far, mine)
    gated_far = lax.all_to_all(gated, "dp", 0, 0, tiled=True)
    tokens = n_ctx * n_dp * rows
    last = n_ctx - 1
    from_left, from_right = [], []
    right = left = gated_far
    for t in range(last):
        right = shift(right, 1, range(t, last))
        left = shift(left, -1, range(1, n_ctx - t))
        from_left.append(right)
        from_right.append(left)

    first_dest = jnp.where(place[1] < n_ctx // 2, last, 0)
    chunk = (1, n_dp, rows, quarter)

    def project(dests, *after):
        count = dests.shape[0]
        whole = count > 1
        return call(
            functools.partial(delta_body, whole), "delta",
            2 * max(count - 1, 1) * n_dp * rows * depth * quarter,
            2 * tokens * depth + 2 * depth * quarter + 2 * count * n_dp * rows * quarter,
            grid_spec=pltpu.PrefetchScalarGridSpec(
                num_scalar_prefetch=2, grid=(count,),
                in_specs=[
                    pl.BlockSpec(
                        (n_dp, n_tp, 1, part, depth), lambda i, p, q: (0, 0, p[1] ^ q[i], 0, 0)
                    ),
                    pl.BlockSpec((n_dp, quarter, feats), lambda i, p, q: (0, 0, 0)),
                ] + ([pl.BlockSpec(chunk, lambda i, p, q: (0, 0, 0, 0))] if whole
                     else [ANY] * len(after)),
                out_specs=pl.BlockSpec(
                    chunk, lambda i, p, q: (q[i] if whole else 0, 0, 0, 0)
                ),
            ),
            out_shape=shape(count, n_dp, rows, quarter),
        )(place, dests, grad, weights, *after)

    first = project(first_dest[None], from_left[0], from_right[0])
    others = (first_dest + 1 + jnp.arange(n_ctx, dtype=jnp.int32)) % n_ctx
    partial = project(others.astype(jnp.int32), first)
    grad_t = call(
        flip_body, "flip", 0, 4 * tokens * depth,
        grid_spec=pltpu.PrefetchScalarGridSpec(
            num_scalar_prefetch=1, grid=(n_ctx, n_dp),
            in_specs=[
                pl.BlockSpec(
                    (1, n_tp, 1, part, depth),
                    lambda i, j, p: (j, 0, p[1] ^ ((p[1] + n_ctx - i) % n_ctx), 0, 0),
                ),
                ANY,
            ],
            out_specs=pl.BlockSpec((depth, rows), lambda i, j, p: (0, i * n_dp + j)),
        ),
        out_shape=shape(depth, tokens),
    )(place, grad, partial)
    right, left = shift(first, 1, [0]), shift(first, -1, [last])

    def pick(ahead):
        return pl.BlockSpec(
            (1, 1, rows, quarter), lambda i, q: (q[ahead], i, 0, 0)
        )

    piece_of = pl.BlockSpec((1, 1, rows, quarter), lambda i, q: (0, i, 0, 0))
    for t in range(1, last):
        after = (from_left[t], from_right[t]) + ((grad_t,) if t == last - 1 else ())
        dests = jnp.clip(jnp.stack([last - t + place[1], t - last + place[1]]), 0, last)
        right, left = call(
            add_body, "add", 0, 12 * n_dp * rows * quarter,
            grid_spec=pltpu.PrefetchScalarGridSpec(
                num_scalar_prefetch=1, grid=(n_dp,),
                in_specs=[pick(0), pick(1), piece_of, piece_of] + [ANY] * len(after),
                out_specs=[piece_of] * 2,
            ),
            out_shape=[shape(*chunk)] * 2,
        )(dests, partial, partial, right, left, *after)
        token = right
        right = shift(right, 1, range(t + 1))
        left = shift(left, -1, range(last - t, n_ctx))
    gated_all = call(
        merge_body, "merge", 0, 2 * (2 * n_ctx + last) * n_dp * rows * quarter,
        grid=(n_dp,),
        in_specs=[pl.BlockSpec((1, rows, quarter), lambda i: (i, 0, 0))] * (1 + 2 * last) + [ANY],
        out_specs=pl.BlockSpec((n_ctx, 1, rows, quarter), lambda i: (0, i, 0, 0)),
        out_shape=shape(n_ctx, n_dp, rows, quarter),
    )(gated_far, *from_left, *from_right[::-1], token).reshape(tokens, quarter)
    weight_part = call(
        weight_body, "weight", 2 * tokens * depth * quarter, 2 * tokens * (depth + quarter),
        grid=(n_dp,),
        in_specs=[
            pl.BlockSpec((feats, tokens), lambda i: (i, 0)),
            pl.BlockSpec((tokens, quarter), lambda i: (0, 0)),
            ANY,
        ],
        out_specs=pl.BlockSpec((1, feats, quarter), lambda i: (i, 0, 0)),
        out_shape=shape(n_dp, feats, quarter),
    )(grad_t, gated_all, token)

    delta = call(
        sum_body, "sum", 0, 8 * n_dp * rows * quarter,
        grid_spec=pltpu.PrefetchScalarGridSpec(
            num_scalar_prefetch=1, grid=(n_dp,),
            in_specs=[
                pl.BlockSpec((1, 1, rows, quarter), lambda i, p: (p[1], p[0] ^ i, 0, 0)),
                pl.BlockSpec((1, 1, rows, quarter), lambda i, p: (0, p[0] ^ i, 0, 0)),
                pl.BlockSpec((1, 1, rows, quarter), lambda i, p: (0, p[0] ^ i, 0, 0)),
                ANY,
            ],
            out_specs=[pl.BlockSpec((rows, quarter), lambda i, p: (0, 0))] * n_dp,
        ),
        out_shape=[shape(rows, quarter)] * n_dp,
    )(place, partial, right, left, weight_part)
    delta = [delta[0]] + [swap(delta[k], "dp", k) for k in range(1, n_dp)]
    held = call(
        wait_body, "hold", 0, 0,
        in_specs=[ANY] * 2, out_specs=ANY,
        out_shape=shape(n_dp, feats, quarter), input_output_aliases={0: 0},
    )(weight_part, delta[1])
    weight_far = lax.all_to_all(held, "dp", 0, 0, tiled=True)

    here = pl.BlockSpec((rows, block), lambda i, p: (0, p[0] ^ i))
    seed, starts, gate_grad = call(
        functools.partial(seed_body, n_dp), "seed", 2 * rows * 128 * width, rows * width * 10,
        grid_spec=pltpu.PrefetchScalarGridSpec(
            num_scalar_prefetch=1, grid=(n_dp,),
            in_specs=[pl.BlockSpec((rows, quarter), lambda i, p: (0, 0))] * n_dp
            + [here, here, pl.BlockSpec((block, rows), lambda i, p: (p[0] ^ i, 0))],
            out_specs=[here, pl.BlockSpec((ORDER, block), lambda i, p: (0, p[0] ^ i)), here],
            scratch_shapes=[pltpu.VMEM((rows, block), BF16)],
        ),
        out_shape=[shape(rows, width), shape(ORDER, width), shape(rows, width)],
    )(place, *delta, gate, long_out, starts_coef)
    starts_far = [shift(starts, -k) for k in range(1, n_ctx)]
    local_bwd = local(True, kernel, seed)
    query_grad, conv_grad = call(
        functools.partial(back_body, n_ctx - 1), "back", 2 * rows * 128 * width, rows * width * 12,
        grid=(steps,),
        in_specs=[wide(rows, block), wide((n_ctx - 1) * rows, block)] + [wide(rows, block)] * 2
        + [wide(ORDER, block)] * (n_ctx - 1),
        out_specs=[wide(rows, block)] * 2,
        out_shape=[shape(rows, width)] * 2,
    )(local_bwd, back_coef, conv, query, *starts_far)

    weight_grad = call(
        lay_body, "lay", 0, 4 * feats * width,
        grid=(n_dp,),
        in_specs=[pl.BlockSpec((1, feats, quarter), lambda i: (i, 0, 0)), ANY],
        out_specs=pl.BlockSpec((feats, quarter), lambda i: (0, i)),
        out_shape=shape(feats, width),
    )(weight_far, query_grad)
    return query_grad, conv_grad, gate_grad, weight_grad


def solution(mesh):
    rows = P(("dp", "ctx"), "tp")
    return jax.shard_map(
        on_device,
        mesh=mesh,
        in_specs=(rows, rows, rows, rows, P(("dp", "ctx"), None), P("tp", ("dp", "ctx")),
                  P("tp", None), P("tp", None), P("tp", None)),
        out_specs=(rows, rows, rows, rows),
        check_vma=False,
    )
```

```python
import functools

import jax
import jax.numpy as jnp
from jax import lax
from jax.experimental import pallas as pl
from jax.experimental.pallas import tpu as pltpu
from jax.sharding import PartitionSpec as P

GROUP = 16
TAPS = 128
ORDER = 16
LANES = 128
PER_SLAB = LANES // GROUP
BF16 = jnp.bfloat16
F32 = jnp.float32
VMEM = 50 * 2**20
ANY = pl.BlockSpec(memory_space=pl.ANY)


def call(body, name, flops, nbytes, **kwargs):
    return pl.pallas_call(
        body,
        name=name,
        cost_estimate=pl.CostEstimate(flops=flops, bytes_accessed=nbytes, transcendentals=0),
        compiler_params=pltpu.CompilerParams(vmem_limit_bytes=VMEM),
        **kwargs,
    )


def circulants(rows_ref, base):
    out = []
    for j in range(PER_SLAB):
        row = rows_ref[base + j : base + j + 1, :]
        out.append(
            pltpu.roll(jnp.broadcast_to(row, (LANES, LANES)), 0, 1, stride=1, stride_axis=0)
        )
    return out


def lower_mask():
    t = lax.broadcasted_iota(jnp.int32, (LANES, LANES), 0)
    u = lax.broadcasted_iota(jnp.int32, (LANES, LANES), 1)
    return u <= t


def pick_groups(stacked, rows):
    lane_group = lax.broadcasted_iota(jnp.int32, (rows, LANES), 1) // GROUP
    out = stacked[:rows]
    for j in range(1, PER_SLAB):
        out = jnp.where(lane_group == j, stacked[j * rows : (j + 1) * rows], out)
    return out


def spread_groups(state):
    tiled = jnp.concatenate([state] * PER_SLAB, axis=0)
    row_group = lax.broadcasted_iota(jnp.int32, (LANES, LANES), 0) // ORDER
    lane_group = lax.broadcasted_iota(jnp.int32, (LANES, LANES), 1) // GROUP
    return jnp.where(row_group == lane_group, tiled, jnp.zeros_like(tiled))


def dot(a, b):
    return jnp.dot(a, b, preferred_element_type=F32)


def conv_body(rim, own_part, query, taps, ends_coef, *refs):
    conv, mixed, ends = refs[-3:]
    lower = lower_mask()
    for s in range(rim.shape[1] // LANES):
        cols = slice(s * LANES, (s + 1) * LANES)
        blocks = [
            jnp.where(lower, jnp.zeros_like(circ), circ).astype(BF16)
            for circ in circulants(taps, s * PER_SLAB)
        ]
        out = own_part[:, cols] + pick_groups(
            dot(jnp.concatenate(blocks, axis=0), rim[:, cols]), LANES
        )
        conv[:, cols] = out.astype(conv.dtype)
        mixed[:, cols] = (query[:, cols].astype(F32) * out).astype(BF16)
    for s in range(rim.shape[1] // LANES):
        cols = slice(s * LANES, (s + 1) * LANES)
        ends[:, cols] = pick_groups(
            dot(ends_coef[s * LANES : (s + 1) * LANES, :], mixed[:, cols]), ORDER
        ).astype(ends.dtype)


def local_body(transposed, rows, x, *refs):
    out = refs[-1]
    lower = lower_mask()
    keep = ~lower | (lax.broadcasted_iota(jnp.int32, (LANES, LANES), 0)
                     == lax.broadcasted_iota(jnp.int32, (LANES, LANES), 1)) if transposed else lower
    for s in range(x.shape[1] // LANES):
        cols = slice(s * LANES, (s + 1) * LANES)
        blocks = [
            jnp.where(keep, circ, jnp.zeros_like(circ)).astype(BF16)
            for circ in circulants(rows, s * PER_SLAB)
        ]
        out[:, cols] = pick_groups(
            dot(jnp.concatenate(blocks, axis=0), x[:, cols]), LANES
        ).astype(out.dtype)


def carried(states, coef, cols):
    wide_states = jnp.concatenate([spread_groups(ref[:, cols]) for ref in states], axis=0)
    count = len(states)
    rows = coef.shape[0] // count
    parts = [coef[k * rows : (k + 1) * rows, cols] for k in range(count)]
    return dot(jnp.concatenate(parts, axis=1), wide_states)


def long_body(count, local, coef, gate, *refs):
    states, (long_out, gated) = refs[:count], refs[-2:]
    for s in range(local.shape[1] // LANES):
        cols = slice(s * LANES, (s + 1) * LANES)
        out = local[:, cols].astype(F32) + carried(states, coef, cols)
        long_out[:, cols] = out.astype(long_out.dtype)
        gated[0, :, cols] = (gate[:, cols].astype(F32) * out).astype(BF16)


def seed_body(count, place, *refs):
    sources = refs[:count]
    gate, long_out, starts_coef, seed, starts, gate_grad, delta = refs[count:]
    for k, source in enumerate(sources):

        @pl.when(pl.program_id(0) == k)
        def _(source=source):
            delta[...] = source[...]

    for s in range(gate.shape[1] // LANES):
        cols = slice(s * LANES, (s + 1) * LANES)
        out = delta[:, cols].astype(F32)
        seed[:, cols] = (out * gate[:, cols].astype(F32)).astype(BF16)
        gate_grad[:, cols] = (out * long_out[:, cols].astype(F32)).astype(BF16)
    for s in range(gate.shape[1] // LANES):
        cols = slice(s * LANES, (s + 1) * LANES)
        starts[:, cols] = pick_groups(
            dot(starts_coef[s * LANES : (s + 1) * LANES, :], seed[:, cols]), ORDER
        ).astype(starts.dtype)


def back_body(count, local, coef, conv, query, *refs):
    states, (query_grad, conv_grad) = refs[:count], refs[-2:]
    for s in range(local.shape[1] // LANES):
        cols = slice(s * LANES, (s + 1) * LANES)
        out = local[:, cols].astype(F32) + carried(states, coef, cols)
        query_grad[:, cols] = (out * conv[:, cols].astype(F32)).astype(BF16)
        conv_grad[:, cols] = (out * query[:, cols].astype(F32)).astype(BF16)


def pack_body(place, *refs):
    count = len(refs) // 2
    for source, target in zip(refs[:count], refs[-count:]):
        target[...] = source[...]


def join_body(*refs):
    out = refs[-1]
    for k in range(out.shape[0]):
        out[k] = refs[k][...]


def delta_body(whole, place, dest, grad, weights, *refs):
    depth, out = weights.shape[2], refs[-1]

    def multiply():
        total = None
        for k in range(weights.shape[0]):
            rows = grad[:, :, :, :, k * depth : (k + 1) * depth].reshape(-1, depth)
            term = lax.dot_general(
                rows, weights[k], (((1,), (1,)), ((), ())), preferred_element_type=F32
            )
            total = term if total is None else total + term
        out[...] = total.astype(BF16).reshape(out.shape)

    if not whole:
        return multiply()
    is_last = pl.program_id(0) == pl.num_programs(0) - 1
    pl.when(jnp.logical_not(is_last))(multiply)

    @pl.when(is_last)
    def _():
        out[...] = refs[0][...]


def flip_body(place, grad, after, out):
    out[...] = grad[...].reshape(-1, grad.shape[-1]).T


def lay_body(source, after, target):
    target[...] = source[0]


def wait_body(*refs):
    pass


def add_body(dests, partial_right, partial_left, right, left, *refs):
    out_right, out_left = refs[-2:]
    out_right[...] = (partial_right[...].astype(F32) + right[...].astype(F32)).astype(BF16)
    out_left[...] = (partial_left[...].astype(F32) + left[...].astype(F32)).astype(BF16)


def merge_body(own, *refs):
    out = refs[-1]
    count = out.shape[0] - 1
    out[0] = own[...]
    for k in range(count):
        out[k + 1] = refs[k][...] + refs[count + k][...]


def sum_body(place, partial, right, left, after, *outs):
    total = partial[0, 0].astype(F32) + right[0, 0].astype(F32) + left[0, 0].astype(F32)
    for k, out in enumerate(outs):

        @pl.when(pl.program_id(0) == k)
        def _(out=out):
            out[...] = total.astype(BF16)


def weight_body(grad_t, gated, after, out):
    out[0] = dot(grad_t[...], gated[...]).astype(out.dtype)


def wide(rows, lanes):
    return pl.BlockSpec((rows, lanes), lambda i: (0, i))


def tall(rows, cols):
    return pl.BlockSpec((rows, cols), lambda i: (i, 0))


def deep(count, rows, lanes):
    return pl.BlockSpec((count, rows, lanes), lambda i: (0, 0, i))


def shape(*dims, dtype=BF16):
    return jax.ShapeDtypeStruct(dims, dtype)


def on_device(query, key_in, value_in, gate, out_grad, proj_weight, mr_filter, lr_rate, lr_residue):
    rows, width = query.shape
    groups = width // GROUP
    n_dp, n_ctx, n_tp = (lax.axis_size(a) for a in ("dp", "ctx", "tp"))
    feats = proj_weight.shape[1]
    quarter = width // n_dp
    depth = n_dp * feats
    block = quarter
    steps = width // block
    part = rows // n_tp

    place = jnp.stack([lax.axis_index(a) for a in ("dp", "ctx", "tp")]).astype(jnp.int32)

    def swap(value, axis, k):
        return lax.ppermute(value, axis, [(i, i ^ k) for i in range(lax.axis_size(axis))])

    def shift(value, k, senders=None):
        ends = [(i, i + k) for i in senders or range(n_ctx) if 0 <= i + k < n_ctx]
        return lax.ppermute(value, "ctx", ends)

    def piece(k):
        return pl.BlockSpec((part, feats), lambda j, p: (p[2], j * n_ctx + (p[1] ^ k)))

    weights = lax.all_to_all(proj_weight.reshape(n_dp, quarter, feats), "dp", 0, 0, tiled=True)
    mine = call(
        pack_body, "pack", 0, 4 * part * depth * n_ctx,
        grid_spec=pltpu.PrefetchScalarGridSpec(
            num_scalar_prefetch=1, grid=(n_dp,),
            in_specs=[piece(k) for k in range(n_ctx)],
            out_specs=[pl.BlockSpec((part, feats), lambda j, p: (0, j))] * n_ctx,
        ),
        out_shape=[shape(part, depth)] * n_ctx,
    )(place, *[out_grad] * n_ctx)
    mine = [mine[0]] + [swap(mine[k], "ctx", k) for k in range(1, n_ctx)]
    product = (key_in.astype(F32) * value_in.astype(F32)).astype(BF16)
    rim = shift(product, 1)
    rate = lr_rate.reshape(-1, 1)
    residue = lr_residue.reshape(-1, 1)
    counts = jnp.arange(rows, dtype=F32)[None, :]
    ends_coef = jnp.exp(-rate * (rows - 1 - counts)).astype(BF16)
    starts_coef = jnp.exp(-rate * counts).astype(BF16)
    away = jnp.arange((n_ctx - 1) * rows, dtype=F32)[:, None]
    inside = away % rows
    carry_coef = (residue.T * jnp.exp(-rate.T * (away + 1))).astype(BF16)
    back_coef = (residue.T * jnp.exp(-rate.T * (away + rows - 2 * inside))).astype(BF16)
    kernel = jnp.sum(
        lr_residue[:, :, None] * jnp.exp(-lr_rate[:, :, None] * counts[:, None, :]), axis=1
    )

    def reversed_row(values):
        return jnp.roll(values[:, ::-1], 1, axis=1)

    taps = reversed_row(mr_filter.astype(F32))
    kernel_rev = reversed_row(kernel)
    def local(transposed, table, x, *after):
        return call(
            functools.partial(local_body, transposed),
            "local_t" if transposed else "local",
            2 * rows * 128 * width * 8, rows * width * 6,
            grid=(steps,),
            in_specs=[tall(block // GROUP, rows), wide(rows, block)] + [ANY] * len(after),
            out_specs=wide(rows, block),
            out_shape=shape(rows, width, dtype=F32),
        )(table, x, *after)

    conv_own = local(
        False, taps, product, ends_coef, starts_coef, carry_coef, back_coef, kernel_rev, kernel
    )
    conv, mixed, ends = call(
        conv_body, "conv", 2 * rows * 128 * width * 8, rows * width * 14,
        grid=(steps,),
        in_specs=[wide(rows, block)] * 3 + [tall(block // GROUP, TAPS), tall(block, rows)],
        out_specs=[wide(rows, block), wide(rows, block), wide(ORDER, block)],
        out_shape=[shape(rows, width), shape(rows, width), shape(ORDER, width)],
    )(rim, conv_own, query, taps, ends_coef)
    ends_far = [shift(ends, k) for k in range(1, n_ctx)]


    local_fwd = local(False, kernel_rev, mixed)
    mine = call(
        join_body, "join", 0, 4 * part * depth * n_ctx,
        grid=(n_dp,),
        in_specs=[wide(part, feats)] * n_ctx + [ANY] * 2,
        out_specs=deep(n_ctx, part, feats),
        out_shape=shape(n_ctx, part, depth),
    )(*mine, weights, local_fwd)
    grad = lax.all_gather(mine, ("dp", "tp"), axis=0, tiled=False)
    grad = grad.reshape(n_dp, n_tp, n_ctx, part, depth)
    long_out, gated = call(
        functools.partial(long_body, n_ctx - 1), "long", 2 * rows * 128 * width, rows * width * 10,
        grid=(steps,),
        in_specs=[wide(rows, block), wide((n_ctx - 1) * rows, block), wide(rows, block)] + [wide(ORDER, block)] * (n_ctx - 1) + [ANY],
        out_specs=[wide(rows, block), pl.BlockSpec((1, rows, block), lambda i: (i, 0, 0))],
        out_shape=[shape(rows, width), shape(n_dp, rows, quarter)],
    )(local_fwd, carry_coef, gate, *ends_far, mine)
    gated_far = lax.all_to_all(gated, "dp", 0, 0, tiled=True)
    tokens = n_ctx * n_dp * rows
    last = n_ctx - 1
    from_left, from_right = [], []
    right = left = gated_far
    for t in range(last):
        right = shift(right, 1, range(t, last))
        left = shift(left, -1, range(1, n_ctx - t))
        from_left.append(right)
        from_right.append(left)

    first_dest = jnp.where(place[1] < n_ctx // 2, last, 0)
    chunk = (1, n_dp, rows, quarter)

    def project(dests, *after):
        count = dests.shape[0]
        whole = count > 1
        return call(
            functools.partial(delta_body, whole), "delta",
            2 * max(count - 1, 1) * n_dp * rows * depth * quarter,
            2 * tokens * depth + 2 * depth * quarter + 2 * count * n_dp * rows * quarter,
            grid_spec=pltpu.PrefetchScalarGridSpec(
                num_scalar_prefetch=2, grid=(count,),
                in_specs=[
                    pl.BlockSpec(
                        (n_dp, n_tp, 1, part, depth), lambda i, p, q: (0, 0, p[1] ^ q[i], 0, 0)
                    ),
                    pl.BlockSpec((n_dp, quarter, feats), lambda i, p, q: (0, 0, 0)),
                ] + ([pl.BlockSpec(chunk, lambda i, p, q: (0, 0, 0, 0))] if whole
                     else [ANY] * len(after)),
                out_specs=pl.BlockSpec(
                    chunk, lambda i, p, q: (q[i] if whole else 0, 0, 0, 0)
                ),
            ),
            out_shape=shape(count, n_dp, rows, quarter),
        )(place, dests, grad, weights, *after)

    first = project(first_dest[None], from_left[0], from_right[0])
    others = (first_dest + 1 + jnp.arange(n_ctx, dtype=jnp.int32)) % n_ctx
    partial = project(others.astype(jnp.int32), first)
    grad_t = call(
        flip_body, "flip", 0, 4 * tokens * depth,
        grid_spec=pltpu.PrefetchScalarGridSpec(
            num_scalar_prefetch=1, grid=(n_ctx, n_dp),
            in_specs=[
                pl.BlockSpec(
                    (1, n_tp, 1, part, depth),
                    lambda i, j, p: (j, 0, p[1] ^ ((p[1] + n_ctx - i) % n_ctx), 0, 0),
                ),
                ANY,
            ],
            out_specs=pl.BlockSpec((depth, rows), lambda i, j, p: (0, i * n_dp + j)),
        ),
        out_shape=shape(depth, tokens),
    )(place, grad, partial)
    right, left = shift(first, 1, [0]), shift(first, -1, [last])

    def pick(ahead):
        return pl.BlockSpec(
            (1, 1, rows, quarter), lambda i, q: (q[ahead], i, 0, 0)
        )

    piece_of = pl.BlockSpec((1, 1, rows, quarter), lambda i, q: (0, i, 0, 0))
    for t in range(1, last):
        after = (from_left[t], from_right[t]) + ((grad_t,) if t == last - 1 else ())
        dests = jnp.clip(jnp.stack([last - t + place[1], t - last + place[1]]), 0, last)
        right, left = call(
            add_body, "add", 0, 12 * n_dp * rows * quarter,
            grid_spec=pltpu.PrefetchScalarGridSpec(
                num_scalar_prefetch=1, grid=(n_dp,),
                in_specs=[pick(0), pick(1), piece_of, piece_of] + [ANY] * len(after),
                out_specs=[piece_of] * 2,
            ),
            out_shape=[shape(*chunk)] * 2,
        )(dests, partial, partial, right, left, *after)
        token = right
        right = shift(right, 1, range(t + 1))
        left = shift(left, -1, range(last - t, n_ctx))
    gated_all = call(
        merge_body, "merge", 0, 2 * (2 * n_ctx + last) * n_dp * rows * quarter,
        grid=(n_dp,),
        in_specs=[pl.BlockSpec((1, rows, quarter), lambda i: (i, 0, 0))] * (1 + 2 * last) + [ANY],
        out_specs=pl.BlockSpec((n_ctx, 1, rows, quarter), lambda i: (0, i, 0, 0)),
        out_shape=shape(n_ctx, n_dp, rows, quarter),
    )(gated_far, *from_left, *from_right[::-1], token).reshape(tokens, quarter)
    weight_part = call(
        weight_body, "weight", 2 * tokens * depth * quarter, 2 * tokens * (depth + quarter),
        grid=(n_dp,),
        in_specs=[
            pl.BlockSpec((feats, tokens), lambda i: (i, 0)),
            pl.BlockSpec((tokens, quarter), lambda i: (0, 0)),
            ANY,
        ],
        out_specs=pl.BlockSpec((1, feats, quarter), lambda i: (i, 0, 0)),
        out_shape=shape(n_dp, feats, quarter),
    )(grad_t, gated_all, token)

    delta = call(
        sum_body, "sum", 0, 8 * n_dp * rows * quarter,
        grid_spec=pltpu.PrefetchScalarGridSpec(
            num_scalar_prefetch=1, grid=(n_dp,),
            in_specs=[
                pl.BlockSpec((1, 1, rows, quarter), lambda i, p: (p[1], p[0] ^ i, 0, 0)),
                pl.BlockSpec((1, 1, rows, quarter), lambda i, p: (0, p[0] ^ i, 0, 0)),
                pl.BlockSpec((1, 1, rows, quarter), lambda i, p: (0, p[0] ^ i, 0, 0)),
                ANY,
            ],
            out_specs=[pl.BlockSpec((rows, quarter), lambda i, p: (0, 0))] * n_dp,
        ),
        out_shape=[shape(rows, quarter)] * n_dp,
    )(place, partial, right, left, weight_part)
    delta = [delta[0]] + [swap(delta[k], "dp", k) for k in range(1, n_dp)]
    held = call(
        wait_body, "hold", 0, 0,
        in_specs=[ANY] * n_dp, out_specs=ANY,
        out_shape=shape(n_dp, feats, quarter), input_output_aliases={0: 0},
    )(weight_part, *delta[1:])
    weight_far = lax.all_to_all(held, "dp", 0, 0, tiled=True)

    here = pl.BlockSpec((rows, block), lambda i, p: (0, p[0] ^ i))
    seed, starts, gate_grad = call(
        functools.partial(seed_body, n_dp), "seed", 2 * rows * 128 * width, rows * width * 10,
        grid_spec=pltpu.PrefetchScalarGridSpec(
            num_scalar_prefetch=1, grid=(n_dp,),
            in_specs=[pl.BlockSpec((rows, quarter), lambda i, p: (0, 0))] * n_dp
            + [here, here, pl.BlockSpec((block, rows), lambda i, p: (p[0] ^ i, 0))],
            out_specs=[here, pl.BlockSpec((ORDER, block), lambda i, p: (0, p[0] ^ i)), here],
            scratch_shapes=[pltpu.VMEM((rows, block), BF16)],
        ),
        out_shape=[shape(rows, width), shape(ORDER, width), shape(rows, width)],
    )(place, *delta, gate, long_out, starts_coef)
    starts_far = [shift(starts, -k) for k in range(1, n_ctx)]
    local_bwd = local(True, kernel, seed)
    query_grad, conv_grad = call(
        functools.partial(back_body, n_ctx - 1), "back", 2 * rows * 128 * width, rows * width * 12,
        grid=(steps,),
        in_specs=[wide(rows, block), wide((n_ctx - 1) * rows, block)] + [wide(rows, block)] * 2
        + [wide(ORDER, block)] * (n_ctx - 1),
        out_specs=[wide(rows, block)] * 2,
        out_shape=[shape(rows, width)] * 2,
    )(local_bwd, back_coef, conv, query, *starts_far)

    weight_grad = call(
        lay_body, "lay", 0, 4 * feats * width,
        grid=(n_dp,),
        in_specs=[pl.BlockSpec((1, feats, quarter), lambda i: (i, 0, 0)), ANY],
        out_specs=pl.BlockSpec((feats, quarter), lambda i: (0, i)),
        out_shape=shape(feats, width),
    )(weight_far, query_grad)
    return query_grad, conv_grad, gate_grad, weight_grad


def solution(mesh):
    rows = P(("dp", "ctx"), "tp")
    return jax.shard_map(
        on_device,
        mesh=mesh,
        in_specs=(rows, rows, rows, rows, P(("dp", "ctx"), None), P("tp", ("dp", "ctx")),
                  P("tp", None), P("tp", None), P("tp", None)),
        out_specs=(rows, rows, rows, rows),
        check_vma=False,
    )
```

```python
import functools

import jax
import jax.numpy as jnp
from jax import lax
from jax.experimental import pallas as pl
from jax.experimental.pallas import tpu as pltpu
from jax.sharding import PartitionSpec as P

GROUP = 16
TAPS = 128
ORDER = 16
LANES = 128
PER_SLAB = LANES // GROUP
BF16 = jnp.bfloat16
F32 = jnp.float32
VMEM = 50 * 2**20
ANY = pl.BlockSpec(memory_space=pl.ANY)


def call(body, name, flops, nbytes, **kwargs):
    return pl.pallas_call(
        body,
        name=name,
        cost_estimate=pl.CostEstimate(flops=flops, bytes_accessed=nbytes, transcendentals=0),
        compiler_params=pltpu.CompilerParams(vmem_limit_bytes=VMEM),
        **kwargs,
    )


def circulants(rows_ref, base):
    out = []
    for j in range(PER_SLAB):
        row = rows_ref[base + j : base + j + 1, :]
        out.append(
            pltpu.roll(jnp.broadcast_to(row, (LANES, LANES)), 0, 1, stride=1, stride_axis=0)
        )
    return out


def lower_mask():
    t = lax.broadcasted_iota(jnp.int32, (LANES, LANES), 0)
    u = lax.broadcasted_iota(jnp.int32, (LANES, LANES), 1)
    return u <= t


def pick_groups(stacked, rows):
    lane_group = lax.broadcasted_iota(jnp.int32, (rows, LANES), 1) // GROUP
    out = stacked[:rows]
    for j in range(1, PER_SLAB):
        out = jnp.where(lane_group == j, stacked[j * rows : (j + 1) * rows], out)
    return out


def spread_groups(state):
    tiled = jnp.concatenate([state] * PER_SLAB, axis=0)
    row_group = lax.broadcasted_iota(jnp.int32, (LANES, LANES), 0) // ORDER
    lane_group = lax.broadcasted_iota(jnp.int32, (LANES, LANES), 1) // GROUP
    return jnp.where(row_group == lane_group, tiled, jnp.zeros_like(tiled))


def dot(a, b):
    return jnp.dot(a, b, preferred_element_type=F32)


def conv_body(rim, own_part, query, taps, ends_coef, *refs):
    conv, mixed, ends = refs[-3:]
    lower = lower_mask()
    for s in range(rim.shape[1] // LANES):
        cols = slice(s * LANES, (s + 1) * LANES)
        blocks = [
            jnp.where(lower, jnp.zeros_like(circ), circ).astype(BF16)
            for circ in circulants(taps, s * PER_SLAB)
        ]
        out = own_part[:, cols] + pick_groups(
            dot(jnp.concatenate(blocks, axis=0), rim[:, cols]), LANES
        )
        conv[:, cols] = out.astype(conv.dtype)
        mixed[:, cols] = (query[:, cols].astype(F32) * out).astype(BF16)
    for s in range(rim.shape[1] // LANES):
        cols = slice(s * LANES, (s + 1) * LANES)
        ends[:, cols] = pick_groups(
            dot(ends_coef[s * LANES : (s + 1) * LANES, :], mixed[:, cols]), ORDER
        ).astype(ends.dtype)


def local_body(transposed, rows, x, *refs):
    out = refs[-1]
    lower = lower_mask()
    keep = ~lower | (lax.broadcasted_iota(jnp.int32, (LANES, LANES), 0)
                     == lax.broadcasted_iota(jnp.int32, (LANES, LANES), 1)) if transposed else lower
    for s in range(x.shape[1] // LANES):
        cols = slice(s * LANES, (s + 1) * LANES)
        blocks = [
            jnp.where(keep, circ, jnp.zeros_like(circ)).astype(BF16)
            for circ in circulants(rows, s * PER_SLAB)
        ]
        out[:, cols] = pick_groups(
            dot(jnp.concatenate(blocks, axis=0), x[:, cols]), LANES
        ).astype(out.dtype)


def carried(states, coef, cols):
    wide_states = jnp.concatenate([spread_groups(ref[:, cols]) for ref in states], axis=0)
    count = len(states)
    rows = coef.shape[0] // count
    parts = [coef[k * rows : (k + 1) * rows, cols] for k in range(count)]
    return dot(jnp.concatenate(parts, axis=1), wide_states)


def long_body(count, local, coef, gate, *refs):
    states, (long_out, gated) = refs[:count], refs[-2:]
    for s in range(local.shape[1] // LANES):
        cols = slice(s * LANES, (s + 1) * LANES)
        out = local[:, cols].astype(F32) + carried(states, coef, cols)
        long_out[:, cols] = out.astype(long_out.dtype)
        gated[0, :, cols] = (gate[:, cols].astype(F32) * out).astype(BF16)


def seed_body(count, place, *refs):
    sources = refs[:count]
    gate, long_out, starts_coef, seed, starts, gate_grad, delta = refs[count:]
    for k, source in enumerate(sources):

        @pl.when(pl.program_id(0) == k)
        def _(source=source):
            delta[...] = source[...]

    for s in range(gate.shape[1] // LANES):
        cols = slice(s * LANES, (s + 1) * LANES)
        out = delta[:, cols].astype(F32)
        seed[:, cols] = (out * gate[:, cols].astype(F32)).astype(BF16)
        gate_grad[:, cols] = (out * long_out[:, cols].astype(F32)).astype(BF16)
    for s in range(gate.shape[1] // LANES):
        cols = slice(s * LANES, (s + 1) * LANES)
        starts[:, cols] = pick_groups(
            dot(starts_coef[s * LANES : (s + 1) * LANES, :], seed[:, cols]), ORDER
        ).astype(starts.dtype)


def back_body(count, local, coef, conv, query, *refs):
    states, (query_grad, conv_grad) = refs[:count], refs[-2:]
    for s in range(local.shape[1] // LANES):
        cols = slice(s * LANES, (s + 1) * LANES)
        out = local[:, cols].astype(F32) + carried(states, coef, cols)
        query_grad[:, cols] = (out * conv[:, cols].astype(F32)).astype(BF16)
        conv_grad[:, cols] = (out * query[:, cols].astype(F32)).astype(BF16)


def pack_body(place, *refs):
    count = len(refs) // 2
    for source, target in zip(refs[:count], refs[-count:]):
        target[...] = source[...]


def join_body(*refs):
    out = refs[-1]
    for k in range(out.shape[0]):
        out[k] = refs[k][...]


def delta_body(whole, place, dest, grad, weights, *refs):
    depth, out = weights.shape[2], refs[-1]

    def multiply():
        total = None
        for k in range(weights.shape[0]):
            rows = grad[:, :, :, :, k * depth : (k + 1) * depth].reshape(-1, depth)
            term = lax.dot_general(
                rows, weights[k], (((1,), (1,)), ((), ())), preferred_element_type=F32
            )
            total = term if total is None else total + term
        out[...] = total.astype(BF16).reshape(out.shape)

    if not whole:
        return multiply()
    is_last = pl.program_id(0) == pl.num_programs(0) - 1
    pl.when(jnp.logical_not(is_last))(multiply)

    @pl.when(is_last)
    def _():
        out[...] = refs[0][...]


def flip_body(place, grad, after, out):
    out[...] = grad[...].reshape(-1, grad.shape[-1]).T


def lay_body(place, *refs):
    sources, out = refs[:-2], refs[-1]
    for k, source in enumerate(sources):
        lanes = source.shape[1]
        out[:, pl.ds(pl.multiple_of((place[0] ^ k) * lanes, lanes), lanes)] = source[...]


def wait_body(*refs):
    pass


def add_body(dests, partial_right, partial_left, right, left, *refs):
    out_right, out_left = refs[-2:]
    out_right[...] = (partial_right[...].astype(F32) + right[...].astype(F32)).astype(BF16)
    out_left[...] = (partial_left[...].astype(F32) + left[...].astype(F32)).astype(BF16)


def merge_body(own, *refs):
    out = refs[-1]
    count = out.shape[0] - 1
    out[0] = own[...]
    for k in range(count):
        out[k + 1] = refs[k][...] + refs[count + k][...]


def sum_body(place, partial, right, left, after, *outs):
    total = partial[0, 0].astype(F32) + right[0, 0].astype(F32) + left[0, 0].astype(F32)
    for k, out in enumerate(outs):

        @pl.when(pl.program_id(0) == k)
        def _(out=out):
            out[...] = total.astype(BF16)


def weight_body(place, grad_t, gated, after, out):
    out[...] = dot(grad_t[...], gated[...]).astype(out.dtype)


def wide(rows, lanes):
    return pl.BlockSpec((rows, lanes), lambda i: (0, i))


def tall(rows, cols):
    return pl.BlockSpec((rows, cols), lambda i: (i, 0))


def deep(count, rows, lanes):
    return pl.BlockSpec((count, rows, lanes), lambda i: (0, 0, i))


def shape(*dims, dtype=BF16):
    return jax.ShapeDtypeStruct(dims, dtype)


def on_device(query, key_in, value_in, gate, out_grad, proj_weight, mr_filter, lr_rate, lr_residue):
    rows, width = query.shape
    groups = width // GROUP
    n_dp, n_ctx, n_tp = (lax.axis_size(a) for a in ("dp", "ctx", "tp"))
    feats = proj_weight.shape[1]
    quarter = width // n_dp
    depth = n_dp * feats
    block = quarter
    steps = width // block
    part = rows // n_tp

    place = jnp.stack([lax.axis_index(a) for a in ("dp", "ctx", "tp")]).astype(jnp.int32)

    def swap(value, axis, k):
        return lax.ppermute(value, axis, [(i, i ^ k) for i in range(lax.axis_size(axis))])

    def shift(value, k, senders=None):
        ends = [(i, i + k) for i in senders or range(n_ctx) if 0 <= i + k < n_ctx]
        return lax.ppermute(value, "ctx", ends)

    def piece(k):
        return pl.BlockSpec((part, feats), lambda j, p: (p[2], j * n_ctx + (p[1] ^ k)))

    weights = lax.all_to_all(proj_weight.reshape(n_dp, quarter, feats), "dp", 0, 0, tiled=True)
    mine = call(
        pack_body, "pack", 0, 4 * part * depth * n_ctx,
        grid_spec=pltpu.PrefetchScalarGridSpec(
            num_scalar_prefetch=1, grid=(n_dp,),
            in_specs=[piece(k) for k in range(n_ctx)],
            out_specs=[pl.BlockSpec((part, feats), lambda j, p: (0, j))] * n_ctx,
        ),
        out_shape=[shape(part, depth)] * n_ctx,
    )(place, *[out_grad] * n_ctx)
    mine = [mine[0]] + [swap(mine[k], "ctx", k) for k in range(1, n_ctx)]
    product = (key_in.astype(F32) * value_in.astype(F32)).astype(BF16)
    rim = shift(product, 1)
    rate = lr_rate.reshape(-1, 1)
    residue = lr_residue.reshape(-1, 1)
    counts = jnp.arange(rows, dtype=F32)[None, :]
    ends_coef = jnp.exp(-rate * (rows - 1 - counts)).astype(BF16)
    starts_coef = jnp.exp(-rate * counts).astype(BF16)
    away = jnp.arange((n_ctx - 1) * rows, dtype=F32)[:, None]
    inside = away % rows
    carry_coef = (residue.T * jnp.exp(-rate.T * (away + 1))).astype(BF16)
    back_coef = (residue.T * jnp.exp(-rate.T * (away + rows - 2 * inside))).astype(BF16)
    kernel = jnp.sum(
        lr_residue[:, :, None] * jnp.exp(-lr_rate[:, :, None] * counts[:, None, :]), axis=1
    )

    def reversed_row(values):
        return jnp.roll(values[:, ::-1], 1, axis=1)

    taps = reversed_row(mr_filter.astype(F32))
    kernel_rev = reversed_row(kernel)
    def local(transposed, table, x, *after):
        return call(
            functools.partial(local_body, transposed),
            "local_t" if transposed else "local",
            2 * rows * 128 * width * 8, rows * width * 6,
            grid=(steps,),
            in_specs=[tall(block // GROUP, rows), wide(rows, block)] + [ANY] * len(after),
            out_specs=wide(rows, block),
            out_shape=shape(rows, width, dtype=F32),
        )(table, x, *after)

    conv_own = local(
        False, taps, product, ends_coef, starts_coef, carry_coef, back_coef, kernel_rev, kernel
    )
    conv, mixed, ends = call(
        conv_body, "conv", 2 * rows * 128 * width * 8, rows * width * 14,
        grid=(steps,),
        in_specs=[wide(rows, block)] * 3 + [tall(block // GROUP, TAPS), tall(block, rows)],
        out_specs=[wide(rows, block), wide(rows, block), wide(ORDER, block)],
        out_shape=[shape(rows, width), shape(rows, width), shape(ORDER, width)],
    )(rim, conv_own, query, taps, ends_coef)
    ends_far = [shift(ends, k) for k in range(1, n_ctx)]


    local_fwd = local(False, kernel_rev, mixed)
    mine = call(
        join_body, "join", 0, 4 * part * depth * n_ctx,
        grid=(n_dp,),
        in_specs=[wide(part, feats)] * n_ctx + [ANY] * 2,
        out_specs=deep(n_ctx, part, feats),
        out_shape=shape(n_ctx, part, depth),
    )(*mine, weights, local_fwd)
    grad = lax.all_gather(mine, ("dp", "tp"), axis=0, tiled=False)
    grad = grad.reshape(n_dp, n_tp, n_ctx, part, depth)
    long_out, gated = call(
        functools.partial(long_body, n_ctx - 1), "long", 2 * rows * 128 * width, rows * width * 10,
        grid=(steps,),
        in_specs=[wide(rows, block), wide((n_ctx - 1) * rows, block), wide(rows, block)] + [wide(ORDER, block)] * (n_ctx - 1) + [ANY],
        out_specs=[wide(rows, block), pl.BlockSpec((1, rows, block), lambda i: (i, 0, 0))],
        out_shape=[shape(rows, width), shape(n_dp, rows, quarter)],
    )(local_fwd, carry_coef, gate, *ends_far, mine)
    gated_far = lax.all_to_all(gated, "dp", 0, 0, tiled=True)
    tokens = n_ctx * n_dp * rows
    last = n_ctx - 1
    from_left, from_right = [], []
    right = left = gated_far
    for t in range(last):
        right = shift(right, 1, range(t, last))
        left = shift(left, -1, range(1, n_ctx - t))
        from_left.append(right)
        from_right.append(left)

    first_dest = jnp.where(place[1] < n_ctx // 2, last, 0)
    chunk = (1, n_dp, rows, quarter)

    def project(dests, *after):
        count = dests.shape[0]
        whole = count > 1
        return call(
            functools.partial(delta_body, whole), "delta",
            2 * max(count - 1, 1) * n_dp * rows * depth * quarter,
            2 * tokens * depth + 2 * depth * quarter + 2 * count * n_dp * rows * quarter,
            grid_spec=pltpu.PrefetchScalarGridSpec(
                num_scalar_prefetch=2, grid=(count,),
                in_specs=[
                    pl.BlockSpec(
                        (n_dp, n_tp, 1, part, depth), lambda i, p, q: (0, 0, p[1] ^ q[i], 0, 0)
                    ),
                    pl.BlockSpec((n_dp, quarter, feats), lambda i, p, q: (0, 0, 0)),
                ] + ([pl.BlockSpec(chunk, lambda i, p, q: (0, 0, 0, 0))] if whole
                     else [ANY] * len(after)),
                out_specs=pl.BlockSpec(
                    chunk, lambda i, p, q: (q[i] if whole else 0, 0, 0, 0)
                ),
            ),
            out_shape=shape(count, n_dp, rows, quarter),
        )(place, dests, grad, weights, *after)

    first = project(first_dest[None], from_left[0], from_right[0])
    others = (first_dest + 1 + jnp.arange(n_ctx, dtype=jnp.int32)) % n_ctx
    partial = project(others.astype(jnp.int32), first)
    grad_t = call(
        flip_body, "flip", 0, 4 * tokens * depth,
        grid_spec=pltpu.PrefetchScalarGridSpec(
            num_scalar_prefetch=1, grid=(n_ctx, n_dp),
            in_specs=[
                pl.BlockSpec(
                    (1, n_tp, 1, part, depth),
                    lambda i, j, p: (j, 0, p[1] ^ ((p[1] + n_ctx - i) % n_ctx), 0, 0),
                ),
                ANY,
            ],
            out_specs=pl.BlockSpec((depth, rows), lambda i, j, p: (0, i * n_dp + j)),
        ),
        out_shape=shape(depth, tokens),
    )(place, grad, partial)
    right, left = shift(first, 1, [0]), shift(first, -1, [last])

    def pick(ahead):
        return pl.BlockSpec(
            (1, 1, rows, quarter), lambda i, q: (q[ahead], i, 0, 0)
        )

    piece_of = pl.BlockSpec((1, 1, rows, quarter), lambda i, q: (0, i, 0, 0))
    for t in range(1, last):
        after = (from_left[t], from_right[t]) + ((grad_t,) if t == last - 1 else ())
        dests = jnp.clip(jnp.stack([last - t + place[1], t - last + place[1]]), 0, last)
        right, left = call(
            add_body, "add", 0, 12 * n_dp * rows * quarter,
            grid_spec=pltpu.PrefetchScalarGridSpec(
                num_scalar_prefetch=1, grid=(n_dp,),
                in_specs=[pick(0), pick(1), piece_of, piece_of] + [ANY] * len(after),
                out_specs=[piece_of] * 2,
            ),
            out_shape=[shape(*chunk)] * 2,
        )(dests, partial, partial, right, left, *after)
        token = right
        right = shift(right, 1, range(t + 1))
        left = shift(left, -1, range(last - t, n_ctx))
    gated_all = call(
        merge_body, "merge", 0, 2 * (2 * n_ctx + last) * n_dp * rows * quarter,
        grid=(n_dp,),
        in_specs=[pl.BlockSpec((1, rows, quarter), lambda i: (i, 0, 0))] * (1 + 2 * last) + [ANY],
        out_specs=pl.BlockSpec((n_ctx, 1, rows, quarter), lambda i: (0, i, 0, 0)),
        out_shape=shape(n_ctx, n_dp, rows, quarter),
    )(gated_far, *from_left, *from_right[::-1], token).reshape(tokens, quarter)
    pieces = {}
    for k in range(n_dp - 1, -1, -1):
        token = pieces[k] = call(
            weight_body, "weight", 2 * tokens * feats * quarter, 2 * tokens * (feats + quarter),
            grid_spec=pltpu.PrefetchScalarGridSpec(
                num_scalar_prefetch=1, grid=(2,),
                in_specs=[
                    pl.BlockSpec((feats, tokens), lambda i, p, k=k: (p[0] ^ k, 0)),
                    pl.BlockSpec((tokens, quarter // 2), lambda i, p: (0, i)),
                    ANY,
                ],
                out_specs=pl.BlockSpec((feats, quarter // 2), lambda i, p: (0, i)),
            ),
            out_shape=shape(feats, quarter),
        )(place, grad_t, gated_all, token)

    def hold(value, *after):
        return call(
            wait_body, "hold", 0, 0,
            in_specs=[ANY] * (1 + len(after)), out_specs=ANY,
            out_shape=shape(*value.shape), input_output_aliases={0: 0},
        )(value, *after)

    diagonal = swap(pieces[n_dp - 1], "dp", n_dp - 1)

    delta = call(
        sum_body, "sum", 0, 8 * n_dp * rows * quarter,
        grid_spec=pltpu.PrefetchScalarGridSpec(
            num_scalar_prefetch=1, grid=(n_dp,),
            in_specs=[
                pl.BlockSpec((1, 1, rows, quarter), lambda i, p: (p[1], p[0] ^ i, 0, 0)),
                pl.BlockSpec((1, 1, rows, quarter), lambda i, p: (0, p[0] ^ i, 0, 0)),
                pl.BlockSpec((1, 1, rows, quarter), lambda i, p: (0, p[0] ^ i, 0, 0)),
                ANY,
            ],
            out_specs=[pl.BlockSpec((rows, quarter), lambda i, p: (0, 0))] * n_dp,
        ),
        out_shape=[shape(rows, quarter)] * n_dp,
    )(place, partial, right, left, pieces[n_dp // 2])
    delta = [delta[0]] + [swap(hold(delta[k], diagonal), "dp", k) for k in range(1, n_dp)]
    weight_far = [pieces[0]] + [
        swap(hold(pieces[k], *delta[1:]), "dp", k) for k in range(1, n_dp - 1)
    ] + [diagonal]

    here = pl.BlockSpec((rows, block), lambda i, p: (0, p[0] ^ i))
    seed, starts, gate_grad = call(
        functools.partial(seed_body, n_dp), "seed", 2 * rows * 128 * width, rows * width * 10,
        grid_spec=pltpu.PrefetchScalarGridSpec(
            num_scalar_prefetch=1, grid=(n_dp,),
            in_specs=[pl.BlockSpec((rows, quarter), lambda i, p: (0, 0))] * n_dp
            + [here, here, pl.BlockSpec((block, rows), lambda i, p: (p[0] ^ i, 0))],
            out_specs=[here, pl.BlockSpec((ORDER, block), lambda i, p: (0, p[0] ^ i)), here],
            scratch_shapes=[pltpu.VMEM((rows, block), BF16)],
        ),
        out_shape=[shape(rows, width), shape(ORDER, width), shape(rows, width)],
    )(place, *delta, gate, long_out, starts_coef)
    starts_far = [shift(starts, -k) for k in range(1, n_ctx)]
    local_bwd = local(True, kernel, seed)
    query_grad, conv_grad = call(
        functools.partial(back_body, n_ctx - 1), "back", 2 * rows * 128 * width, rows * width * 12,
        grid=(steps,),
        in_specs=[wide(rows, block), wide((n_ctx - 1) * rows, block)] + [wide(rows, block)] * 2
        + [wide(ORDER, block)] * (n_ctx - 1),
        out_specs=[wide(rows, block)] * 2,
        out_shape=[shape(rows, width)] * 2,
    )(local_bwd, back_coef, conv, query, *starts_far)

    cut = feats // n_dp
    weight_grad = call(
        lay_body, "lay", 0, 4 * feats * width,
        grid_spec=pltpu.PrefetchScalarGridSpec(
            num_scalar_prefetch=1, grid=(n_dp,),
            in_specs=[pl.BlockSpec((cut, quarter), lambda i, p: (i, 0))] * n_dp + [ANY],
            out_specs=pl.BlockSpec((cut, width), lambda i, p: (i, 0)),
        ),
        out_shape=shape(feats, width),
    )(place, *weight_far, query_grad)
    return query_grad, conv_grad, gate_grad, weight_grad


def solution(mesh):
    rows = P(("dp", "ctx"), "tp")
    return jax.shard_map(
        on_device,
        mesh=mesh,
        in_specs=(rows, rows, rows, rows, P(("dp", "ctx"), None), P("tp", ("dp", "ctx")),
                  P("tp", None), P("tp", None), P("tp", None)),
        out_specs=(rows, rows, rows, rows),
        check_vma=False,
    )
```

```python
import functools

import jax
import jax.numpy as jnp
from jax import lax
from jax.experimental import pallas as pl
from jax.experimental.pallas import tpu as pltpu
from jax.sharding import PartitionSpec as P

GROUP = 16
TAPS = 128
ORDER = 16
LANES = 128
PER_SLAB = LANES // GROUP
BF16 = jnp.bfloat16
F32 = jnp.float32
VMEM = 50 * 2**20
ANY = pl.BlockSpec(memory_space=pl.ANY)


def call(body, name, flops, nbytes, **kwargs):
    return pl.pallas_call(
        body,
        name=name,
        cost_estimate=pl.CostEstimate(flops=flops, bytes_accessed=nbytes, transcendentals=0),
        compiler_params=pltpu.CompilerParams(vmem_limit_bytes=VMEM),
        **kwargs,
    )


def circulants(rows_ref, base):
    out = []
    for j in range(PER_SLAB):
        row = rows_ref[base + j : base + j + 1, :]
        out.append(
            pltpu.roll(jnp.broadcast_to(row, (LANES, LANES)), 0, 1, stride=1, stride_axis=0)
        )
    return out


def lower_mask():
    t = lax.broadcasted_iota(jnp.int32, (LANES, LANES), 0)
    u = lax.broadcasted_iota(jnp.int32, (LANES, LANES), 1)
    return u <= t


def pick_groups(stacked, rows):
    lane_group = lax.broadcasted_iota(jnp.int32, (rows, LANES), 1) // GROUP
    out = stacked[:rows]
    for j in range(1, PER_SLAB):
        out = jnp.where(lane_group == j, stacked[j * rows : (j + 1) * rows], out)
    return out


def spread_groups(state):
    tiled = jnp.concatenate([state] * PER_SLAB, axis=0)
    row_group = lax.broadcasted_iota(jnp.int32, (LANES, LANES), 0) // ORDER
    lane_group = lax.broadcasted_iota(jnp.int32, (LANES, LANES), 1) // GROUP
    return jnp.where(row_group == lane_group, tiled, jnp.zeros_like(tiled))


def dot(a, b):
    return jnp.dot(a, b, preferred_element_type=F32)


def conv_body(rim, own_part, query, taps, ends_coef, *refs):
    conv, mixed, ends = refs[-3:]
    lower = lower_mask()
    for s in range(rim.shape[1] // LANES):
        cols = slice(s * LANES, (s + 1) * LANES)
        blocks = [
            jnp.where(lower, jnp.zeros_like(circ), circ).astype(BF16)
            for circ in circulants(taps, s * PER_SLAB)
        ]
        out = own_part[:, cols] + pick_groups(
            dot(jnp.concatenate(blocks, axis=0), rim[:, cols]), LANES
        )
        conv[:, cols] = out.astype(conv.dtype)
        mixed[:, cols] = (query[:, cols].astype(F32) * out).astype(BF16)
    for s in range(rim.shape[1] // LANES):
        cols = slice(s * LANES, (s + 1) * LANES)
        ends[:, cols] = pick_groups(
            dot(ends_coef[s * LANES : (s + 1) * LANES, :], mixed[:, cols]), ORDER
        ).astype(ends.dtype)


def local_body(transposed, rows, x, *refs):
    out = refs[-1]
    lower = lower_mask()
    keep = ~lower | (lax.broadcasted_iota(jnp.int32, (LANES, LANES), 0)
                     == lax.broadcasted_iota(jnp.int32, (LANES, LANES), 1)) if transposed else lower
    for s in range(x.shape[1] // LANES):
        cols = slice(s * LANES, (s + 1) * LANES)
        blocks = [
            jnp.where(keep, circ, jnp.zeros_like(circ)).astype(BF16)
            for circ in circulants(rows, s * PER_SLAB)
        ]
        out[:, cols] = pick_groups(
            dot(jnp.concatenate(blocks, axis=0), x[:, cols]), LANES
        ).astype(out.dtype)


def carried(states, coef, cols):
    wide_states = jnp.concatenate([spread_groups(ref[:, cols]) for ref in states], axis=0)
    count = len(states)
    rows = coef.shape[0] // count
    parts = [coef[k * rows : (k + 1) * rows, cols] for k in range(count)]
    return dot(jnp.concatenate(parts, axis=1), wide_states)


def long_body(count, local, coef, gate, *refs):
    states, (long_out, gated) = refs[:count], refs[-2:]
    for s in range(local.shape[1] // LANES):
        cols = slice(s * LANES, (s + 1) * LANES)
        out = local[:, cols].astype(F32) + carried(states, coef, cols)
        long_out[:, cols] = out.astype(long_out.dtype)
        gated[0, :, cols] = (gate[:, cols].astype(F32) * out).astype(BF16)


def seed_body(count, place, *refs):
    sources = refs[:count]
    gate, long_out, starts_coef, seed, starts, gate_grad, delta = refs[count:]
    for k, source in enumerate(sources):

        @pl.when(pl.program_id(0) == k)
        def _(source=source):
            delta[...] = source[...]

    for s in range(gate.shape[1] // LANES):
        cols = slice(s * LANES, (s + 1) * LANES)
        out = delta[:, cols].astype(F32)
        seed[:, cols] = (out * gate[:, cols].astype(F32)).astype(BF16)
        gate_grad[:, cols] = (out * long_out[:, cols].astype(F32)).astype(BF16)
    for s in range(gate.shape[1] // LANES):
        cols = slice(s * LANES, (s + 1) * LANES)
        starts[:, cols] = pick_groups(
            dot(starts_coef[s * LANES : (s + 1) * LANES, :], seed[:, cols]), ORDER
        ).astype(starts.dtype)


def back_body(count, local, coef, conv, query, *refs):
    states, (query_grad, conv_grad) = refs[:count], refs[-2:]
    for s in range(local.shape[1] // LANES):
        cols = slice(s * LANES, (s + 1) * LANES)
        out = local[:, cols].astype(F32) + carried(states, coef, cols)
        query_grad[:, cols] = (out * conv[:, cols].astype(F32)).astype(BF16)
        conv_grad[:, cols] = (out * query[:, cols].astype(F32)).astype(BF16)


def pack_body(place, *refs):
    count = len(refs) // 2
    for source, target in zip(refs[:count], refs[-count:]):
        target[...] = source[...]


def join_body(*refs):
    out = refs[-1]
    for k in range(out.shape[0]):
        out[k] = refs[k][...]


def delta_body(whole, place, dest, grad, weights, *refs):
    depth, out = weights.shape[2], refs[-1]

    def multiply():
        total = None
        for k in range(weights.shape[0]):
            rows = grad[:, :, :, :, k * depth : (k + 1) * depth].reshape(-1, depth)
            term = lax.dot_general(
                rows, weights[k], (((1,), (1,)), ((), ())), preferred_element_type=F32
            )
            total = term if total is None else total + term
        out[...] = total.astype(BF16).reshape(out.shape)

    if not whole:
        return multiply()
    is_last = pl.program_id(0) == pl.num_programs(0) - 1
    pl.when(jnp.logical_not(is_last))(multiply)

    @pl.when(is_last)
    def _():
        out[...] = refs[0][...]


def flip_body(place, grad, after, out):
    out[...] = grad[...].reshape(-1, grad.shape[-1]).T


def lay_body(place, *refs):
    sources, out = refs[:-2], refs[-1]
    for k, source in enumerate(sources):
        lanes = source.shape[1]
        out[:, pl.ds(pl.multiple_of((place[0] ^ k) * lanes, lanes), lanes)] = source[...]


def wait_body(*refs):
    pass


def add_body(dests, partial_right, partial_left, right, left, *refs):
    out_right, out_left = refs[-2:]
    out_right[...] = (partial_right[...].astype(F32) + right[...].astype(F32)).astype(BF16)
    out_left[...] = (partial_left[...].astype(F32) + left[...].astype(F32)).astype(BF16)


def merge_body(own, *refs):
    out = refs[-1]
    count = out.shape[0] - 1
    out[0] = own[...]
    for k in range(count):
        out[k + 1] = refs[k][...] + refs[count + k][...]


def sum_body(place, partial, right, left, after, *outs):
    total = partial[0, 0].astype(F32) + right[0, 0].astype(F32) + left[0, 0].astype(F32)
    for k, out in enumerate(outs):

        @pl.when(pl.program_id(0) == k)
        def _(out=out):
            out[...] = total.astype(BF16)


def weight_body(place, grad_t, gated, after, out):
    out[...] = dot(grad_t[...], gated[...]).astype(out.dtype)


def wide(rows, lanes):
    return pl.BlockSpec((rows, lanes), lambda i: (0, i))


def tall(rows, cols):
    return pl.BlockSpec((rows, cols), lambda i: (i, 0))


def deep(count, rows, lanes):
    return pl.BlockSpec((count, rows, lanes), lambda i: (0, 0, i))


def shape(*dims, dtype=BF16):
    return jax.ShapeDtypeStruct(dims, dtype)


def on_device(query, key_in, value_in, gate, out_grad, proj_weight, mr_filter, lr_rate, lr_residue):
    rows, width = query.shape
    groups = width // GROUP
    n_dp, n_ctx, n_tp = (lax.axis_size(a) for a in ("dp", "ctx", "tp"))
    feats = proj_weight.shape[1]
    quarter = width // n_dp
    depth = n_dp * feats
    block = quarter
    steps = width // block
    part = rows // n_tp

    place = jnp.stack([lax.axis_index(a) for a in ("dp", "ctx", "tp")]).astype(jnp.int32)

    def swap(value, axis, k):
        return lax.ppermute(value, axis, [(i, i ^ k) for i in range(lax.axis_size(axis))])

    def shift(value, k, senders=None):
        ends = [(i, i + k) for i in senders or range(n_ctx) if 0 <= i + k < n_ctx]
        return lax.ppermute(value, "ctx", ends)

    def piece(k):
        return pl.BlockSpec((part, feats), lambda j, p: (p[2], j * n_ctx + (p[1] ^ k)))

    weights = lax.all_to_all(proj_weight.reshape(n_dp, quarter, feats), "dp", 0, 0, tiled=True)
    mine = call(
        pack_body, "pack", 0, 4 * part * depth * n_ctx,
        grid_spec=pltpu.PrefetchScalarGridSpec(
            num_scalar_prefetch=1, grid=(n_dp,),
            in_specs=[piece(k) for k in range(n_ctx)],
            out_specs=[pl.BlockSpec((part, feats), lambda j, p: (0, j))] * n_ctx,
        ),
        out_shape=[shape(part, depth)] * n_ctx,
    )(place, *[out_grad] * n_ctx)
    mine = [mine[0]] + [swap(mine[k], "ctx", k) for k in range(1, n_ctx)]
    product = (key_in.astype(F32) * value_in.astype(F32)).astype(BF16)
    rim = shift(product, 1)
    rate = lr_rate.reshape(-1, 1)
    residue = lr_residue.reshape(-1, 1)
    counts = jnp.arange(rows, dtype=F32)[None, :]
    ends_coef = jnp.exp(-rate * (rows - 1 - counts)).astype(BF16)
    starts_coef = jnp.exp(-rate * counts).astype(BF16)
    away = jnp.arange((n_ctx - 1) * rows, dtype=F32)[:, None]
    inside = away % rows
    carry_coef = (residue.T * jnp.exp(-rate.T * (away + 1))).astype(BF16)
    back_coef = (residue.T * jnp.exp(-rate.T * (away + rows - 2 * inside))).astype(BF16)
    kernel = jnp.sum(
        lr_residue[:, :, None] * jnp.exp(-lr_rate[:, :, None] * counts[:, None, :]), axis=1
    )

    def reversed_row(values):
        return jnp.roll(values[:, ::-1], 1, axis=1)

    taps = reversed_row(mr_filter.astype(F32))
    kernel_rev = reversed_row(kernel)
    def local(transposed, table, x, *after):
        return call(
            functools.partial(local_body, transposed),
            "local_t" if transposed else "local",
            2 * rows * 128 * width * 8, rows * width * 6,
            grid=(steps,),
            in_specs=[tall(block // GROUP, rows), wide(rows, block)] + [ANY] * len(after),
            out_specs=wide(rows, block),
            out_shape=shape(rows, width, dtype=F32),
        )(table, x, *after)

    conv_own = local(
        False, taps, product, ends_coef, starts_coef, carry_coef, back_coef, kernel_rev, kernel
    )
    conv, mixed, ends = call(
        conv_body, "conv", 2 * rows * 128 * width * 8, rows * width * 14,
        grid=(steps,),
        in_specs=[wide(rows, block)] * 3 + [tall(block // GROUP, TAPS), tall(block, rows)],
        out_specs=[wide(rows, block), wide(rows, block), wide(ORDER, block)],
        out_shape=[shape(rows, width), shape(rows, width), shape(ORDER, width)],
    )(rim, conv_own, query, taps, ends_coef)
    ends_far = [shift(ends, k) for k in range(1, n_ctx)]


    local_fwd = local(False, kernel_rev, mixed)
    mine = call(
        join_body, "join", 0, 4 * part * depth * n_ctx,
        grid=(n_dp,),
        in_specs=[wide(part, feats)] * n_ctx + [ANY] * 2,
        out_specs=deep(n_ctx, part, feats),
        out_shape=shape(n_ctx, part, depth),
    )(*mine, weights, local_fwd)
    grad = lax.all_gather(mine, ("dp", "tp"), axis=0, tiled=False)
    grad = grad.reshape(n_dp, n_tp, n_ctx, part, depth)
    long_out, gated = call(
        functools.partial(long_body, n_ctx - 1), "long", 2 * rows * 128 * width, rows * width * 10,
        grid=(steps,),
        in_specs=[wide(rows, block), wide((n_ctx - 1) * rows, block), wide(rows, block)] + [wide(ORDER, block)] * (n_ctx - 1) + [ANY],
        out_specs=[wide(rows, block), pl.BlockSpec((1, rows, block), lambda i: (i, 0, 0))],
        out_shape=[shape(rows, width), shape(n_dp, rows, quarter)],
    )(local_fwd, carry_coef, gate, *ends_far, mine)
    gated_far = lax.all_to_all(gated, "dp", 0, 0, tiled=True)
    tokens = n_ctx * n_dp * rows
    last = n_ctx - 1
    from_left, from_right = [], []
    right = left = gated_far
    for t in range(last):
        right = shift(right, 1, range(t, last))
        left = shift(left, -1, range(1, n_ctx - t))
        from_left.append(right)
        from_right.append(left)

    first_dest = jnp.where(place[1] < n_ctx // 2, last, 0)
    chunk = (1, n_dp, rows, quarter)

    def project(dests, *after):
        count = dests.shape[0]
        whole = count > 1
        return call(
            functools.partial(delta_body, whole), "delta",
            2 * max(count - 1, 1) * n_dp * rows * depth * quarter,
            2 * tokens * depth + 2 * depth * quarter + 2 * count * n_dp * rows * quarter,
            grid_spec=pltpu.PrefetchScalarGridSpec(
                num_scalar_prefetch=2, grid=(count,),
                in_specs=[
                    pl.BlockSpec(
                        (n_dp, n_tp, 1, part, depth), lambda i, p, q: (0, 0, p[1] ^ q[i], 0, 0)
                    ),
                    pl.BlockSpec((n_dp, quarter, feats), lambda i, p, q: (0, 0, 0)),
                ] + ([pl.BlockSpec(chunk, lambda i, p, q: (0, 0, 0, 0))] if whole
                     else [ANY] * len(after)),
                out_specs=pl.BlockSpec(
                    chunk, lambda i, p, q: (q[i] if whole else 0, 0, 0, 0)
                ),
            ),
            out_shape=shape(count, n_dp, rows, quarter),
        )(place, dests, grad, weights, *after)

    first = project(first_dest[None], from_left[0], from_right[0])
    others = (first_dest + 1 + jnp.arange(n_ctx, dtype=jnp.int32)) % n_ctx
    partial = project(others.astype(jnp.int32), first)
    grad_t = call(
        flip_body, "flip", 0, 4 * tokens * depth,
        grid_spec=pltpu.PrefetchScalarGridSpec(
            num_scalar_prefetch=1, grid=(n_ctx, n_dp),
            in_specs=[
                pl.BlockSpec(
                    (1, n_tp, 1, part, depth),
                    lambda i, j, p: (j, 0, p[1] ^ ((p[1] + n_ctx - i) % n_ctx), 0, 0),
                ),
                ANY,
            ],
            out_specs=pl.BlockSpec((depth, rows), lambda i, j, p: (0, i * n_dp + j)),
        ),
        out_shape=shape(depth, tokens),
    )(place, grad, partial)
    right, left = shift(first, 1, [0]), shift(first, -1, [last])

    def pick(ahead):
        return pl.BlockSpec(
            (1, 1, rows, quarter), lambda i, q: (q[ahead], i, 0, 0)
        )

    piece_of = pl.BlockSpec((1, 1, rows, quarter), lambda i, q: (0, i, 0, 0))
    for t in range(1, last):
        after = (from_left[t], from_right[t]) + ((grad_t,) if t == last - 1 else ())
        dests = jnp.clip(jnp.stack([last - t + place[1], t - last + place[1]]), 0, last)
        right, left = call(
            add_body, "add", 0, 12 * n_dp * rows * quarter,
            grid_spec=pltpu.PrefetchScalarGridSpec(
                num_scalar_prefetch=1, grid=(n_dp,),
                in_specs=[pick(0), pick(1), piece_of, piece_of] + [ANY] * len(after),
                out_specs=[piece_of] * 2,
            ),
            out_shape=[shape(*chunk)] * 2,
        )(dests, partial, partial, right, left, *after)
        token = right
        right = shift(right, 1, range(t + 1))
        left = shift(left, -1, range(last - t, n_ctx))
    gated_all = call(
        merge_body, "merge", 0, 2 * (2 * n_ctx + last) * n_dp * rows * quarter,
        grid=(n_dp,),
        in_specs=[pl.BlockSpec((1, rows, quarter), lambda i: (i, 0, 0))] * (1 + 2 * last) + [ANY],
        out_specs=pl.BlockSpec((n_ctx, 1, rows, quarter), lambda i: (0, i, 0, 0)),
        out_shape=shape(n_ctx, n_dp, rows, quarter),
    )(gated_far, *from_left, *from_right[::-1], token).reshape(tokens, quarter)
    pieces = {}
    for k in range(n_dp - 1, -1, -1):
        token = pieces[k] = call(
            weight_body, "weight", 2 * tokens * feats * quarter, 2 * tokens * (feats + quarter),
            grid_spec=pltpu.PrefetchScalarGridSpec(
                num_scalar_prefetch=1, grid=(2,),
                in_specs=[
                    pl.BlockSpec((feats, tokens), lambda i, p, k=k: (p[0] ^ k, 0)),
                    pl.BlockSpec((tokens, quarter // 2), lambda i, p: (0, i)),
                    ANY,
                ],
                out_specs=pl.BlockSpec((feats, quarter // 2), lambda i, p: (0, i)),
            ),
            out_shape=shape(feats, quarter),
        )(place, grad_t, gated_all, token)

    def hold(value, *after):
        return call(
            wait_body, "hold", 0, 0,
            in_specs=[ANY] * (1 + len(after)), out_specs=ANY,
            out_shape=shape(*value.shape), input_output_aliases={0: 0},
        )(value, *after)

    diagonal = swap(pieces[n_dp - 1], "dp", n_dp - 1)

    delta = call(
        sum_body, "sum", 0, 8 * n_dp * rows * quarter,
        grid_spec=pltpu.PrefetchScalarGridSpec(
            num_scalar_prefetch=1, grid=(n_dp,),
            in_specs=[
                pl.BlockSpec((1, 1, rows, quarter), lambda i, p: (p[1], p[0] ^ i, 0, 0)),
                pl.BlockSpec((1, 1, rows, quarter), lambda i, p: (0, p[0] ^ i, 0, 0)),
                pl.BlockSpec((1, 1, rows, quarter), lambda i, p: (0, p[0] ^ i, 0, 0)),
                ANY,
            ],
            out_specs=[pl.BlockSpec((rows, quarter), lambda i, p: (0, 0))] * n_dp,
        ),
        out_shape=[shape(rows, quarter)] * n_dp,
    )(place, partial, right, left, pieces[n_dp // 2])
    delta = [delta[0]] + [swap(hold(delta[k], diagonal, pieces[0]), "dp", k) for k in range(1, n_dp)]
    weight_far = [pieces[0]] + [
        swap(hold(pieces[k], *delta[1:]), "dp", k) for k in range(1, n_dp - 1)
    ] + [diagonal]

    here = pl.BlockSpec((rows, block), lambda i, p: (0, p[0] ^ i))
    seed, starts, gate_grad = call(
        functools.partial(seed_body, n_dp), "seed", 2 * rows * 128 * width, rows * width * 10,
        grid_spec=pltpu.PrefetchScalarGridSpec(
            num_scalar_prefetch=1, grid=(n_dp,),
            in_specs=[pl.BlockSpec((rows, quarter), lambda i, p: (0, 0))] * n_dp
            + [here, here, pl.BlockSpec((block, rows), lambda i, p: (p[0] ^ i, 0))],
            out_specs=[here, pl.BlockSpec((ORDER, block), lambda i, p: (0, p[0] ^ i)), here],
            scratch_shapes=[pltpu.VMEM((rows, block), BF16)],
        ),
        out_shape=[shape(rows, width), shape(ORDER, width), shape(rows, width)],
    )(place, *delta, gate, long_out, starts_coef)
    starts_far = [shift(starts, -k) for k in range(1, n_ctx)]
    local_bwd = local(True, kernel, seed)
    query_grad, conv_grad = call(
        functools.partial(back_body, n_ctx - 1), "back", 2 * rows * 128 * width, rows * width * 12,
        grid=(steps,),
        in_specs=[wide(rows, block), wide((n_ctx - 1) * rows, block)] + [wide(rows, block)] * 2
        + [wide(ORDER, block)] * (n_ctx - 1),
        out_specs=[wide(rows, block)] * 2,
        out_shape=[shape(rows, width)] * 2,
    )(local_bwd, back_coef, conv, query, *starts_far)

    cut = feats // n_dp
    weight_grad = call(
        lay_body, "lay", 0, 4 * feats * width,
        grid_spec=pltpu.PrefetchScalarGridSpec(
            num_scalar_prefetch=1, grid=(n_dp,),
            in_specs=[pl.BlockSpec((cut, quarter), lambda i, p: (i, 0))] * n_dp + [ANY],
            out_specs=pl.BlockSpec((cut, width), lambda i, p: (i, 0)),
        ),
        out_shape=shape(feats, width),
    )(place, *weight_far, query_grad)
    return query_grad, conv_grad, gate_grad, weight_grad


def solution(mesh):
    rows = P(("dp", "ctx"), "tp")
    return jax.shard_map(
        on_device,
        mesh=mesh,
        in_specs=(rows, rows, rows, rows, P(("dp", "ctx"), None), P("tp", ("dp", "ctx")),
                  P("tp", None), P("tp", None), P("tp", None)),
        out_specs=(rows, rows, rows, rows),
        check_vma=False,
    )
```
